32 devices in a mesh: dp: 4 (over y, x), blk: 8 (over z, core).
Axes of the slice: x: 2, y: 2, z: 4, core: 2. Of those that a mesh axis runs over, the one named last changes fastest.
Arguments:
- tokens: bfloat16 [2, 8192, 768], P(None, ('dp', 'blk')), may hold values from -6 to 6
- cotangent: bfloat16 [2, 8192, 768], P(None, ('dp', 'blk')), may hold values from -6 to 6
- lengths: int32 [2, 4, 4], P(None, 'dp'), may hold values from 1 to 2045, as said below
- norm_gain: bfloat16 [768], replicated, may hold values from 0.099609375 to 1.8984375
- norm_bias: bfloat16 [768], replicated, may hold values from -3 to 3
- w_qkv: bfloat16 [768, 2304], replicated, may hold values from -0.3125 to 0.3125
- w_out: bfloat16 [768, 768], replicated, may hold values from -0.875 to 0.875
- w_up: bfloat16 [768, 3072], replicated, may hold values from -0.21875 to 0.21875
- w_down: bfloat16 [3072, 768], replicated, may hold values from -0.109375 to 0.109375
Outputs:
- output: bfloat16 [2, 8192, 768], P(None, ('dp', 'blk'))
- input_grad: float32 [2, 8192, 768], P(None, ('dp', 'blk'))
- grad_gain: float32 [768], replicated
- grad_bias: float32 [768], replicated
- grad_qkv: float32 [768, 2304], replicated
- grad_out: float32 [768, 768], replicated
- grad_up: float32 [768, 3072], replicated
- grad_down: float32 [3072, 768], replicated
The draws below stay inside these ranges and needn't reach their ends.
Inputs may be any that keep to these rules, and one draw needn't show every extreme that they name: Each of the 2 x 4 rows holds 4 document lengths of 1 or more that sum to 2048.
All inputs are finite; a program needn't handle non-finite values.
Results may differ from the reference program's by a relative error of at most 0.012.
The reference program's roundings to bfloat16 on the way count: a program that leaves them out, or rounds other values in their place, can miss the bound.
Values may be sent and summed in bfloat16 or wider, within the bound.
No kernel may reach another device: no remote copies, remote signals or barrier semaphores. Data moves between devices by JAX's collectives and lax.ppermute only.
A program may use at most 320 MiB of HBM per device.

```python
import jax
import jax.numpy as jnp
from jax import lax

D = 768
HEADS = 12
HEAD = 64
FF = 3072
ROT = 16
TOK_DEV = 256
MICRO = 2
DOCS = 4
GROUPS = 4
GROUP_TOK = 2048
TOKENS = 8192
N_BLK = 8


def draw_lengths(key, part):
    key = jax.random.fold_in(key, 11)
    row_total = MICRO * GROUPS
    subkeys = jax.random.split(key, 4)
    leading = jax.random.randint(subkeys[0], (row_total,), 1, TOK_DEV)
    trailing = jax.random.randint(subkeys[1], (row_total,), 2, TOK_DEV)
    third_len = jax.random.randint(subkeys[2], (row_total,), 0, 1 << 20) % (trailing - 1) + 1
    picked_row = jax.random.randint(subkeys[3], (), 0, row_total)
    forced = jnp.arange(row_total) == picked_row
    leading = jnp.where(forced, 1, leading)
    trailing = jnp.where(forced, 2, trailing)
    third_len = jnp.where(forced, 1, third_len)
    spanning = GROUP_TOK - leading - trailing
    fourth = trailing - third_len
    return jnp.stack([leading, spanning, third_len, fourth], axis=-1).reshape(MICRO, GROUPS, DOCS).astype(jnp.int32)


def level_of(rng, dims, cuts, low, high):
    factor_of, own = 1.0, jax.random.fold_in(rng, 6)
    for position, parts in cuts:
        heights = jnp.exp(jax.random.uniform(jax.random.fold_in(own, position), (parts,), jnp.float32, low / len(cuts), high / len(cuts)))
        factor_of = factor_of * jnp.repeat(heights, dims[position] // parts).reshape([-1 if axis == position else 1 for axis in range(len(dims))])
    return factor_of


def bell_draw(rng, dims, deviation, limit, pieces=(), kind=jnp.bfloat16):
    factor_of = level_of(rng, dims, pieces, -0.22, 0.18) if pieces else 1.0
    entries = jax.random.normal(rng, dims, jnp.float32) * deviation * factor_of
    return jnp.minimum(jnp.maximum(entries, -limit), limit).astype(kind)


def setup_inputs(seed: int = 0) -> dict:
    splits = jax.random.split(jax.random.key(seed), 10)
    return {
        "tokens": bell_draw(splits[0], (MICRO, TOKENS, D), 1.0, 6.0, ((1, 32),)),
        "cotangent": bell_draw(splits[1], (MICRO, TOKENS, D), 1.0, 6.0, ((1, 32),)),
        "lengths": draw_lengths(jax.random.fold_in(splits[9], 71), 0),
        "norm_gain": jnp.clip(1.0 + 0.18 * jax.random.normal(splits[3], (D,), jnp.float32), 0.099609375, 1.8984375).astype(jnp.bfloat16),
        "norm_bias": bell_draw(splits[4], (D,), 0.5, 3.0),
        "w_qkv": bell_draw(splits[5], (D, 3 * D), (D // 2) ** -0.5, 0.3125),
        "w_out": bell_draw(splits[6], (D, D), (D // 16) ** -0.5, 0.875),
        "w_up": bell_draw(splits[7], (D, FF), D ** -0.5, 0.21875),
        "w_down": bell_draw(splits[8], (FF, D), FF ** -0.5, 0.109375),
    }


@jax.custom_vjp
def low(v):
    return lax.optimization_barrier(v.astype(jnp.bfloat16)).astype(jnp.float32)

@jax.custom_vjp
def low_back(v):
    return v

def low_keep(v):
    return (low(v), None)

def low_pass(kept, grad):
    return (grad,)

def back_keep(v):
    return (v, None)

def back_low(kept, grad):
    return (low(grad),)
low.defvjp(low_keep, low_pass)
low_back.defvjp(back_keep, back_low)
norm_eps = 1e-05
masked_score = -1e+30
highest = lax.Precision.HIGHEST

def matmul(operand, factor):
    return jnp.dot(operand, factor, precision=highest, preferred_element_type=jnp.float32)

def doc_layout(doc_lengths, row_count):
    doc_ends = jnp.cumsum(doc_lengths, dtype=jnp.int32)
    doc_starts = doc_ends - doc_lengths
    index_rows = jnp.arange(row_count, dtype=jnp.int32)
    doc_ids = lax.optimization_barrier(jnp.sum((index_rows[:, None] >= doc_ends[None, :]).astype(jnp.int32), axis=1)).astype(jnp.int32)
    picked = doc_ids[:, None] == jnp.arange(doc_lengths.shape[0], dtype=jnp.int32)[None, :]
    shifts = lax.optimization_barrier(jnp.sum(jnp.where(picked, doc_starts[None, :], 0), axis=1)).astype(jnp.int32)
    return (doc_ids, index_rows - shifts)

def angles(positions, rot_dims):
    half_dims = rot_dims // 2
    frequency = 10000.0 ** (-2.0 * jnp.arange(half_dims, dtype=jnp.float32) / rot_dims)
    phases = positions.astype(jnp.float32)[:, None] * frequency[None, :]
    return (jnp.cos(phases)[:, None, :], jnp.sin(phases)[:, None, :])

def turn_field(rows_in, cos_rows, sin_rows, rot_dims):
    half_dims = rot_dims // 2
    first_half = rows_in[..., :half_dims]
    second = rows_in[..., half_dims:rot_dims]
    return jnp.concatenate([first_half * cos_rows - second * sin_rows, second * cos_rows + first_half * sin_rows, rows_in[..., rot_dims:]], axis=-1)

def forward_group(x_rows, gain, shift_vec, w_qkv, w_out, w_up, w_down, doc_ids, positions):
    row_count = x_rows.shape[0]
    row_mean = lax.optimization_barrier(jnp.mean(x_rows, axis=1, keepdims=True))
    centred = x_rows - row_mean
    spread = lax.optimization_barrier(jnp.mean(centred * centred, axis=1, keepdims=True))
    normed = low(centred * lax.rsqrt(spread + norm_eps) * gain + shift_vec)
    projected = low_back(matmul(normed, w_qkv)).reshape(row_count, 3, HEADS, HEAD)
    cos_rows, sin_rows = angles(positions, ROT)
    queries = low(turn_field(projected[:, 0], cos_rows, sin_rows, ROT))
    key_rows = low(turn_field(projected[:, 1], cos_rows, sin_rows, ROT))
    values = low(projected[:, 2])
    block_rows = min(512, row_count)
    score_scale = HEAD ** (-0.5)
    key_index = jnp.arange(row_count, dtype=jnp.int32)

    def attend(first_row):
        query_block = lax.dynamic_slice_in_dim(queries, first_row, block_rows, 0)
        query_docs = lax.dynamic_slice_in_dim(doc_ids, first_row, block_rows, 0)
        query_index = first_row + jnp.arange(block_rows, dtype=jnp.int32)
        scores = jnp.einsum('qhd,khd->hqk', query_block, key_rows, precision=highest) * score_scale
        allowed = (query_docs[:, None] == doc_ids[None, :]) & (query_index[:, None] >= key_index[None, :])
        scores = low_back(jnp.where(allowed[None], scores, masked_score))
        weights = low(jax.nn.softmax(scores, axis=-1))
        return jnp.einsum('hqk,khd->qhd', weights, values, precision=highest).reshape(block_rows, HEADS * HEAD)
    block_firsts = jnp.arange(row_count // block_rows, dtype=jnp.int32) * block_rows
    attended = lax.map(jax.checkpoint(attend), block_firsts).reshape(row_count, HEADS * HEAD)
    attended = low(low_back(attended))
    hidden = low_back(matmul(normed, w_up))
    active = low(jax.nn.gelu(hidden, approximate=False))
    return x_rows + matmul(attended, w_out) + matmul(active, w_down)

def reference(tokens, cotangent, lengths, norm_gain, norm_bias, w_qkv, w_out, w_up, w_down):
    group_rows = TOK_DEV * N_BLK
    params_all = tuple((matrix.astype(jnp.float32) for matrix in (norm_gain, norm_bias, w_qkv, w_out, w_up, w_down)))
    inputs = tokens.reshape(MICRO * GROUPS, group_rows, D)
    grads_in = cotangent.reshape(MICRO * GROUPS, group_rows, D)
    doc_lengths = lengths.reshape(MICRO * GROUPS, DOCS)

    def one_group(summed, group_data):
        x_rows, dy_rows, length_row = group_data
        doc_ids, positions = doc_layout(length_row, group_rows)

        def forward(x_value, *params):
            return forward_group(x_value, *params, doc_ids, positions)
        result, pullback = jax.vjp(forward, x_rows.astype(jnp.float32), *params_all)
        gradients = pullback(dy_rows.astype(jnp.float32))
        summed = tuple((acc_grad + new_grad for acc_grad, new_grad in zip(summed, gradients[1:])))
        return (summed, (result.astype(jnp.bfloat16), gradients[0]))
    initial = tuple((jnp.zeros(matrix.shape, jnp.float32) for matrix in params_all))
    summed, (results, input_grads) = lax.scan(one_group, initial, (inputs, grads_in, doc_lengths))
    return (results.reshape(MICRO, GROUPS * group_rows, D), input_grads.reshape(MICRO, GROUPS * group_rows, D), summed[0], summed[1], summed[2], summed[3], summed[4], summed[5])
```

```python
from functools import partial

import jax
import jax.numpy as jnp
from jax import lax
from jax.experimental import pallas as pl
from jax.experimental.pallas import tpu as pltpu
from jax.sharding import PartitionSpec as P

HEAD = 64
ROT = 16
TENSOR = 4
LANES = 128
norm_eps = 1e-05
masked_score = -1e30
F32 = jnp.float32
BF16 = jnp.bfloat16
VMEM_LIMIT = 56 * 1024 * 1024

NN = (((1,), (0,)), ((), ()))
NT = (((1,), (1,)), ((), ()))
TN = (((0,), (0,)), ((), ()))


def mul(a, b, dims=NN):
    return lax.dot_general(a, b, dims, preferred_element_type=F32)


def params(semantics=1):
    return pltpu.CompilerParams(
        dimension_semantics=("arbitrary",) * semantics, vmem_limit_bytes=VMEM_LIMIT
    )


def cost(flops, moved, special=0):
    return pl.CostEstimate(flops=int(flops), bytes_accessed=int(moved), transcendentals=int(special))


def sds(shape, dtype):
    return jax.ShapeDtypeStruct(shape, dtype)


def whole(shape):
    return pl.BlockSpec(shape, lambda *_: (0,) * len(shape))


def lane_low(rows):
    return lax.broadcasted_iota(jnp.int32, (rows, LANES), 1) < HEAD


def project_kernel(n_heads, scalars, x_ref, gain_ref, bias_ref, w_ref, cc_ref, ss_ref, *refs):
    normed_ref, q_ref, k_ref, kt_ref, v_ref, vt_ref = refs[-6:]
    x = x_ref[0].astype(F32)
    mean = jnp.mean(x, axis=1, keepdims=True)
    centred = x - mean
    inverse = lax.rsqrt(jnp.mean(centred * centred, axis=1, keepdims=True) + norm_eps)
    normed = (centred * inverse * gain_ref[...] + bias_ref[...]).astype(BF16)
    normed_ref[0] = normed
    wide = mul(normed, w_ref[...])
    cc, ss = cc_ref[0], ss_ref[0]

    def turned(index):
        part = wide[:, index * LANES : (index + 1) * LANES]
        return part * cc + pltpu.roll(part, HEAD, 1) * ss

    for h in range(n_heads):
        q_ref[0, h] = (turned(h) * (0.5 * HEAD**-0.5)).astype(BF16)
        key = turned(n_heads + h)
        k_ref[0, h] = key.astype(BF16)
        kt_ref[0, h] = key.T.astype(BF16)
    values = wide[:, 2 * n_heads * LANES :]
    v_ref[0] = values.astype(BF16)
    vt_ref[0] = values.T.astype(BF16)


def project(x_blocks, base, total, shared, earlier, sizes):
    n, rows, width = x_blocks.shape
    n_heads, v_wide = sizes
    gain, bias, w_wide, cc, ss = shared
    out_shapes = [
        sds((total, rows, width), BF16),
        sds((total, n_heads, rows, LANES), BF16),
        sds((total, n_heads, rows, LANES), BF16),
        sds((total, n_heads, LANES, rows), BF16),
        sds((total, rows, v_wide), BF16),
        sds((total, v_wide, rows), BF16),
    ]

    def at(shape):
        zeros = (0,) * (len(shape) - 1)
        return pl.BlockSpec((1,) + tuple(shape[1:]), lambda i, s: (i + base,) + zeros)

    in_specs = [
        pl.BlockSpec((1, rows, width), lambda i, s: (i, 0, 0)),
        whole((1, width)),
        whole((1, width)),
        whole(w_wide.shape),
        at(cc.shape),
        at(ss.shape),
    ]
    operands = [x_blocks, gain, bias, w_wide, cc, ss]
    aliases = {}
    if earlier is not None:
        for k, array in enumerate(earlier):
            aliases[1 + len(operands)] = k
            operands.append(array)
            in_specs.append(pl.BlockSpec(memory_space=pl.ANY))
    return pl.pallas_call(
        partial(project_kernel, n_heads),
        out_shape=out_shapes,
        grid_spec=pltpu.PrefetchScalarGridSpec(
            num_scalar_prefetch=1,
            grid=(n,),
            in_specs=in_specs,
            out_specs=[at(o.shape) for o in out_shapes],
        ),
        input_output_aliases=aliases,
        compiler_params=params(),
        cost_estimate=cost(2 * n * rows * width * w_wide.shape[1], 4 * n * rows * width * 3),
        name="project",
    )(jnp.zeros((1,), jnp.int32), *operands)


def attend_kernel(n_heads, tabs, q_ref, k_ref, vt_ref, start_ref, att_ref, attf_ref, lse_ref):
    q_log, d_first, d_last, k_arr = tabs
    j = pl.program_id(0)
    rows = q_ref.shape[2]
    block = q_log[j]
    starts = start_ref[0]
    q_index = block * rows + lax.broadcasted_iota(jnp.int32, (1, rows), 1)

    def step(kb, carry, masked):
        ka = k_arr[kb]
        if masked:
            k_index = kb * rows + lax.broadcasted_iota(jnp.int32, (rows, rows), 0)
            allowed = (k_index >= starts) & (k_index <= q_index)
        new = []
        for h in range(n_heads):
            m, l, acc = carry[h]
            s = mul(k_ref[ka, h], q_ref[0, h], NT)
            if masked:
                s = jnp.where(allowed, s, masked_score)
            top = jnp.maximum(m, jnp.max(s, axis=0, keepdims=True))
            p = jnp.exp(s - top)
            fade = jnp.exp(m - top)
            l = l * fade + jnp.sum(p, axis=0, keepdims=True)
            acc = acc * fade + mul(vt_ref[ka, h * HEAD : (h + 1) * HEAD], p.astype(BF16))
            new.append((top, l, acc))
        return tuple(new)

    carry = tuple(
        (
            jnp.full((1, rows), masked_score, F32),
            jnp.zeros((1, rows), F32),
            jnp.zeros((HEAD, rows), F32),
        )
        for _ in range(n_heads)
    )
    carry = step(block, carry, True)
    low = d_first[j] // rows
    full = jnp.minimum(block, (d_last[j] + rows - 1) // rows)
    carry = lax.fori_loop(low, full, lambda kb, c: step(kb, c, True), carry)
    carry = lax.fori_loop(full, block, lambda kb, c: step(kb, c, False), carry)
    lse_ref[0] = jnp.zeros_like(lse_ref[0])
    for h in range(n_heads):
        m, l, acc = carry[h]
        out = acc / l
        attf_ref[0, h * HEAD : (h + 1) * HEAD] = out
        att_ref[0, h * HEAD : (h + 1) * HEAD] = out.astype(BF16)
        lse_ref[0, h : h + 1] = m + jnp.log(l)


def attend(tabs, q, k, vt, starts):
    n, n_heads, rows, _ = q.shape
    wide = n_heads * HEAD
    pairs = 0.56 * n * k.shape[0]

    def at(shape):
        zeros = (0,) * (len(shape) - 1)
        return pl.BlockSpec((1,) + tuple(shape[1:]), lambda i, *s: (i,) + zeros)

    out_shapes = [
        sds((n, wide, rows), BF16),
        sds((n, wide, rows), F32),
        sds((n, 8, rows), F32),
    ]

    def body(a, b, c, d, *refs):
        attend_kernel(n_heads, (a, b, c, d), *refs)

    return pl.pallas_call(
        body,
        out_shape=out_shapes,
        grid_spec=pltpu.PrefetchScalarGridSpec(
            num_scalar_prefetch=4,
            grid=(n,),
            in_specs=[at(q.shape), whole(k.shape), whole(vt.shape), at(starts.shape)],
            out_specs=[at(o.shape) for o in out_shapes],
        ),
        compiler_params=params(),
        cost_estimate=cost(
            pairs * n_heads * rows * rows * 256 * 2, 8 * n * rows * LANES * 12, pairs * rows * rows * 3
        ),
        name="attend",
    )(*tabs, q, k, vt, starts)


def gelu_pair(hidden):
    cdf = 0.5 + 0.5 * lax.erf(hidden * (0.5**0.5))
    density = jnp.exp(hidden * hidden * -0.5) * 0.3989422804014327
    return hidden * cdf, cdf + hidden * density


def put_pieces(scratch, where, piece, outs, slot):
    x, y = where
    send_a, keep_a, send_b, keep_b = outs

    def rows_of(ab, cx, cy):
        return scratch[pl.ds(pl.multiple_of(((ab * 2 + cx) * 2 + cy) * piece, 16), piece), :].astype(BF16)

    for other in range(2):
        cy = jnp.bitwise_xor(y, other)
        send_a[other, slot, 0:piece] = rows_of(0, 1 - x, cy)
        keep_a[other, slot, 0:piece] = rows_of(0, x, cy)
        cx = jnp.bitwise_xor(x, other)
        send_b[other, slot, 0:piece] = rows_of(1, cx, 1 - y)
        keep_b[other, slot, 0:piece] = rows_of(1, cx, y)


def feed_kernel(n, first, last, where, normed_ref, cot_ref, up_ref, down_ref, *refs):
    n_in = 0 if first else 4
    ins, outs = refs[:n_in], refs[n_in:]
    mo_ref, ng_ref = outs[0], outs[1]
    gup_ref, gdn_ref = (outs[2], outs[3]) if not last else outs[-2:]
    i = pl.program_id(0)
    normed, cot = normed_ref[0], cot_ref[0]
    up, down = up_ref[...], down_ref[...]
    hidden = mul(normed, up)
    active, slope = gelu_pair(hidden)
    active = active.astype(BF16)
    mo_ref[0] = mul(active, down)
    hidden_grad = (mul(cot, down, NT) * slope).astype(BF16)
    ng_ref[0] = mul(hidden_grad, up, NT)
    gup = mul(normed, hidden_grad, TN)
    gdn = mul(active, cot, TN)

    @pl.when(i == 0)
    def _():
        if first:
            gup_ref[...] = gup
            gdn_ref[...] = gdn
        else:
            gup_ref[...] = ins[2][...] + gup
            gdn_ref[...] = ins[3][...] + gdn

    @pl.when(i > 0)
    def _():
        gup_ref[...] += gup
        gdn_ref[...] += gdn

    if last:

        @pl.when(i == n - 1)
        def _():
            piece = gup_ref.shape[0] // 8
            spot = (where[1], where[2])
            put_pieces(gup_ref, spot, piece, outs[2:6], 0)
            put_pieces(gdn_ref, spot, piece, outs[2:6], 1)


def feed(where, normed, cot_blocks, base, w_up, w_down, earlier, last):
    n, rows, width = cot_blocks.shape
    total = normed.shape[0]
    inner = w_up.shape[1] // TENSOR
    first = earlier is None
    at = pl.BlockSpec((1, rows, width), lambda i, s: (i + base, 0, 0))
    in_specs = [
        at,
        pl.BlockSpec((1, rows, width), lambda i, s: (i, 0, 0)),
        pl.BlockSpec((width, inner), lambda i, s: (0, s[0])),
        pl.BlockSpec((inner, width), lambda i, s: (s[0], 0)),
    ]
    operands = [normed, cot_blocks, w_up, w_down]
    out_shapes = [sds((total, rows, width), F32)] * 2
    out_specs = [at, at]
    scratch = []
    aliases = {}
    if not first:
        in_specs += [pl.BlockSpec(memory_space=pl.ANY)] * 2 + [whole((width, inner)), whole((inner, width))]
        operands += list(earlier)
        aliases = {5: 0, 6: 1}
    if last:
        piece = sds((2, 2, inner // 8, width), BF16)
        out_shapes += [piece] * 4
        out_specs += [whole(piece.shape)] * 4
        scratch = [pltpu.VMEM((width, inner), F32), pltpu.VMEM((inner, width), F32)]
    else:
        out_shapes += [sds((width, inner), F32), sds((inner, width), F32)]
        out_specs += [whole((width, inner)), whole((inner, width))]
    return pl.pallas_call(
        partial(feed_kernel, n, first, last),
        out_shape=out_shapes,
        grid_spec=pltpu.PrefetchScalarGridSpec(
            num_scalar_prefetch=1,
            grid=(n,),
            in_specs=in_specs,
            out_specs=out_specs,
            scratch_shapes=scratch,
        ),
        input_output_aliases=aliases,
        compiler_params=params(),
        cost_estimate=cost(12 * n * rows * width * inner, 12 * n * rows * width + 4 * width * inner),
        name="feed",
    )(where, *operands)


def mix_kernel(n_heads, where, att_ref, attf_ref, cot_ref, mo_ref, w_ref, out_ref, do_ref, delta_ref, go_ref):
    i = pl.program_id(0)
    wide = n_heads * HEAD
    att, cot, w = att_ref[0], cot_ref[0], w_ref[...]
    out_ref[0] = (mo_ref[0] + mul(att, w, TN)).astype(BF16)
    grad = mul(cot, w, NT).astype(BF16)
    do_ref[0] = jnp.zeros_like(do_ref[0])
    do_ref[0, :, 0:wide] = grad
    rows = cot.shape[0]
    product = mul(w, cot, NT).astype(BF16).astype(F32) * attf_ref[0]
    delta_ref[0] = jnp.zeros_like(delta_ref[0])
    for h in range(n_heads):
        delta_ref[0, h : h + 1] = jnp.sum(product[h * HEAD : (h + 1) * HEAD], axis=0, keepdims=True)
    go = mul(att, cot)

    @pl.when(i == 0)
    def _():
        go_ref[...] = go

    @pl.when(i > 0)
    def _():
        go_ref[...] += go


def mix(where, att, attf, cot, mo, w_out, v_wide):
    n, rows, width = cot.shape
    wide = att.shape[1]
    n_heads = wide // HEAD

    def at(shape):
        zeros = (0,) * (len(shape) - 1)
        return pl.BlockSpec((1,) + tuple(shape[1:]), lambda i, s: (i,) + zeros)

    out_shapes = [
        sds((n, rows, width), BF16),
        sds((n, rows, v_wide), BF16),
        sds((n, 8, rows), F32),
        sds((wide, width), F32),
    ]
    return pl.pallas_call(
        partial(mix_kernel, n_heads),
        out_shape=out_shapes,
        grid_spec=pltpu.PrefetchScalarGridSpec(
            num_scalar_prefetch=1,
            grid=(n,),
            in_specs=[
                at(att.shape),
                at(attf.shape),
                at(cot.shape),
                at(mo.shape),
                pl.BlockSpec((wide, width), lambda i, s: (s[0], 0)),
            ],
            out_specs=[at(o.shape) for o in out_shapes[:3]] + [whole((wide, width))],
        ),
        compiler_params=params(),
        cost_estimate=cost(8 * n * rows * width * wide, 10 * n * rows * width),
        name="mix",
    )(where, att, attf, cot, mo, w_out)


def back_kernel(
    n_heads, n_q, n_k, tabs, q_ref, do_ref, lse_ref, delta_ref, start_ref, ccq_ref, ssq_ref, k_ref, kt_ref, v_ref, cck_ref, ssk_ref, jq_ref, jk_ref, jv_ref, dq_ref, dk_ref, dv_ref
):
    q_log, d_first, d_last, k_log = tabs
    i = pl.program_id(0)
    rows = k_ref.shape[2]
    kb = k_log[i]
    low = lane_low(rows)

    @pl.when(i == 0)
    def _():
        dq_ref[...] = jnp.zeros_like(dq_ref)

    dk_ref[...] = jnp.zeros_like(dk_ref)
    dv_ref[...] = jnp.zeros_like(dv_ref)
    v_heads = []
    for h in range(n_heads):
        tile = v_ref[0, :, (h // 2) * LANES : (h // 2 + 1) * LANES]
        keep = low if h % 2 == 0 else ~low
        v_heads.append(jnp.where(keep, tile, jnp.zeros_like(tile)))

    def step(j, masked):
        if masked:
            k_index = kb * rows + lax.broadcasted_iota(jnp.int32, (rows, rows), 0)
            q_index = q_log[j] * rows + lax.broadcasted_iota(jnp.int32, (1, rows), 1)
            allowed = (k_index >= start_ref[j]) & (k_index <= q_index)
        for h in range(n_heads):
            q = q_ref[j, h]
            do = do_ref[j, :, (h // 2) * LANES : (h // 2 + 1) * LANES]
            s = mul(k_ref[0, h], q, NT)
            p = jnp.exp(s - lse_ref[j, h : h + 1])
            if masked:
                p = jnp.where(allowed, p, 0.0)
            dp = mul(v_heads[h], do, NT)
            ds = (p * (dp - delta_ref[j, h : h + 1])).astype(BF16)
            dv_ref[h] += mul(p.astype(BF16), do)
            dk_ref[h] += mul(ds, q)
            dq_ref[j, h] += mul(kt_ref[0, h], ds)

    def visit(j, _):
        block = q_log[j]
        active = (block >= kb) & (d_first[j] < (kb + 1) * rows)
        masked = (block == kb) | (d_last[j] > kb * rows)

        @pl.when(active & masked)
        def _():
            step(j, True)

        @pl.when(active & jnp.logical_not(masked))
        def _():
            step(j, False)

        return 0

    lax.fori_loop(0, n_q, visit, 0)

    def unturn(grad, cc, ss, scale):
        both = grad * jnp.where(low, cc, ss)
        return (both + pltpu.roll(both, HEAD, 1)) * scale

    def pack(parts):
        tiles = []
        for h in range(0, n_heads, 2):
            second = parts[h + 1] if h + 1 < n_heads else jnp.zeros_like(parts[h])
            tiles.append(jnp.where(low, parts[h], second))
        return tiles

    cck, ssk = cck_ref[0], ssk_ref[0]
    for t, tile in enumerate(pack([unturn(dk_ref[h], cck, ssk, 2.0) for h in range(n_heads)])):
        jk_ref[0, :, t * LANES : (t + 1) * LANES] = tile.astype(BF16)
    for t, tile in enumerate(pack([dv_ref[h] for h in range(n_heads)])):
        jv_ref[0, :, t * LANES : (t + 1) * LANES] = tile.astype(BF16)

    @pl.when(i == n_k - 1)
    def _():
        def finish(j, _):
            cc, ss = ccq_ref[j], ssq_ref[j]
            parts = [unturn(dq_ref[j, h].T, cc, ss, HEAD**-0.5) for h in range(n_heads)]
            for t, tile in enumerate(pack(parts)):
                jq_ref[j, :, t * LANES : (t + 1) * LANES] = tile.astype(BF16)
            return 0

        lax.fori_loop(0, n_q, finish, 0)


def attend_back(tabs, q, do, lse, delta, starts, ccq, ssq, k, kt, v, cck, ssk):
    n_q, n_heads, rows, _ = q.shape
    n_k = k.shape[0]
    v_wide = v.shape[2]
    pairs = 0.56 * n_q * n_k

    def at(shape):
        zeros = (0,) * (len(shape) - 1)
        return pl.BlockSpec((1,) + tuple(shape[1:]), lambda i, *s: (i,) + zeros)

    def body(a, b, c, d, *refs):
        back_kernel(n_heads, n_q, n_k, (a, b, c, d), *refs)

    full = [q, do, lse, delta, starts, ccq, ssq]
    cut = [k, kt, v, cck, ssk]
    out_shapes = [
        sds((n_q, rows, v_wide), BF16),
        sds((n_k, rows, v_wide), BF16),
        sds((n_k, rows, v_wide), BF16),
    ]
    return pl.pallas_call(
        body,
        out_shape=out_shapes,
        grid_spec=pltpu.PrefetchScalarGridSpec(
            num_scalar_prefetch=4,
            grid=(n_k,),
            in_specs=[whole(a.shape) for a in full] + [at(a.shape) for a in cut],
            out_specs=[whole(out_shapes[0].shape)] + [at(o.shape) for o in out_shapes[1:]],
            scratch_shapes=[
                pltpu.VMEM((n_q, n_heads, LANES, rows), F32),
                pltpu.VMEM((n_heads, rows, LANES), F32),
                pltpu.VMEM((n_heads, rows, LANES), F32),
            ],
        ),
        compiler_params=params(),
        cost_estimate=cost(
            pairs * n_heads * rows * rows * 256 * 2 * 3, 10 * n_q * rows * 768, pairs * rows * rows * 3
        ),
        name="attend_back",
    )(*tabs, *full, *cut)


def join_kernel(n, n_heads, where, jq_ref, jk_ref, jv_ref, normed_ref, x_ref, ngm_ref, w_ref, go_ref, ng_ref, *refs):
    outs, (gq_ref, gb_ref, all_ref) = refs[:4], refs[4:]
    i = pl.program_id(0)
    v_wide = jq_ref.shape[2]
    wide = n_heads * HEAD
    joined = jnp.concatenate([jq_ref[0], jk_ref[0], jv_ref[0]], axis=1)
    gq = mul(joined, normed_ref[0], TN)
    ng = ngm_ref[0] + mul(joined, w_ref[...], NT)
    ng_ref[0] = ng.astype(BF16)
    x = x_ref[0].astype(F32)
    centred = x - jnp.mean(x, axis=1, keepdims=True)
    xhat = centred * lax.rsqrt(jnp.mean(centred * centred, axis=1, keepdims=True) + norm_eps)
    sums = jnp.concatenate(
        [jnp.sum(ng * xhat, axis=0, keepdims=True), jnp.sum(ng, axis=0, keepdims=True), jnp.zeros((14, ng.shape[1]), F32)],
        axis=0,
    )

    @pl.when(i == 0)
    def _():
        gq_ref[...] = gq
        gb_ref[...] = sums

    @pl.when(i > 0)
    def _():
        gq_ref[...] += gq
        gb_ref[...] += sums

    @pl.when(i == n - 1)
    def _():
        for third in range(3):
            all_ref[third * wide : (third + 1) * wide, :] = gq_ref[third * v_wide : third * v_wide + wide, :]
        all_ref[3 * wide :, :] = go_ref[...]
        piece = all_ref.shape[0] // 8
        put_pieces(all_ref, (where[1], where[2]), piece, outs, 0)
        extra = gb_ref[...].astype(BF16)
        for out in outs:
            for other in range(2):
                out[other, 0, piece:] = extra


def join(where, jq, jk, jv, normed, x, ngm, w_pad, grad_out):
    n, rows, width = normed.shape
    wide = grad_out.shape[0]
    n_heads = wide // HEAD

    def at(shape):
        zeros = (0,) * (len(shape) - 1)
        return pl.BlockSpec((1,) + tuple(shape[1:]), lambda i, s: (i,) + zeros)

    piece = sds((2, 1, 4 * wide // 8 + 16, width), BF16)
    tiled = [jq, jk, jv, normed, x, ngm]
    return pl.pallas_call(
        partial(join_kernel, n, n_heads),
        out_shape=[sds((n, rows, width), BF16)] + [piece] * 4,
        grid_spec=pltpu.PrefetchScalarGridSpec(
            num_scalar_prefetch=1,
            grid=(n,),
            in_specs=[at(a.shape) for a in tiled] + [whole(w_pad.shape), whole(grad_out.shape)],
            out_specs=[at(normed.shape)] + [whole(piece.shape)] * 4,
            scratch_shapes=[
                pltpu.VMEM((w_pad.shape[1], width), F32),
                pltpu.VMEM((16, width), F32),
                pltpu.VMEM((4 * wide, width), F32),
            ],
        ),
        compiler_params=params(),
        cost_estimate=cost(4 * n * rows * width * w_pad.shape[1], 14 * n * rows * width),
        name="join",
    )(where, *tiled, w_pad, grad_out)


def swap(x, axis, size, mask):
    return lax.ppermute(x, axis, [(i, i ^ mask) for i in range(size)])


def add(a, b):
    return a.astype(F32) + b.astype(F32)


def fill_kernel(table, src_ref, *refs):
    up_ref, down_ref = refs[-2:]
    up_ref[...] = src_ref[0, 0, 0].astype(F32)
    down_ref[...] = src_ref[0, 0, 1].astype(F32)


def fill(arrays, tables, shapes, earlier):
    for array, table in zip(arrays, tables):
        a, b, _, rows, width = array.shape
        aliases, extra, specs = {}, [], []
        if earlier is not None:
            aliases = {2: 0, 3: 1}
            extra = list(earlier)
            specs = [pl.BlockSpec(memory_space=pl.ANY)] * 2
        earlier = pl.pallas_call(
            fill_kernel,
            out_shape=[sds(s, F32) for s in shapes],
            grid_spec=pltpu.PrefetchScalarGridSpec(
                num_scalar_prefetch=1,
                grid=(a * b,),
                in_specs=[
                    pl.BlockSpec((1, 1, 2, rows, width), lambda i, s: (i // b, lax.rem(i, b), 0, 0, 0))
                ]
                + specs,
                out_specs=[
                    pl.BlockSpec((rows, width), lambda i, s: (s[2 * i], s[2 * i + 1])),
                    pl.BlockSpec((rows, width), lambda i, s: (s[2 * i + 1] * 8 + s[2 * i], 0)),
                ],
            ),
            input_output_aliases=aliases,
            compiler_params=params(),
            cost_estimate=cost(0, array.size * 6),
            name="fill",
        )(table, array, *extra)
    return earlier


def reduce_over_dp(parts):
    send_a, keep_a, send_b, keep_b = parts
    got_a, got_b = swap(send_a, "dp", 4, 1), swap(send_b, "dp", 4, 2)
    sum_a, sum_b = add(keep_a, got_a).astype(BF16), add(keep_b, got_b).astype(BF16)
    got_a, got_b = swap(sum_a[1], "dp", 4, 2), swap(sum_b[1], "dp", 4, 1)
    return jnp.stack([add(sum_a[0], got_a), add(sum_b[0], got_b)]).astype(BF16)


def spread(own, n_blk):
    other = swap(own, "blk", n_blk, n_blk // 2)
    total = add(own, other).astype(BF16)
    near = swap(total, "blk", n_blk, 2)
    pair = jnp.stack([total, near])
    pair_a, pair_b = pair[:, 0], pair[:, 1]
    x_a, y_b = swap(pair_a, "dp", 4, 1), swap(pair_b, "dp", 4, 2)
    two_a, two_b = jnp.stack([pair_a, x_a]), jnp.stack([pair_b, y_b])
    far_a, far_b = swap(two_a, "dp", 4, 2), swap(two_b, "dp", 4, 1)
    out = [two_a, two_b, far_a, far_b]
    return out, [swap(o, "blk", n_blk, 1) for o in out]


def piece_tables(x, y, t):
    tables = []
    for core in range(2):
        for name in ("two_a", "two_b", "far_a", "far_b"):
            rows = []
            for outer in range(2):
                for rt1 in range(2):
                    if name == "two_a":
                        ab, rx, ry = 0, outer, 0
                    elif name == "two_b":
                        ab, rx, ry = 1, 0, outer
                    elif name == "far_a":
                        ab, rx, ry = 0, outer, 1
                    else:
                        ab, rx, ry = 1, 1, outer
                    piece = (ab * 2 + jnp.bitwise_xor(x, rx)) * 2 + jnp.bitwise_xor(y, ry)
                    shard = jnp.bitwise_xor(t, rt1 * 2 + core)
                    rows += [piece, shard]
            tables.append(jnp.stack(rows).astype(jnp.int32))
    return tables


def tail_kernel(n_src, wide, tabs, *refs):
    srcs, (gq_ref, go_ref, hold_ref) = refs[:n_src], refs[n_src:]
    rows = srcs[0].shape[3] - 16
    width = srcs[0].shape[4]
    for k, src in enumerate(srcs):
        for a in range(2):
            for b in range(2):
                at = (k * 4 + a * 2 + b) * 2
                piece, shard = tabs[at], tabs[at + 1]
                hold_ref[pl.ds(pl.multiple_of(shard * 4 * wide + piece * rows, 16), rows), :] = src[a, b, 0, 0:rows].astype(F32)
    for shard in range(TENSOR):
        go_ref[shard * wide : (shard + 1) * wide, :] = hold_ref[shard * 4 * wide + 3 * wide : (shard + 1) * 4 * wide, :]
    for third in range(3):
        block = jnp.concatenate(
            [hold_ref[s * 4 * wide + third * wide : s * 4 * wide + (third + 1) * wide, :] for s in range(TENSOR)], axis=0
        )
        gq_ref[:, third * width : (third + 1) * width] = block.T


def tail(arrays, tables, width, wide):
    table = jnp.concatenate(tables)
    return pl.pallas_call(
        partial(tail_kernel, len(arrays), wide),
        out_shape=[sds((width, 3 * TENSOR * wide), F32), sds((TENSOR * wide, width), F32)],
        grid_spec=pltpu.PrefetchScalarGridSpec(
            num_scalar_prefetch=1,
            grid=(1,),
            in_specs=[whole(a.shape) for a in arrays],
            out_specs=[whole((width, 3 * TENSOR * wide)), whole((TENSOR * wide, width))],
            scratch_shapes=[pltpu.VMEM((TENSOR * 4 * wide, width), F32)],
        ),
        compiler_params=params(),
        cost_estimate=cost(0, 6 * 4 * width * width),
        name="tail",
    )(table, *arrays)


def natural(parts):
    send_a, keep_a, send_b, keep_b = parts
    a = jnp.stack([keep_a, send_a])
    b = jnp.stack([keep_b, send_b]).swapaxes(0, 1)
    both = jnp.stack([a, b])
    n, rows, width = both.shape[3:]
    return both.reshape(8, n, rows, width)


def xor_gather(x, n_blk, masks):
    for mask in reversed(masks):
        x = jnp.concatenate([x, swap(x, "blk", n_blk, mask)])
    return x


def gather_half(own, n_blk):
    pair = jnp.stack([own, swap(own, "blk", n_blk, 2)])
    return jnp.concatenate([pair, swap(pair, "blk", n_blk, 1)])


def scatter_blocks(blocks, n_blk):
    send = jnp.concatenate([blocks[6:8], blocks[2:4]])
    got = swap(send, "blk", n_blk, 1)
    far = add(blocks[4:6], got[0:2]).astype(BF16)
    near = add(blocks[0:2], got[2:4]).astype(BF16)
    far_got = swap(far[1], "blk", n_blk, 2)
    far_sum = add(far[0], far_got).astype(BF16)
    other = swap(far_sum, "blk", n_blk, n_blk // 2)
    near_got = swap(near[1], "blk", n_blk, 2)
    return add(near[0], near_got), other.astype(F32)


def local(n_dp, n_blk, tokens, cotangent, lengths, norm_gain, norm_bias, w_qkv, w_out, w_up, w_down):
    micro_count, rows, width = tokens.shape
    heads = width // HEAD
    n_heads = heads // TENSOR
    v_wide = (n_heads + 1) // 2 * LANES
    wide = n_heads * HEAD
    inner = w_up.shape[1] // TENSOR
    splits = n_blk // (2 * TENSOR)
    s_masks = [TENSOR << b for b in reversed(range(splits.bit_length() - 1))]
    fast = n_dp == 4 and splits == 1
    me = lax.axis_index("blk")
    dp = lax.axis_index("dp")
    half = me // (n_blk // 2)
    quarter = lax.rem(me, TENSOR)
    x_pos, y_pos = (lax.rem(dp, 2), dp // 2) if fast else (jnp.int32(0), jnp.int32(0))
    where = jnp.stack([quarter, x_pos, y_pos]).astype(jnp.int32)

    masks = [h * (n_blk // 2) + r for h in range(2) for r in (0, 2, 1, 3)]
    n_q = len(masks)
    q_log = jnp.bitwise_xor(me, jnp.array(masks, jnp.int32))
    s_list = [0]
    for mask in reversed(s_masks):
        s_list = s_list + [v ^ mask for v in s_list]
    k_log = jnp.bitwise_xor(me, jnp.array([m ^ s for s in s_list for m in masks], jnp.int32))
    n_k = n_q * splits
    k_arr = jnp.sum(
        jnp.where(k_log[None, :] == jnp.arange(n_k)[:, None], jnp.arange(n_k)[None, :], 0), axis=1
    ).astype(jnp.int32)

    doc_lengths = lax.dynamic_index_in_dim(lengths, half, 0, False)[0]
    doc_ends = jnp.cumsum(doc_lengths, dtype=jnp.int32)
    doc_starts = doc_ends - doc_lengths

    def start_of(index):
        begun = (index[..., None] >= doc_starts).astype(jnp.int32) * doc_lengths_before
        return jnp.sum(begun, axis=-1)

    doc_lengths_before = doc_starts - jnp.concatenate([jnp.zeros((1,), jnp.int32), doc_starts[:-1]])
    q_index = q_log[:, None] * rows + jnp.arange(rows, dtype=jnp.int32)[None, :]
    starts = start_of(q_index)
    d_first, d_last = starts[:, 0], starts[:, -1]

    frequency = 10000.0 ** (-2.0 * jnp.arange(ROT // 2, dtype=F32) / ROT)

    def turn_tables(index):
        phases = (index - start_of(index)).astype(F32)[:, None, :] * frequency[None, :, None]
        cos, sin = jnp.cos(phases), jnp.sin(phases)
        ones = jnp.ones((index.shape[0], HEAD - ROT, rows), F32)
        zeros = jnp.zeros_like(ones)
        cc = jnp.concatenate([cos, cos, ones] * 2, axis=1).swapaxes(1, 2)
        ss = jnp.concatenate([-sin, sin, zeros, sin, -sin, zeros], axis=1).swapaxes(1, 2)
        return cc, ss

    cc_q, ss_q = turn_tables(q_index)
    if splits > 1:
        cc_k, ss_k = turn_tables(k_log[:, None] * rows + jnp.arange(rows, dtype=jnp.int32)[None, :])
    else:
        cc_k, ss_k = cc_q, ss_q

    cut = lax.dynamic_slice_in_dim(w_qkv.reshape(width, 3, heads * HEAD), quarter * wide, wide, 2)
    cut = cut.reshape(width, 3, n_heads, HEAD)
    swapped = jnp.concatenate([cut[..., ROT // 2 : ROT], cut[..., : ROT // 2], cut[..., ROT:]], axis=-1)
    doubled = jnp.concatenate([cut, swapped], axis=-1)[:, :2].reshape(width, 2 * n_heads * LANES)
    pad = jnp.zeros((width, 3, v_wide - wide), BF16)
    w_pad = jnp.concatenate([cut.reshape(width, 3, wide), pad], axis=2)
    w_wide = jnp.concatenate([doubled, w_pad[:, 2]], axis=1)
    w_pad = w_pad.reshape(width, 3 * v_wide)

    gain = norm_gain.astype(F32).reshape(1, width)
    bias = norm_bias.astype(F32).reshape(1, width)

    def mine(array):
        return lax.dynamic_index_in_dim(array, half, 0, False), lax.dynamic_index_in_dim(array, 1 - half, 0, False)

    x_mine, x_other = mine(tokens)
    c_mine, c_other = mine(cotangent)
    x_cross = swap(x_other, "blk", n_blk, n_blk // 2)
    x_near = gather_half(x_mine, n_blk)
    x_far = gather_half(x_cross, n_blk)
    c_cross = swap(c_other, "blk", n_blk, n_blk // 2)
    c_near = gather_half(c_mine, n_blk)
    c_far = gather_half(c_cross, n_blk)

    shared = (gain, bias, w_wide, cc_q, ss_q)
    sizes = (n_heads, v_wide)
    stage = project(x_near, 0, n_q, shared, None, sizes)
    normed, q, k, kt, v, vt = project(x_far, 4, n_q, shared, stage, sizes)
    if splits > 1:
        k, kt, v, vt = (xor_gather(a, n_blk, s_masks) for a in (k, kt, v, vt))
    starts_rows = starts[:, None, :]
    att, attf, lse = attend((q_log, d_first, d_last, k_arr), q, k, vt, starts_rows)

    feed_state = feed(where, normed, c_near, 0, w_up, w_down, None, False)
    mo, ngm, *mlp_parts = feed(where, normed, c_far, 4, w_up, w_down, feed_state, True)
    cot = jnp.concatenate([c_near, c_far])
    x_all = jnp.concatenate([x_near, x_far])
    out_part, do, delta, grad_out_part = mix(where, att, attf, cot, mo, w_out, v_wide)
    jq, jk, jv = attend_back(
        (q_log, d_first, d_last, k_log), q, do, lse, delta, starts_rows, cc_q, ss_q, k, kt, v, cc_k, ss_k
    )
    if splits > 1:
        for mask in s_masks:
            count = jk.shape[0] // 2
            jk = add(jk[:count], swap(jk[count:], "blk", n_blk, mask)).astype(BF16)
            jv = add(jv[:count], swap(jv[count:], "blk", n_blk, mask)).astype(BF16)
    ng_part, *join_parts = join(where, jq, jk, jv, normed, x_all, ngm, w_pad, grad_out_part)

    def ordered(own, other):
        return jnp.where(half == 0, jnp.stack([own, other]), jnp.stack([other, own]))

    output = (tokens.astype(F32) + ordered(*scatter_blocks(out_part, n_blk))).astype(BF16)
    normed_grad = ordered(*scatter_blocks(ng_part, n_blk))
    x_rows = tokens.astype(F32)
    centred = x_rows - jnp.mean(x_rows, axis=2, keepdims=True)
    inverse = lax.rsqrt(jnp.mean(centred * centred, axis=2, keepdims=True) + norm_eps)
    scaled = centred * inverse
    scaled_grad = normed_grad * norm_gain.astype(F32)
    input_grad = cotangent.astype(F32) + inverse * (
        scaled_grad
        - jnp.mean(scaled_grad, axis=2, keepdims=True)
        - scaled * jnp.mean(scaled_grad * scaled, axis=2, keepdims=True)
    )

    if fast:
        tables = piece_tables(x_pos, y_pos, quarter)
        first, twin = spread(reduce_over_dp(mlp_parts), n_blk)
        grad_up, grad_down = fill(first + twin, tables, [w_up.shape, w_down.shape], None)
        first, twin = spread(reduce_over_dp(join_parts), n_blk)
        grad_qkv, grad_out = tail(first + twin, tables, width, wide)
        norm_sums = sum(a[0, b, 0, -16:-14].astype(F32) for a in (first[0], twin[0]) for b in range(2))
        quads = jnp.stack([a[0, b, 0, -16:-14].astype(F32) for a in (first[0], twin[0]) for b in range(2)])
        order = jnp.bitwise_xor(quarter, jnp.array([0, 2, 1, 3], jnp.int32))
        norm_sums = sum(jnp.sum(jnp.where((order == s)[:, None, None], quads, 0.0), axis=0) for s in range(TENSOR))
    else:
        mlp = natural(mlp_parts)
        up = mlp[:, 0].reshape(width, inner)
        down = mlp[:, 1].reshape(inner, width)
        rest = natural(join_parts)[:, 0]
        norm_part = rest[0, -16:-14].astype(F32)
        rest = rest[:, :-16].reshape(4 * wide, width)
        turned = rest[: 3 * wide].T.reshape(width, 3, wide)
        zeros = partial(jnp.zeros, dtype=BF16)
        up = lax.dynamic_update_slice_in_dim(zeros(w_up.shape), up, quarter * inner, 1)
        down = lax.dynamic_update_slice_in_dim(zeros(w_down.shape), down, quarter * inner, 0)
        turned = lax.dynamic_update_slice_in_dim(zeros((width, 3, TENSOR * wide)), turned, quarter * wide, 2)
        out = lax.dynamic_update_slice_in_dim(zeros(w_out.shape), rest[3 * wide :], quarter * wide, 0)
        grads = lax.psum((up, down, turned, out), ("dp", "blk"))
        grad_up, grad_down, turned, grad_out = (g.astype(F32) for g in grads)
        grad_qkv = turned.reshape(w_qkv.shape)
        norm_sums = lax.psum(norm_part, ("dp", "blk"))
    return (output, input_grad, norm_sums[0], norm_sums[1], grad_qkv, grad_out, grad_up, grad_down)


def solution(mesh):
    tokens = P(None, ("dp", "blk"), None)
    return jax.shard_map(
        partial(local, mesh.shape["dp"], mesh.shape["blk"]),
        mesh=mesh,
        in_specs=(tokens, tokens, P(None, "dp", None)) + (P(),) * 6,
        out_specs=(tokens, tokens) + (P(),) * 6,
        check_vma=False,
    )
```

```python
from functools import partial

import jax
import jax.numpy as jnp
from jax import lax
from jax.experimental import pallas as pl
from jax.experimental.pallas import tpu as pltpu
from jax.sharding import PartitionSpec as P

HEAD = 64
ROT = 16
TENSOR = 4
QUADS = 8
norm_eps = 1e-05
masked_score = -1e30
F32 = jnp.float32
BF16 = jnp.bfloat16
VMEM_LIMIT = 56 * 1024 * 1024
COST = 0.02
TAIL = "QUNSSDUQDSNUSQDQOSUNuQDSOdQON"

NN = (((1,), (0,)), ((), ()))
NT = (((1,), (1,)), ((), ()))
TN = (((0,), (0,)), ((), ()))

QUARTER, X_POS, Y_POS, PLACE, HALF, DOCS = range(6)


def mul(a, b, dims=NN):
    return lax.dot_general(a, b, dims, preferred_element_type=F32)


def sds(shape, dtype):
    return jax.ShapeDtypeStruct(tuple(shape), dtype)


def whole(shape):
    return pl.BlockSpec(tuple(shape), lambda *_: (0,) * len(shape))


def once(shape):
    return pl.BlockSpec(tuple(shape), lambda *_: (0,) * len(shape), pipeline_mode=pl.Buffered(1))


def rows_at(shape, base=0, count=1):
    zeros = (0,) * (len(shape) - 1)
    return pl.BlockSpec((count,) + tuple(shape[1:]), lambda i, s: (i + base,) + zeros)


def call(body, name, meta, grid, operands, in_specs, out_shapes, out_specs, flops, moved, special=0, scratch=(), aliases=None, after=()):
    after = list(after)
    n_in = len(operands)

    def kernel(meta_ref, *refs):
        body(meta_ref, *refs[:n_in], *refs[n_in + len(after) :])

    return pl.pallas_call(
        kernel,
        out_shape=out_shapes,
        grid_spec=pltpu.PrefetchScalarGridSpec(
            num_scalar_prefetch=1,
            grid=grid,
            in_specs=list(in_specs) + [pl.BlockSpec(memory_space=pl.ANY)] * len(after),
            out_specs=out_specs,
            scratch_shapes=list(scratch),
        ),
        input_output_aliases=aliases or {},
        compiler_params=pltpu.CompilerParams(
            dimension_semantics=("arbitrary",) * len(grid), vmem_limit_bytes=VMEM_LIMIT
        ),
        cost_estimate=pl.CostEstimate(flops=int(flops * COST), bytes_accessed=int(moved * COST), transcendentals=int(special * COST)),
        name=name,
    )(meta, *operands, *after)


def place_mask(j, n_blk):
    return (j // 4) * (n_blk // 2) + lax.rem(j, 2) * 2 + lax.rem(j // 2, 2)


def q_block(meta, j, n_blk):
    return jnp.bitwise_xor(meta[PLACE], place_mask(j, n_blk))


def k_block(meta, i, n_blk):
    return jnp.bitwise_xor(q_block(meta, lax.rem(i, QUADS), n_blk), (i // QUADS) * TENSOR)


def k_slot(meta, block, n_blk):
    r = jnp.bitwise_xor(meta[PLACE], block)
    low = lax.rem(r, TENSOR)
    split = lax.rem(r, n_blk // 2) // TENSOR
    return split * QUADS + (r // (n_blk // 2)) * 4 + lax.rem(low, 2) * 2 + low // 2


def doc_start(meta, index, n_docs):
    start = jnp.zeros_like(index)
    for d in range(n_docs):
        first = meta[DOCS + d]
        start = jnp.where(index >= first, first, start)
    return start


def token_index(block, rows):
    return block * rows + lax.broadcasted_iota(jnp.int32, (1, rows), 1)


def angles(meta, block, rows, n_docs):
    index = token_index(block, rows)
    position = (index - doc_start(meta, index, n_docs)).astype(F32)
    order = lax.broadcasted_iota(jnp.int32, (ROT // 2, 1), 0)
    frequency = jnp.ones((ROT // 2, 1), F32)
    for i in range(1, ROT // 2):
        frequency = jnp.where(order == i, 10000.0 ** (-2.0 * i / ROT), frequency)
    phases = position * frequency
    return jnp.cos(phases), jnp.sin(phases)


def turned(head, cos, sin):
    a, b = head[: ROT // 2], head[ROT // 2 : ROT]
    return jnp.concatenate([a * cos - b * sin, b * cos + a * sin, head[ROT:]], axis=0)


def cut_kernel(wide, meta, *refs):
    srcs, out_ref, hold_ref = refs[:3], refs[3], refs[4]
    first = pl.multiple_of(lax.rem(meta[QUARTER], 2) * wide, 16)
    for third in range(3):
        hold_ref[...] = srcs[third][...].astype(F32).T
        out_ref[third * wide : (third + 1) * wide, :] = hold_ref[pl.ds(first, wide), :].astype(BF16)


def cut(meta, w_qkv, wide):
    width = w_qkv.shape[0]
    per = w_qkv.shape[1] // 3 // (2 * wide)

    def spec(third):
        return pl.BlockSpec((width, 2 * wide), lambda i, s: (0, third * per + s[QUARTER] // 2))

    return call(
        partial(cut_kernel, wide),
        "cut",
        meta,
        (1,),
        [w_qkv] * 3,
        [spec(third) for third in range(3)],
        sds((3 * wide, width), BF16),
        whole((3 * wide, width)),
        0,
        18 * wide * width,
        scratch=[pltpu.VMEM((2 * wide, width), F32)],
    )


def pick_kernel(meta, src_ref, out_ref):
    out_ref[...] = src_ref[0]


def pick(meta, array, other, after=()):
    _, rows, width = array.shape
    return call(
        pick_kernel,
        "pick",
        meta,
        (1,),
        [array],
        [pl.BlockSpec((1, rows, width), lambda i, s: ((1 - s[HALF]) if other else s[HALF], 0, 0))],
        sds((rows, width), array.dtype),
        whole((rows, width)),
        0,
        4 * rows * width,
        after=after,
    )


def project_kernel(n_heads, n_blk, n_docs, base, meta, *refs):
    pieces, (gain_ref, bias_ref, w_ref) = refs[:4], refs[4:7]
    x_ref, normed_ref, q_ref, k_ref, v_ref, kn_ref, vn_ref = refs[-7:]
    i = pl.program_id(0)
    rows = x_ref.shape[1]
    wide = n_heads * HEAD
    for k in range(4):

        @pl.when(i == k // 2)
        def _():
            x_ref[k % 2] = pieces[k][...]

    for b in range(2):
        x = x_ref[b].astype(F32)
        mean = jnp.mean(x, axis=1, keepdims=True)
        centred = x - mean
        inverse = lax.rsqrt(jnp.mean(centred * centred, axis=1, keepdims=True) + norm_eps)
        normed_ref[b] = (centred * inverse * gain_ref[...] + bias_ref[...]).astype(BF16)
    flats = [mul(w_ref[...], normed_ref[b], NT) for b in range(2)]
    for b in range(2):
        flat = flats[b]
        cos, sin = angles(meta, q_block(meta, 2 * i + b + base, n_blk), rows, n_docs)
        for h in range(n_heads):
            at = slice(h * HEAD, (h + 1) * HEAD)
            q_ref[b, at] = (turned(flat[at], cos, sin) * HEAD**-0.5).astype(BF16)
            key = turned(flat[wide + h * HEAD : wide + (h + 1) * HEAD], cos, sin)
            k_ref[b, at] = key.astype(BF16)
            kn_ref[b, h] = key.T.astype(BF16)
            value = flat[2 * wide + h * HEAD : 2 * wide + (h + 1) * HEAD]
            v_ref[b, at] = value.astype(BF16)
            vn_ref[b, h] = value.T.astype(BF16)


def project(meta, pieces, base, total, gain, bias, w_cut, n_blk, n_docs, earlier, after=()):
    rows, width = pieces[0].shape
    wide = w_cut.shape[0] // 3
    n_heads = wide // HEAD
    outs = [
        sds((total, rows, width), BF16),
        sds((total, rows, width), BF16),
        sds((total, wide, rows), BF16),
        sds((total, wide, rows), BF16),
        sds((total, wide, rows), BF16),
        sds((total, n_heads, rows, HEAD), BF16),
        sds((total, n_heads, rows, HEAD), BF16),
    ]
    operands = list(pieces) + [gain, bias, w_cut]
    specs = [whole(o.shape) for o in operands]
    aliases = {}
    if earlier is not None:
        aliases = {1 + len(operands) + k: k for k in range(len(outs))}
        operands += list(earlier)
        specs += [pl.BlockSpec(memory_space=pl.ANY)] * len(outs)
    return call(
        partial(project_kernel, n_heads, n_blk, n_docs, base),
        "project",
        meta,
        (2,),
        operands,
        specs,
        outs,
        [rows_at(o.shape, base // 2, 2) for o in outs],
        8 * rows * width * 3 * wide,
        4 * rows * width * 10,
        aliases=aliases,
        after=after,
    )


def list_pairs(meta, base, count, rows, n_blk, n_docs, q_list, k_list):
    def of_block(j, found):
        block = q_block(meta, base + j, n_blk)
        first = doc_start(meta, block * rows, n_docs) // rows

        def put(kb, at):
            q_list[at] = j
            k_list[at] = kb
            return at + 1

        return lax.fori_loop(first, block + 1, put, found)

    return lax.fori_loop(0, count, of_block, jnp.int32(0))


def seen(meta, kb, block, rows, n_docs):
    index = token_index(block, rows)
    k_index = kb * rows + lax.broadcasted_iota(jnp.int32, (rows, rows), 0)
    return (k_index >= doc_start(meta, index, n_docs)) & (k_index <= index)


def attend_kernel(n_heads, n_blk, n_docs, meta, q_ref, kn_ref, v_ref, att_ref, attf_ref, lse_ref, s_ref, acc_ref, top_ref, sum_ref, q_list, k_list):
    count, _, rows = q_ref.shape
    heads = range(n_heads)
    base = pl.program_id(0) * count
    found = list_pairs(meta, base, count, rows, n_blk, n_docs, q_list, k_list)
    q_list[found] = count
    k_list[found] = 0
    steps = (found + 1) // 2
    top_ref[...] = jnp.full_like(top_ref, masked_score)
    sum_ref[...] = jnp.zeros_like(sum_ref)
    acc_ref[...] = jnp.zeros_like(acc_ref)

    def fold(tile, how):
        return how(tile.reshape(rows // 8, 8, rows), axis=0)

    def score(n, _):
        for at in (2 * n, 2 * n + 1):
            j, kb = q_list[at], k_list[at]
            jq = jnp.minimum(j, count - 1)
            ka = k_slot(meta, kb, n_blk)
            allowed = seen(meta, kb, q_block(meta, base + jq, n_blk), rows, n_docs)
            scores = [mul(kn_ref[ka, h], q_ref[jq, h * HEAD : (h + 1) * HEAD]) for h in heads]
            for h in heads:
                s = jnp.where(allowed, scores[h], masked_score)
                s_ref[at, h] = s
                top_ref[j, h] = jnp.maximum(top_ref[j, h], fold(s, jnp.max))
        return 0

    lax.fori_loop(0, steps, score, 0)

    def settle(j, _):
        for h in heads:
            top_ref[j, h, 0:1] = jnp.max(top_ref[j, h], axis=0, keepdims=True)
        return 0

    lax.fori_loop(0, count + 1, settle, 0)

    def weigh(n, _):
        both = (2 * n, 2 * n + 1)
        weights = []
        for at in both:
            j = q_list[at]
            for h in heads:
                p = jnp.exp(s_ref[at, h] - top_ref[j, h, 0:1])
                sum_ref[j, h] += fold(p, jnp.sum)
                weights.append(p.astype(BF16))
        for m, at in enumerate(both):
            j, ka = q_list[at], k_slot(meta, k_list[at], n_blk)
            for h in heads:
                acc_ref[j, h] += mul(v_ref[ka, h * HEAD : (h + 1) * HEAD], weights[m * n_heads + h])
        return 0

    lax.fori_loop(0, steps, weigh, 0)
    lse_ref[...] = jnp.zeros_like(lse_ref)

    def finish(j, _):
        for h in heads:
            at = slice(h * HEAD, (h + 1) * HEAD)
            total = jnp.sum(sum_ref[j, h], axis=0, keepdims=True)
            out = acc_ref[j, h] / total
            attf_ref[j, at] = out
            att_ref[j, at] = out.astype(BF16)
            lse_ref[j, h : h + 1] = top_ref[j, h, 0:1] + jnp.log(total)
        return 0

    lax.fori_loop(0, count, finish, 0)


def attend(meta, q, kn, v, n_blk, n_docs, after=()):
    n, wide, rows = q.shape
    n_k, n_heads = kn.shape[:2]
    pairs = 0.56 * n * n_k
    count = n if n_k == n else 1
    most = (n * (n + 1) // 2 if n_k == n else n_k) + 2
    outs = [sds((n, wide, rows), BF16), sds((n, wide, rows), F32), sds((n, 8, rows), F32)]

    def some(shape):
        zeros = (0,) * (len(shape) - 1)
        return pl.BlockSpec((count,) + tuple(shape[1:]), lambda i, s: (i,) + zeros)

    return call(
        partial(attend_kernel, n_heads, n_blk, n_docs),
        "attend",
        meta,
        (n // count,),
        [q, kn, v],
        [some(q.shape), once(kn.shape), once(v.shape)],
        outs,
        [some(o.shape) for o in outs],
        pairs * n_heads * rows * rows * 256 * 2,
        16 * n * rows * wide,
        pairs * n_heads * rows * rows,
        scratch=[
            pltpu.VMEM((most, n_heads, rows, rows), F32),
            pltpu.VMEM((count + 1, n_heads, HEAD, rows), F32),
            pltpu.VMEM((count + 1, n_heads, 8, rows), F32),
            pltpu.VMEM((count + 1, n_heads, 8, rows), F32),
            pltpu.SMEM((most,), jnp.int32),
            pltpu.SMEM((most,), jnp.int32),
        ],
        after=after,
    )


def gelu_pair(hidden):
    bell = jnp.exp(hidden * hidden * -0.5)
    t = 1.0 / (1.0 + (0.3275911 * 0.5**0.5) * jnp.abs(hidden))
    tail = ((((0.5 * 1.061405429 * t - 0.5 * 1.453152027) * t + 0.5 * 1.421413741) * t - 0.5 * 0.284496736) * t + 0.5 * 0.254829592) * t * bell
    cdf = jnp.where(hidden >= 0, 1.0 - tail, tail)
    return hidden * cdf, cdf + hidden * bell * 0.3989422804014327


def put_pieces(scratch, meta, outs, slot):
    rows = scratch.shape[0] // 4
    for k, out in enumerate(outs):
        cx, cy = jnp.bitwise_xor(meta[X_POS], k % 2), jnp.bitwise_xor(meta[Y_POS], k // 2)
        out[slot] = scratch[pl.ds(pl.multiple_of((cx * 2 + cy) * rows, 16), rows), :].astype(BF16)


def put_halves(scratch, meta, outs, slot):
    x, y = meta[X_POS], meta[Y_POS]
    rows = scratch.shape[0] // 8

    def part(cx, cy, b):
        return scratch[pl.ds(pl.multiple_of(((cx * 2 + cy) * 2 + b) * rows, 16), rows), :].astype(BF16)

    for other in range(2):
        cx, cy = jnp.bitwise_xor(x, other), jnp.bitwise_xor(y, other)
        outs[0][other, slot] = part(1 - x, cy, 0)
        outs[1][other, slot] = part(x, cy, 0)
        outs[2][other, slot] = part(cx, 1 - y, 1)
        outs[3][other, slot] = part(cx, y, 1)


def feed_kernel(meta, *refs):
    pieces, (normed_ref, up_ref, down_ref), (cot_ref, mo_ref, ng_ref), outs, (gup_ref, gdn_ref) = (
        refs[:QUADS],
        refs[QUADS : QUADS + 3],
        refs[QUADS + 3 : QUADS + 6],
        refs[QUADS + 6 : -2],
        refs[-2:],
    )
    i = pl.program_id(0)
    rows, width = pieces[0].shape
    for k in range(QUADS):

        @pl.when(i == k // 2)
        def _():
            cot_ref[k % 2] = pieces[k][...]

    @pl.when(i == 0)
    def _():
        gup_ref[...] = jnp.zeros_like(gup_ref)
        gdn_ref[...] = jnp.zeros_like(gdn_ref)

    normed = normed_ref[...].reshape(2 * rows, width)
    cot = cot_ref[...].reshape(2 * rows, width)
    inner = up_ref.shape[1]
    chunk = inner // 3 if inner % 768 == 0 else inner
    spans = [slice(c, c + chunk) for c in range(0, inner, chunk)]

    def open_up(at):
        return mul(normed, up_ref[:, at]), mul(cot, down_ref[at, :], NT)

    opened = [open_up(at) for at in spans[:2]]
    mo = ng = None
    for c, at in enumerate(spans):
        hidden, active_grad = opened[c]
        active, slope = gelu_pair(hidden)
        active = active.astype(BF16)
        hidden_grad = (active_grad * slope).astype(BF16)
        if c + 2 < len(spans):
            opened.append(open_up(spans[c + 2]))
        part, back = mul(active, down_ref[at, :]), mul(hidden_grad, up_ref[:, at], NT)
        mo, ng = (part, back) if c == 0 else (mo + part, ng + back)
        gdn_ref[at, :] += mul(active, cot, TN)
        gup_ref[:, at] += mul(normed, hidden_grad, TN)
    mo_ref[...] = mo.astype(BF16).reshape(2, rows, width)
    ng_ref[...] = ng.astype(BF16).reshape(2, rows, width)

    @pl.when(i == QUADS // 2 - 1)
    def _():
        put_halves(gup_ref, meta, outs, 0)
        put_halves(gdn_ref, meta, outs, 1)


def feed(meta, normed, pieces, w_up, w_down, after=()):
    rows, width = pieces[0].shape
    inner = w_up.shape[1] // TENSOR
    two = rows_at(normed.shape, 0, 2)
    piece = sds((2, 2, inner // 8, width), BF16)
    return call(
        feed_kernel,
        "feed",
        meta,
        (QUADS // 2,),
        list(pieces) + [normed, w_up, w_down],
        [whole(p.shape) for p in pieces]
        + [
            two,
            pl.BlockSpec((width, inner), lambda i, s: (0, s[QUARTER])),
            pl.BlockSpec((inner, width), lambda i, s: (s[QUARTER], 0)),
        ],
        [sds(normed.shape, BF16)] * 3 + [piece] * 4,
        [two] * 3 + [whole(piece.shape)] * 4,
        12 * QUADS * rows * width * inner,
        8 * QUADS * rows * width + 8 * width * inner,
        scratch=[pltpu.VMEM((width, inner), F32), pltpu.VMEM((inner, width), F32)],
        after=after,
    )


def mix_kernel(n_heads, meta, att_ref, attf_ref, cot_ref, mo_ref, w_ref, out_ref, do_ref, delta_ref, go_ref):
    i = pl.program_id(0)
    w = w_ref[...]
    both = range(2)
    grads = [mul(w, cot_ref[b], NT).astype(BF16) for b in both]
    outs = [mul(att_ref[b], w, TN) for b in both]
    go = mul(att_ref[0], cot_ref[0]) + mul(att_ref[1], cot_ref[1])
    delta_ref[...] = jnp.zeros_like(delta_ref)
    for b in both:
        out_ref[b] = (mo_ref[b].astype(F32) + outs[b]).astype(BF16)
        do_ref[b] = grads[b]
        product = grads[b].astype(F32) * attf_ref[b]
        for h in range(n_heads):
            delta_ref[b, h : h + 1] = jnp.sum(product[h * HEAD : (h + 1) * HEAD], axis=0, keepdims=True)

    @pl.when(i == 0)
    def _():
        go_ref[...] = go

    @pl.when(i > 0)
    def _():
        go_ref[...] += go


def mix(meta, att, attf, cot, mo, w_out, after=()):
    n, rows, width = cot.shape
    wide = att.shape[1]
    outs = [
        sds((n, rows, width), BF16),
        sds((n, wide, rows), BF16),
        sds((n, 8, rows), F32),
        sds((wide, width), F32),
    ]
    return call(
        partial(mix_kernel, wide // HEAD),
        "mix",
        meta,
        (n // 2,),
        [att, attf, cot, mo, w_out],
        [rows_at(a.shape, 0, 2) for a in (att, attf, cot, mo)]
        + [pl.BlockSpec((wide, width), lambda i, s: (s[QUARTER], 0))],
        outs,
        [rows_at(o.shape, 0, 2) for o in outs[:3]] + [whole((wide, width))],
        6 * n * rows * width * wide,
        10 * n * rows * width,
        after=after,
    )


def back_kernel(heads, n_blk, n_docs, n_q, n_k, meta, q_ref, do_ref, lse_ref, delta_ref, kn_ref, vn_ref, k_ref, *refs):
    rest, (dq_ref, dk_ref, dv_ref, p_ref, ds_ref, q_list, k_list) = refs[:-7], refs[-7:]
    if len(rest) > 3:
        joins, (jq_ref, jk_ref, jv_ref) = rest[:-3], rest[-3:]
    else:
        joins, (jq_ref, jk_ref, jv_ref) = (), rest
    rows = k_ref.shape[2]
    spots = [slice(h * HEAD, (h + 1) * HEAD) for h in heads]
    dq_ref[...] = jnp.zeros_like(dq_ref)
    dk_ref[...] = jnp.zeros_like(dk_ref)
    dv_ref[...] = jnp.zeros_like(dv_ref)
    found = list_pairs(meta, 0, n_q, rows, n_blk, n_docs, q_list, k_list)

    q_list[found] = n_q - 1
    k_list[found] = q_block(meta, n_q - 1, n_blk) + 1

    def parts(n):
        for at in (2 * n, 2 * n + 1):
            j, ka = q_list[at], k_slot(meta, jnp.minimum(k_list[at], n_k - 1), n_blk)
            for m, h in enumerate(heads):
                yield at, j, ka, m, h, spots[m]

    def weigh(n):
        slot = lax.rem(n, 2)
        allowed = [seen(meta, k_list[at], q_block(meta, q_list[at], n_blk), rows, n_docs) for at in (2 * n, 2 * n + 1)]
        scores = [mul(kn_ref[ka, h], q_ref[j, at]) for _, j, ka, _, h, at in parts(n)]
        grads = [mul(vn_ref[ka, h], do_ref[j, at]) for _, j, ka, _, h, at in parts(n)]
        for c, (_, j, ka, m, h, at) in enumerate(parts(n)):
            p = jnp.where(allowed[c // len(heads)], jnp.exp(scores[c] - lse_ref[j, h : h + 1]), 0.0)
            p_ref[slot, c] = p.astype(BF16)
            ds_ref[slot, c] = (p * (grads[c] - delta_ref[j, h : h + 1])).astype(BF16)

    def gather(n):
        slot = lax.rem(n, 2)
        for c, (_, j, ka, m, h, at) in enumerate(parts(n)):
            dv_ref[ka, m] += mul(do_ref[j, at], p_ref[slot, c], NT)
            dk_ref[ka, m] += mul(q_ref[j, at], ds_ref[slot, c], NT)
            dq_ref[j, m] += mul(k_ref[ka, at], ds_ref[slot, c])

    weigh(0)

    def both(n, _):
        gather(n - 1)
        weigh(n)
        return 0

    steps = (found + 1) // 2
    lax.fori_loop(1, steps, both, 0)
    gather(steps - 1)

    def finish_k(i, _):
        cos, sin = angles(meta, k_block(meta, i, n_blk), rows, n_docs)
        for n in range(len(heads)):
            at = slice(n * HEAD, (n + 1) * HEAD)
            jk_ref[i, at] = turned(dk_ref[i, n], cos, -sin).astype(BF16)
            jv_ref[i, at] = dv_ref[i, n].astype(BF16)
        return 0

    def finish_q(j, _):
        cos, sin = angles(meta, q_block(meta, j, n_blk), rows, n_docs)
        for n in range(len(heads)):
            jq_ref[j, n * HEAD : (n + 1) * HEAD] = (turned(dq_ref[j, n], cos, -sin) * HEAD**-0.5).astype(BF16)
        return 0

    lax.fori_loop(0, n_k, finish_k, 0)
    lax.fori_loop(0, n_q, finish_q, 0)
    if joins:
        join_kernel(meta, jq_ref, jk_ref, jv_ref, *joins)


def join_kernel(meta, jq_ref, jk_ref, jv_ref, normed_ref, x_ref, ngm_ref, w_ref, go_ref, ng_ref, sums_ref, *refs):
    outs, all_ref = refs[:4], refs[4]
    wide = go_ref.shape[0]
    for third, ref in enumerate((jq_ref, jk_ref, jv_ref)):
        total = mul(ref[0], normed_ref[0])
        for j in range(1, QUADS):
            total = total + mul(ref[j], normed_ref[j])
        all_ref[third * wide : (third + 1) * wide] = total
    all_ref[3 * wide :] = go_ref[...]
    put_pieces(all_ref, meta, outs, 0)
    sums_ref[...] = jnp.zeros_like(sums_ref)

    def block(n, _):
        for j in (2 * n, 2 * n + 1):
            joined = jnp.concatenate([jq_ref[j], jk_ref[j], jv_ref[j]], axis=0)
            ng = ngm_ref[j].astype(F32) + mul(joined, w_ref[...], TN)
            ng_ref[j] = ng.astype(BF16)
            x = x_ref[j].astype(F32)
            centred = x - jnp.mean(x, axis=1, keepdims=True)
            xhat = centred * lax.rsqrt(jnp.mean(centred * centred, axis=1, keepdims=True) + norm_eps)
            sums_ref[0:1] += jnp.sum(ng * xhat, axis=0, keepdims=True)
            sums_ref[1:2] += jnp.sum(ng, axis=0, keepdims=True)
        return 0

    lax.fori_loop(0, QUADS // 2, block, 0)


def join_parts(normed, x, ngm, w_cut, grad_out):
    wide, width = grad_out.shape
    results = [sds(x.shape, BF16), sds((8, width), F32)] + [sds((1, wide, width), BF16)] * 4
    return [normed, x, ngm, w_cut, grad_out], results, [pltpu.VMEM((4 * wide, width), F32)]


def join(meta, grads, *rest):
    operands, outs, scratch = join_parts(*rest)
    operands = list(grads) + operands
    return call(
        join_kernel,
        "join",
        meta,
        (1,),
        operands,
        [once(a.shape) for a in operands],
        outs,
        [once(o.shape) for o in outs],
        0,
        0,
        scratch=scratch,
    )


def attend_back(meta, q, do, lse, delta, kn, vn, k, n_blk, n_docs, rest):
    n_q, wide, rows = q.shape
    n_k = k.shape[0]
    n_heads = wide // HEAD
    pairs = 0.56 * n_q * n_k
    outs = [sds((n_q, wide, rows), BF16), sds((n_k, wide, rows), BF16), sds((n_k, wide, rows), BF16)]
    grads = [pltpu.VMEM(o.shape, BF16) for o in outs] if rest else []
    operands = [q, do, lse, delta, kn, vn, k]
    scratch = []
    if rest:
        more, outs, scratch = join_parts(*rest)
        operands += more

    def body(meta_ref, *refs):
        back_kernel(range(n_heads), n_blk, n_docs, n_q, n_k, meta_ref, *refs[: len(refs) - 7 - len(grads)], *refs[len(refs) - len(grads) :], *refs[len(refs) - 7 - len(grads) : len(refs) - len(grads)])

    return call(
        body,
        "attend_back",
        meta,
        (1,),
        operands,
        [once(a.shape) for a in operands],
        outs,
        [once(o.shape) for o in outs],
        pairs * n_heads * rows * rows * 256 * 2 * 2.5,
        16 * n_q * rows * wide,
        pairs * n_heads * rows * rows,
        scratch=scratch
        + [
            pltpu.VMEM((n_q, n_heads, HEAD, rows), F32),
            pltpu.VMEM((n_k, n_heads, HEAD, rows), F32),
            pltpu.VMEM((n_k, n_heads, HEAD, rows), F32),
            pltpu.VMEM((2, 2 * n_heads, rows, rows), BF16),
            pltpu.VMEM((2, 2 * n_heads, rows, rows), BF16),
            pltpu.SMEM((n_q * n_k + 2,), jnp.int32),
            pltpu.SMEM((n_q * n_k + 2,), jnp.int32),
        ]
        + grads,
    )


def swap(x, axis, size, mask):
    return lax.ppermute(x, axis, [(i, i ^ mask) for i in range(size)])


def add(a, b):
    return a.astype(F32) + b.astype(F32)


class Order:
    def __init__(self, sizes):
        self.sizes = sizes
        self.token = []

    def hold(self, arrays):
        arrays = list(arrays)
        held = lax.optimization_barrier(tuple(arrays) + tuple(self.token))
        return list(held[: len(arrays)])

    def done(self, results):
        self.token = jax.tree.leaves(results)[:1]
        return results

    def send(self, exchanges):
        if not isinstance(exchanges[0], tuple):
            return exchanges
        sent = self.hold([array for array, _, _ in exchanges])
        self.token = sent
        return [swap(a, axis, self.sizes[axis], mask) for a, (_, axis, mask) in zip(sent, exchanges)]

    def start(self, generator):
        return Steps(generator, self)

    def advance(self, *chains):
        for chain in chains:
            chain.advance()


class Steps:
    def __init__(self, generator, order):
        self.generator, self.order = generator, order
        self.held = order.send(next(generator))

    def advance(self):
        self.held = self.order.send(self.generator.send(self.order.hold(self.held)))

    def end(self):
        try:
            while True:
                self.advance()
        except StopIteration:
            return self.held


def reduce_pieces(parts):
    got = yield [(part, "dp", k + 1) for k, part in enumerate(parts[1:])]
    return [(add(parts[0], got[0]) + add(got[1], got[2])).astype(BF16)]


def reduce_halves(parts, n_blk):
    send_a, keep_a, send_b, keep_b = parts
    got_a, got_b = yield [(send_a, "dp", 1), (send_b, "dp", 2)]
    sum_a, sum_b = add(keep_a, got_a).astype(BF16), add(keep_b, got_b).astype(BF16)
    got_a, got_b = yield [(sum_a[1], "dp", 2), (sum_b[1], "dp", 1)]
    own = jnp.stack([add(sum_a[0], got_a), add(sum_b[0], got_b)]).astype(BF16)
    (got,) = yield [(own, "blk", n_blk // 2)]
    yield [add(own, got).astype(BF16)]


def sum_halves(own, n_blk):
    (got,) = yield [(own, "blk", n_blk // 2)]
    total = add(own, got).astype(BF16)
    yield from spread_pieces(total.reshape(2, -1, total.shape[1]))


def spread_pieces(total):
    (near,) = yield [(total, "blk", 2)]
    pair_a, pair_b = jnp.stack([total[0], near[0]]), jnp.stack([total[1], near[1]])
    got_a, got_b = yield [(pair_a, "dp", 1), (pair_b, "dp", 2)]
    two = [jnp.stack([pair_a, got_a]), jnp.stack([pair_b, got_b])]
    *far, twin_a, twin_b = yield [(two[0], "dp", 2), (two[1], "dp", 1)] + [(o, "blk", 1) for o in two]
    far_twins = yield [(o, "blk", 1) for o in far]
    yield two + far + [twin_a, twin_b] + far_twins


def placed(k, outer, meta, rows):
    b, far = k % 2, (k // 2) % 2
    cx = jnp.bitwise_xor(meta[X_POS], far if b else outer)
    cy = jnp.bitwise_xor(meta[Y_POS], outer if b else far)
    return ((cx * 2 + cy) * 2 + b) * rows


def fill_kernel(meta, *refs):
    srcs, out_ref = refs[:8], refs[8]
    rows = srcs[0].shape[2]
    for core in range(2):

        @pl.when(pl.program_id(0) // 2 == core)
        def _():
            for k in range(4):
                for outer in range(2):
                    at = pl.multiple_of(placed(k, outer, meta, rows), 16)
                    out_ref[pl.ds(at, rows), :] = srcs[k + 4 * core][outer, 0].astype(F32)


def fill(meta, arrays, shape):
    _, _, rows, width = arrays[0].shape
    across = shape[1] > shape[0]

    def at(i, s):
        shard = jnp.bitwise_xor(s[QUARTER], lax.rem(i, 2) * 2 + i // 2)
        return (0, shard) if across else (shard, 0)

    def source(k):
        return pl.BlockSpec((2, 1, rows, width), lambda i, s: (0, jnp.clip(i - 2 * (k // 4), 0, 1), 0, 0))

    return call(
        fill_kernel,
        "fill",
        meta,
        (TENSOR,),
        list(arrays),
        [source(k) for k in range(8)],
        sds(shape, F32),
        pl.BlockSpec((8 * rows, width), at),
        0,
        6 * 8 * 4 * rows * width,
    )


def tail_kernel(wide, meta, *refs):
    srcs, (gq_ref, go_ref, hold_ref) = refs[:8], refs[8:]
    rows = srcs[0].shape[2]
    i = pl.program_id(0)

    @pl.when(i == 0)
    def _():
        for k, src in enumerate(srcs):
            for outer in range(2):
                row = placed(k % 4, outer, meta, rows)
                for rt1 in range(2):
                    shard = jnp.bitwise_xor(meta[QUARTER], rt1 * 2 + k // 4)
                    at = pl.multiple_of(shard * 4 * wide + row, 16)
                    hold_ref[pl.ds(at, rows), :] = src[outer, rt1].astype(F32)

    def block(part):
        return jnp.concatenate([hold_ref[(4 * s + part) * wide : (4 * s + part + 1) * wide, :] for s in range(TENSOR)], axis=0)

    for third in range(3):

        @pl.when(i == third)
        def _():
            gq_ref[...] = block(third).T

    @pl.when(i == 3)
    def _():
        go_ref[...] = block(3)


def tail(meta, arrays, width, wide):
    outs = [sds((width, 3 * TENSOR * wide), F32), sds((TENSOR * wide, width), F32)]
    return call(
        partial(tail_kernel, wide),
        "tail",
        meta,
        (4,),
        list(arrays),
        [once(a.shape) for a in arrays],
        outs,
        [pl.BlockSpec((width, TENSOR * wide), lambda i, s: (0, jnp.minimum(i, 2))), whole(outs[1].shape)],
        0,
        6 * 4 * width * width,
        scratch=[pltpu.VMEM((TENSOR * 4 * wide, width), F32)],
    )


def natural(parts):
    own, to_x, to_y, across = parts
    return jnp.concatenate([own, to_y, to_x, across], axis=1)


def natural_halves(parts):
    send_a, keep_a, send_b, keep_b = parts
    a = jnp.stack([keep_a, send_a])
    b = jnp.stack([keep_b, send_b], axis=1)
    both = jnp.moveaxis(jnp.stack([a, b], axis=2), 3, 0)
    return both.reshape(both.shape[0], -1, both.shape[-1])


def xor_gather(x, n_blk, masks):
    for mask in reversed(masks):
        x = jnp.concatenate([x, swap(x, "blk", n_blk, mask)])
    return x


def scatter_blocks(blocks, n_blk):
    (got,) = yield [(jnp.concatenate([blocks[6:8], blocks[2:4]]), "blk", 1)]
    far = add(blocks[4:6], got[0:2]).astype(BF16)
    near = add(blocks[0:2], got[2:4]).astype(BF16)
    (far_got,) = yield [(far[1], "blk", 2)]
    far_sum = add(far[0], far_got).astype(BF16)
    other, near_got = yield [(far_sum, "blk", n_blk // 2), (near[1], "blk", 2)]
    yield [add(near[0], near_got).astype(BF16), other]


def local(n_dp, n_blk, tokens, cotangent, lengths, norm_gain, norm_bias, w_qkv, w_out, w_up, w_down):
    micro_count, rows, width = tokens.shape
    n_docs = lengths.shape[2]
    n_heads = width // HEAD // TENSOR
    wide = n_heads * HEAD
    inner = w_up.shape[1] // TENSOR
    splits = n_blk // (2 * TENSOR)
    s_masks = [TENSOR << b for b in reversed(range(splits.bit_length() - 1))]
    fast = n_dp == 4 and splits == 1
    me = lax.axis_index("blk")
    dp = lax.axis_index("dp")
    half = me // (n_blk // 2)
    quarter = lax.rem(me, TENSOR)
    x_pos, y_pos = (lax.rem(dp, 2), dp // 2) if fast else (0 * dp, 0 * dp)
    docs = lax.dynamic_index_in_dim(lengths, half, 0, False)[0]
    firsts = jnp.cumsum(docs, dtype=jnp.int32) - docs
    meta = jnp.concatenate([jnp.stack([quarter, x_pos, y_pos, me, half]).astype(jnp.int32), firsts])

    gain = norm_gain.astype(F32).reshape(1, width)
    bias = norm_bias.astype(F32).reshape(1, width)

    def mine(array):
        return lax.dynamic_index_in_dim(array, half, 0, False), lax.dynamic_index_in_dim(array, 1 - half, 0, False)

    def fourfold(own):
        near, twin = yield [(own, "blk", 2), (own, "blk", 1)]
        (far_twin,) = yield [(near, "blk", 1)]
        yield [own, near, twin, far_twin]

    def cross(array):
        (got,) = yield [(array, "blk", n_blk // 2)]
        yield from fourfold(got)

    order = Order({"dp": n_dp, "blk": n_blk})
    x_mine, x_other = mine(tokens)
    c_mine, c_other = mine(cotangent)
    x_far = order.start(cross(x_other))
    x_near = order.start(fourfold(x_mine))
    w_cut = order.done(cut(meta, w_qkv, wide))
    order.advance(x_near, x_far)
    c_far = order.start(cross(c_other))
    order.advance(x_near)
    stage = order.done(project(meta, order.hold(x_near.held), 0, QUADS, gain, bias, w_cut, n_blk, n_docs, None))
    order.advance(x_far)
    c_near = order.start(fourfold(c_mine))
    order.advance(c_far, x_far)
    stage = order.done(project(meta, order.hold(x_far.held), 4, QUADS, gain, bias, w_cut, n_blk, n_docs, stage))
    x_all, normed, q, k, v, kn, vn = stage
    if splits > 1:
        k, v, kn, vn = (xor_gather(a, n_blk, s_masks) for a in (k, v, kn, vn))
    order.advance(c_near)
    order.advance(c_far, c_near, c_far)
    cot, mo, ngm, *mlp_parts = order.done(feed(meta, normed, order.hold(c_near.held + c_far.held), w_up, w_down))
    if fast:
        mlp = order.start(reduce_halves(mlp_parts, n_blk))
    att, attf, lse = order.done(attend(meta, *order.hold([q]), kn, v, n_blk, n_docs))
    if fast:
        order.advance(mlp)
    out_part, do, delta, grad_out_part = order.done(mix(meta, *order.hold([att, attf, cot, mo]), w_out))
    out_steps = order.start(scatter_blocks(out_part, n_blk))
    if fast:
        order.advance(mlp)
    rest = (normed, x_all, ngm, w_cut, grad_out_part)
    q, do = order.hold([q, do])
    grads = order.done(attend_back(meta, q, do, lse, delta, kn, vn, k, n_blk, n_docs, rest if splits == 1 else None))
    if splits > 1:
        grads = list(grads)
        for at, mask in [(at, mask) for at in (1, 2) for mask in s_masks]:
            count = grads[at].shape[0] // 2
            grads[at] = add(grads[at][:count], swap(grads[at][count:], "blk", n_blk, mask)).astype(BF16)
        grads = order.done(join(meta, grads, *rest))
    ng_part, sums, *rest_parts = grads

    def gather_sums():
        total = sums
        for axis, mask in (("blk", 1), ("dp", 1), ("dp", 2), ("blk", 2), ("blk", n_blk // 2)):
            (got,) = yield [(total, axis, mask)]
            total = total + got
        yield [total]

    if fast:
        order.advance(mlp)
        (total,) = mlp.held

        def of_rest():
            (own,) = yield from reduce_pieces(rest_parts)
            yield from sum_halves(own[0], n_blk)

        makers = {
            "Q": of_rest(),
            "U": spread_pieces(total[:, 0]),
            "D": spread_pieces(total[:, 1]),
            "N": scatter_blocks(ng_part, n_blk),
            "S": gather_sums(),
            "O": out_steps,
        }
        chains = {"O": out_steps}
        for name in TAIL:
            if name == "u":
                grad_up = order.done(fill(meta, order.hold(chains["U"].end()), w_up.shape))
            elif name == "d":
                grad_down = order.done(fill(meta, order.hold(chains["D"].end()), w_down.shape))
            elif name in chains:
                order.advance(chains[name])
            else:
                chains[name] = order.start(makers[name])
        ng_steps, norm_steps, rest = (chains[name] for name in "NSQ")
    else:
        ng_steps = order.start(scatter_blocks(ng_part, n_blk))

    def ordered(own, other):
        return jnp.where(half == 0, jnp.stack([own, other]), jnp.stack([other, own])).astype(F32)

    output = (tokens.astype(F32) + ordered(*out_steps.end())).astype(BF16)
    normed_grad = ordered(*ng_steps.end())
    x_rows = tokens.astype(F32)
    centred = x_rows - jnp.mean(x_rows, axis=2, keepdims=True)
    inverse = lax.rsqrt(jnp.mean(centred * centred, axis=2, keepdims=True) + norm_eps)
    scaled = centred * inverse
    scaled_grad = normed_grad * norm_gain.astype(F32)
    input_grad = cotangent.astype(F32) + inverse * (
        scaled_grad
        - jnp.mean(scaled_grad, axis=2, keepdims=True)
        - scaled * jnp.mean(scaled_grad * scaled, axis=2, keepdims=True)
    )

    if fast:
        grad_qkv, grad_out = tail(meta, rest.end(), width, wide)
        (norm_sums,) = norm_steps.end()
    else:
        up, down = natural_halves(mlp_parts)
        (rest,) = natural(rest_parts)
        turn = rest[: 3 * wide].T.reshape(width, 3, wide)
        zeros = partial(jnp.zeros, dtype=BF16)
        up = lax.dynamic_update_slice_in_dim(zeros(w_up.shape), up, quarter * inner, 1)
        down = lax.dynamic_update_slice_in_dim(zeros(w_down.shape), down, quarter * inner, 0)
        turn = lax.dynamic_update_slice_in_dim(zeros((width, 3, TENSOR * wide)), turn, quarter * wide, 2)
        out = lax.dynamic_update_slice_in_dim(zeros(w_out.shape), rest[3 * wide :], quarter * wide, 0)
        grads = lax.psum((up, down, turn, out), ("dp", "blk"))
        grad_up, grad_down, turn, grad_out = (g.astype(F32) for g in grads)
        grad_qkv = turn.reshape(w_qkv.shape)
        norm_sums = lax.psum(sums, ("dp", "blk"))
    return (output, input_grad, norm_sums[0], norm_sums[1], grad_qkv, grad_out, grad_up, grad_down)


def solution(mesh):
    tokens = P(None, ("dp", "blk"), None)
    return jax.shard_map(
        partial(local, mesh.shape["dp"], mesh.shape["blk"]),
        mesh=mesh,
        in_specs=(tokens, tokens, P(None, "dp", None)) + (P(),) * 6,
        out_specs=(tokens, tokens) + (P(),) * 6,
        check_vma=False,
    )
```

```python
from functools import partial

import jax
import jax.numpy as jnp
from jax import lax
from jax.experimental import pallas as pl
from jax.experimental.pallas import tpu as pltpu
from jax.sharding import PartitionSpec as P

HEAD = 64
ROT = 16
TENSOR = 4
QUADS = 8
norm_eps = 1e-05
masked_score = -1e30
F32 = jnp.float32
BF16 = jnp.bfloat16
VMEM_LIMIT = 56 * 1024 * 1024
COST = 0.02
ATTEND_PAIRS = 9
BACK_PAIRS = 3
TAIL = "NMQONMQQOMMNQmNQnQ"

NN = (((1,), (0,)), ((), ()))
NT = (((1,), (1,)), ((), ()))
TN = (((0,), (0,)), ((), ()))

QUARTER, X_POS, Y_POS, PLACE, HALF, DOCS = range(6)


def mul(a, b, dims=NN):
    return lax.dot_general(a, b, dims, preferred_element_type=F32)


def sds(shape, dtype):
    return jax.ShapeDtypeStruct(tuple(shape), dtype)


def whole(shape):
    return pl.BlockSpec(tuple(shape), lambda *_: (0,) * len(shape))


def once(shape):
    return pl.BlockSpec(tuple(shape), lambda *_: (0,) * len(shape), pipeline_mode=pl.Buffered(1))


def rows_at(shape, base=0, count=1):
    zeros = (0,) * (len(shape) - 1)
    return pl.BlockSpec((count,) + tuple(shape[1:]), lambda i, s: (i + base,) + zeros)


def call(body, name, meta, grid, operands, in_specs, out_shapes, out_specs, flops, moved, special=0, scratch=(), aliases=None, after=()):
    after = list(after)
    n_in = len(operands)

    def kernel(meta_ref, *refs):
        body(meta_ref, *refs[:n_in], *refs[n_in + len(after) :])

    return pl.pallas_call(
        kernel,
        out_shape=out_shapes,
        grid_spec=pltpu.PrefetchScalarGridSpec(
            num_scalar_prefetch=1,
            grid=grid,
            in_specs=list(in_specs) + [pl.BlockSpec(memory_space=pl.ANY)] * len(after),
            out_specs=out_specs,
            scratch_shapes=list(scratch),
        ),
        input_output_aliases=aliases or {},
        compiler_params=pltpu.CompilerParams(
            dimension_semantics=("arbitrary",) * len(grid), vmem_limit_bytes=VMEM_LIMIT
        ),
        cost_estimate=pl.CostEstimate(flops=int(flops * COST), bytes_accessed=int(moved * COST), transcendentals=int(special * COST)),
        name=name,
    )(meta, *operands, *after)


def place_mask(j, n_blk):
    return (j // 4) * (n_blk // 2) + lax.rem(j, 2) * 2 + lax.rem(j // 2, 2)


def q_block(meta, j, n_blk):
    return jnp.bitwise_xor(meta[PLACE], place_mask(j, n_blk))


def k_block(meta, i, n_blk):
    return jnp.bitwise_xor(q_block(meta, lax.rem(i, QUADS), n_blk), (i // QUADS) * TENSOR)


def k_slot(meta, block, n_blk):
    r = jnp.bitwise_xor(meta[PLACE], block)
    low = lax.rem(r, TENSOR)
    split = lax.rem(r, n_blk // 2) // TENSOR
    return split * QUADS + (r // (n_blk // 2)) * 4 + lax.rem(low, 2) * 2 + low // 2


def doc_start(meta, index, n_docs):
    start = jnp.zeros_like(index)
    for d in range(n_docs):
        first = meta[DOCS + d]
        start = jnp.where(index >= first, first, start)
    return start


def token_index(block, rows):
    return block * rows + lax.broadcasted_iota(jnp.int32, (1, rows), 1)


def angles(meta, block, rows, n_docs):
    index = token_index(block, rows)
    position = (index - doc_start(meta, index, n_docs)).astype(F32)
    order = lax.broadcasted_iota(jnp.int32, (ROT // 2, 1), 0)
    frequency = jnp.ones((ROT // 2, 1), F32)
    for i in range(1, ROT // 2):
        frequency = jnp.where(order == i, 10000.0 ** (-2.0 * i / ROT), frequency)
    phases = position * frequency
    return jnp.cos(phases), jnp.sin(phases)


def turned(head, cos, sin):
    a, b = head[: ROT // 2], head[ROT // 2 : ROT]
    return jnp.concatenate([a * cos - b * sin, b * cos + a * sin, head[ROT:]], axis=0)


def cut_kernel(wide, meta, *refs):
    srcs, out_ref, hold_ref = refs[:3], refs[3], refs[4]
    first = pl.multiple_of(lax.rem(meta[QUARTER], 2) * wide, 16)
    for third in range(3):
        hold_ref[...] = srcs[third][...].astype(F32).T
        out_ref[third * wide : (third + 1) * wide, :] = hold_ref[pl.ds(first, wide), :].astype(BF16)


def cut(meta, w_qkv, wide):
    width = w_qkv.shape[0]
    per = w_qkv.shape[1] // 3 // (2 * wide)

    def spec(third):
        return pl.BlockSpec((width, 2 * wide), lambda i, s: (0, third * per + s[QUARTER] // 2))

    return call(
        partial(cut_kernel, wide),
        "cut",
        meta,
        (1,),
        [w_qkv] * 3,
        [spec(third) for third in range(3)],
        sds((3 * wide, width), BF16),
        whole((3 * wide, width)),
        0,
        18 * wide * width,
        scratch=[pltpu.VMEM((2 * wide, width), F32)],
    )


def pick_kernel(meta, src_ref, out_ref):
    out_ref[...] = src_ref[0]


def pick(meta, array, other, after=()):
    _, rows, width = array.shape
    return call(
        pick_kernel,
        "pick",
        meta,
        (1,),
        [array],
        [pl.BlockSpec((1, rows, width), lambda i, s: ((1 - s[HALF]) if other else s[HALF], 0, 0))],
        sds((rows, width), array.dtype),
        whole((rows, width)),
        0,
        4 * rows * width,
        after=after,
    )


def project_kernel(n_heads, n_blk, n_docs, base, meta, *refs):
    pieces, (gain_ref, bias_ref, w_ref) = refs[:4], refs[4:7]
    x_ref, normed_ref, q_ref, k_ref, v_ref, kn_ref, vn_ref = refs[-7:]
    i = pl.program_id(0)
    rows = x_ref.shape[1]
    wide = n_heads * HEAD
    for k in range(4):

        @pl.when(i == k // 2)
        def _():
            x_ref[k % 2] = pieces[k][...]

    for b in range(2):
        x = x_ref[b].astype(F32)
        mean = jnp.mean(x, axis=1, keepdims=True)
        centred = x - mean
        inverse = lax.rsqrt(jnp.mean(centred * centred, axis=1, keepdims=True) + norm_eps)
        normed_ref[b] = (centred * inverse * gain_ref[...] + bias_ref[...]).astype(BF16)
    flats = [mul(w_ref[...], normed_ref[b], NT) for b in range(2)]
    for b in range(2):
        flat = flats[b]
        cos, sin = angles(meta, q_block(meta, 2 * i + b + base, n_blk), rows, n_docs)
        for h in range(n_heads):
            at = slice(h * HEAD, (h + 1) * HEAD)
            q_ref[b, at] = (turned(flat[at], cos, sin) * HEAD**-0.5).astype(BF16)
            key = turned(flat[wide + h * HEAD : wide + (h + 1) * HEAD], cos, sin)
            k_ref[b, at] = key.astype(BF16)
            kn_ref[b, h] = key.T.astype(BF16)
            value = flat[2 * wide + h * HEAD : 2 * wide + (h + 1) * HEAD]
            v_ref[b, at] = value.astype(BF16)
            vn_ref[b, h] = value.T.astype(BF16)


def project(meta, pieces, base, total, gain, bias, w_cut, n_blk, n_docs, earlier, after=()):
    rows, width = pieces[0].shape
    wide = w_cut.shape[0] // 3
    n_heads = wide // HEAD
    outs = [
        sds((total, rows, width), BF16),
        sds((total, rows, width), BF16),
        sds((total, wide, rows), BF16),
        sds((total, wide, rows), BF16),
        sds((total, wide, rows), BF16),
        sds((total, n_heads, rows, HEAD), BF16),
        sds((total, n_heads, rows, HEAD), BF16),
    ]
    operands = list(pieces) + [gain, bias, w_cut]
    specs = [whole(o.shape) for o in operands]
    aliases = {}
    if earlier is not None:
        aliases = {1 + len(operands) + k: k for k in range(len(outs))}
        operands += list(earlier)
        specs += [pl.BlockSpec(memory_space=pl.ANY)] * len(outs)
    return call(
        partial(project_kernel, n_heads, n_blk, n_docs, base),
        "project",
        meta,
        (2,),
        operands,
        specs,
        outs,
        [rows_at(o.shape, base // 2, 2) for o in outs],
        8 * rows * width * 3 * wide,
        4 * rows * width * 10,
        aliases=aliases,
        after=after,
    )


def list_pairs(meta, base, count, rows, n_blk, n_docs, q_list, k_list):
    def of_block(j, found):
        block = q_block(meta, base + j, n_blk)
        first = doc_start(meta, block * rows, n_docs) // rows

        def put(kb, at):
            q_list[at] = j
            k_list[at] = kb
            return at + 1

        return lax.fori_loop(first, block + 1, put, found)

    return lax.fori_loop(0, count, of_block, jnp.int32(0))


def seen(meta, kb, block, rows, n_docs):
    index = token_index(block, rows)
    k_index = kb * rows + lax.broadcasted_iota(jnp.int32, (rows, rows), 0)
    return (k_index >= doc_start(meta, index, n_docs)) & (k_index <= index)


def attend_kernel(n_heads, n_blk, n_docs, meta, q_ref, kn_ref, v_ref, att_ref, lse_ref, s_ref, acc_ref, top_ref, sum_ref, q_list, k_list):
    count, _, rows = q_ref.shape
    heads = range(n_heads)
    base = pl.program_id(0) * count
    found = list_pairs(meta, base, count, rows, n_blk, n_docs, q_list, k_list)
    for extra in range(ATTEND_PAIRS - 1):
        q_list[found + extra] = count
        k_list[found + extra] = 0
    steps = (found + ATTEND_PAIRS - 1) // ATTEND_PAIRS
    top_ref[...] = jnp.full_like(top_ref, masked_score)
    sum_ref[...] = jnp.zeros_like(sum_ref)
    acc_ref[...] = jnp.zeros_like(acc_ref)

    def fold(tile, how):
        return how(tile.reshape(rows // 8, 8, rows), axis=0)

    def score(n, _):
        for at in [ATTEND_PAIRS * n + e for e in range(ATTEND_PAIRS)]:
            j, kb = q_list[at], k_list[at]
            jq = jnp.minimum(j, count - 1)
            ka = k_slot(meta, kb, n_blk)
            allowed = seen(meta, kb, q_block(meta, base + jq, n_blk), rows, n_docs)
            scores = [mul(kn_ref[ka, h], q_ref[jq, h * HEAD : (h + 1) * HEAD]) for h in heads]
            for h in heads:
                s = jnp.where(allowed, scores[h], masked_score)
                s_ref[at, h] = s
                top_ref[j, h] = jnp.maximum(top_ref[j, h], fold(s, jnp.max))
        return 0

    lax.fori_loop(0, steps, score, 0)

    def settle(j, _):
        for h in heads:
            top_ref[j, h, 0:1] = jnp.max(top_ref[j, h], axis=0, keepdims=True)
        return 0

    lax.fori_loop(0, count + 1, settle, 0)

    def weigh(n, _):
        many = [ATTEND_PAIRS * n + e for e in range(ATTEND_PAIRS)]
        weights = []
        for at in many:
            j = q_list[at]
            for h in heads:
                p = jnp.exp(s_ref[at, h] - top_ref[j, h, 0:1])
                sum_ref[j, h] += fold(p, jnp.sum)
                weights.append(p.astype(BF16))
        for m, at in enumerate(many):
            j, ka = q_list[at], k_slot(meta, k_list[at], n_blk)
            for h in heads:
                acc_ref[j, h] += mul(v_ref[ka, h * HEAD : (h + 1) * HEAD], weights[m * n_heads + h])
        return 0

    lax.fori_loop(0, steps, weigh, 0)
    lse_ref[...] = jnp.zeros_like(lse_ref)

    def finish(j, _):
        for h in heads:
            at = slice(h * HEAD, (h + 1) * HEAD)
            total = jnp.sum(sum_ref[j, h], axis=0, keepdims=True)
            att_ref[j, at] = (acc_ref[j, h] / total).astype(BF16)
            lse_ref[j, h : h + 1] = top_ref[j, h, 0:1] + jnp.log(total)
        return 0

    lax.fori_loop(0, count, finish, 0)


def attend(meta, q, kn, v, n_blk, n_docs, after=()):
    n, wide, rows = q.shape
    n_k, n_heads = kn.shape[:2]
    pairs = 0.56 * n * n_k
    count = n if n_k == n else 1
    most = (n * (n + 1) // 2 if n_k == n else n_k) + ATTEND_PAIRS
    outs = [sds((n, wide, rows), BF16), sds((n, 8, rows), F32)]

    def some(shape):
        zeros = (0,) * (len(shape) - 1)
        return pl.BlockSpec((count,) + tuple(shape[1:]), lambda i, s: (i,) + zeros)

    return call(
        partial(attend_kernel, n_heads, n_blk, n_docs),
        "attend",
        meta,
        (n // count,),
        [q, kn, v],
        [some(q.shape), once(kn.shape), once(v.shape)],
        outs,
        [some(o.shape) for o in outs],
        pairs * n_heads * rows * rows * 256 * 2,
        16 * n * rows * wide,
        pairs * n_heads * rows * rows,
        scratch=[
            pltpu.VMEM((most, n_heads, rows, rows), F32),
            pltpu.VMEM((count + 1, n_heads, HEAD, rows), F32),
            pltpu.VMEM((count + 1, n_heads, 8, rows), F32),
            pltpu.VMEM((count + 1, n_heads, 8, rows), F32),
            pltpu.SMEM((most,), jnp.int32),
            pltpu.SMEM((most,), jnp.int32),
        ],
        after=after,
    )


def gelu_pair(hidden):
    bell = jnp.exp(hidden * hidden * -0.5)
    t = 1.0 / (1.0 + (0.3275911 * 0.5**0.5) * jnp.abs(hidden))
    tail = ((((0.5 * 1.061405429 * t - 0.5 * 1.453152027) * t + 0.5 * 1.421413741) * t - 0.5 * 0.284496736) * t + 0.5 * 0.254829592) * t * bell
    cdf = jnp.where(hidden >= 0, 1.0 - tail, tail)
    return hidden * cdf, cdf + hidden * bell * 0.3989422804014327


def put_pieces(scratch, meta, outs, slot):
    rows = scratch.shape[0] // 4
    for k, out in enumerate(outs):
        cx, cy = jnp.bitwise_xor(meta[X_POS], k % 2), jnp.bitwise_xor(meta[Y_POS], k // 2)
        out[slot] = scratch[pl.ds(pl.multiple_of((cx * 2 + cy) * rows, 16), rows), :].astype(BF16)


def put_halves(scratch, meta, outs, slot):
    x, y = meta[X_POS], meta[Y_POS]
    rows = scratch.shape[0] // 8

    def part(cx, cy, b):
        return scratch[pl.ds(pl.multiple_of(((cx * 2 + cy) * 2 + b) * rows, 16), rows), :].astype(BF16)

    for other in range(2):
        cx, cy = jnp.bitwise_xor(x, other), jnp.bitwise_xor(y, other)
        outs[0][other, slot] = part(1 - x, cy, 0)
        outs[1][other, slot] = part(x, cy, 0)
        outs[2][other, slot] = part(cx, 1 - y, 1)
        outs[3][other, slot] = part(cx, y, 1)


def feed_kernel(meta, *refs):
    pieces, (normed_ref, up_ref, down_ref), (cot_ref, mo_ref, ng_ref), outs, (gup_ref, gdn_ref) = (
        refs[:QUADS],
        refs[QUADS : QUADS + 3],
        refs[QUADS + 3 : QUADS + 6],
        refs[QUADS + 6 : -2],
        refs[-2:],
    )
    i = pl.program_id(0)
    rows, width = pieces[0].shape
    for k in range(QUADS):

        @pl.when(i == k // 2)
        def _():
            cot_ref[k % 2] = pieces[k][...]

    @pl.when(i == 0)
    def _():
        gup_ref[...] = jnp.zeros_like(gup_ref)
        gdn_ref[...] = jnp.zeros_like(gdn_ref)

    normed = normed_ref[...].reshape(2 * rows, width)
    cot = cot_ref[...].reshape(2 * rows, width)
    inner = up_ref.shape[1]
    chunk = inner // 3 if inner % 768 == 0 else inner
    spans = [slice(c, c + chunk) for c in range(0, inner, chunk)]

    def open_up(at):
        return mul(normed, up_ref[:, at]), mul(cot, down_ref[at, :], NT)

    opened = [open_up(at) for at in spans[:2]]
    mo = ng = None
    for c, at in enumerate(spans):
        hidden, active_grad = opened[c]
        active, slope = gelu_pair(hidden)
        active = active.astype(BF16)
        hidden_grad = (active_grad * slope).astype(BF16)
        if c + 2 < len(spans):
            opened.append(open_up(spans[c + 2]))
        part, back = mul(active, down_ref[at, :]), mul(hidden_grad, up_ref[:, at], NT)
        mo, ng = (part, back) if c == 0 else (mo + part, ng + back)
        gdn_ref[at, :] += mul(active, cot, TN)
        gup_ref[:, at] += mul(normed, hidden_grad, TN)
    mo_ref[...] = mo.astype(BF16).reshape(2, rows, width)
    ng_ref[...] = ng.astype(BF16).reshape(2, rows, width)

    @pl.when(i == QUADS // 2 - 1)
    def _():
        put_halves(gup_ref, meta, outs, 0)
        put_halves(gdn_ref, meta, outs, 1)


def feed(meta, normed, pieces, w_up, w_down, after=()):
    rows, width = pieces[0].shape
    inner = w_up.shape[1] // TENSOR
    two = rows_at(normed.shape, 0, 2)
    piece = sds((2, 2, inner // 8, width), BF16)
    return call(
        feed_kernel,
        "feed",
        meta,
        (QUADS // 2,),
        list(pieces) + [normed, w_up, w_down],
        [whole(p.shape) for p in pieces]
        + [
            two,
            pl.BlockSpec((width, inner), lambda i, s: (0, s[QUARTER])),
            pl.BlockSpec((inner, width), lambda i, s: (s[QUARTER], 0)),
        ],
        [sds(normed.shape, BF16)] * 3 + [piece] * 4,
        [two] * 3 + [whole(piece.shape)] * 4,
        12 * QUADS * rows * width * inner,
        8 * QUADS * rows * width + 8 * width * inner,
        scratch=[pltpu.VMEM((width, inner), F32), pltpu.VMEM((inner, width), F32)],
        after=after,
    )


def mix_kernel(n_heads, meta, att_ref, cot_ref, mo_ref, w_ref, out_ref, do_ref, delta_ref, go_ref):
    i = pl.program_id(0)
    w = w_ref[...]
    both = range(2)
    grads = [mul(w, cot_ref[b], NT).astype(BF16) for b in both]
    outs = [mul(att_ref[b], w, TN) for b in both]
    go = mul(att_ref[0], cot_ref[0]) + mul(att_ref[1], cot_ref[1])
    delta_ref[...] = jnp.zeros_like(delta_ref)
    for b in both:
        out_ref[b] = (mo_ref[b].astype(F32) + outs[b]).astype(BF16)
        do_ref[b] = grads[b]
        product = grads[b].astype(F32) * att_ref[b].astype(F32)
        for h in range(n_heads):
            delta_ref[b, h : h + 1] = jnp.sum(product[h * HEAD : (h + 1) * HEAD], axis=0, keepdims=True)

    @pl.when(i == 0)
    def _():
        go_ref[...] = go

    @pl.when(i > 0)
    def _():
        go_ref[...] += go


def mix(meta, att, cot, mo, w_out, after=()):
    n, rows, width = cot.shape
    wide = att.shape[1]
    outs = [
        sds((n, rows, width), BF16),
        sds((n, wide, rows), BF16),
        sds((n, 8, rows), F32),
        sds((wide, width), F32),
    ]
    return call(
        partial(mix_kernel, wide // HEAD),
        "mix",
        meta,
        (n // 2,),
        [att, cot, mo, w_out],
        [rows_at(a.shape, 0, 2) for a in (att, cot, mo)]
        + [pl.BlockSpec((wide, width), lambda i, s: (s[QUARTER], 0))],
        outs,
        [rows_at(o.shape, 0, 2) for o in outs[:3]] + [whole((wide, width))],
        6 * n * rows * width * wide,
        10 * n * rows * width,
        after=after,
    )


def back_kernel(heads, n_blk, n_docs, n_q, n_k, meta, q_ref, do_ref, lse_ref, delta_ref, kn_ref, vn_ref, k_ref, *refs):
    rest, (dq_ref, dk_ref, dv_ref, p_ref, ds_ref, q_list, k_list) = refs[:-7], refs[-7:]
    if len(rest) > 3:
        joins, (jq_ref, jk_ref, jv_ref) = rest[:-3], rest[-3:]
    else:
        joins, (jq_ref, jk_ref, jv_ref) = (), rest
    rows = k_ref.shape[2]
    spots = [slice(h * HEAD, (h + 1) * HEAD) for h in heads]
    dq_ref[...] = jnp.zeros_like(dq_ref)
    dk_ref[...] = jnp.zeros_like(dk_ref)
    dv_ref[...] = jnp.zeros_like(dv_ref)
    found = list_pairs(meta, 0, n_q, rows, n_blk, n_docs, q_list, k_list)

    for extra in range(BACK_PAIRS - 1):
        q_list[found + extra] = n_q - 1
        k_list[found + extra] = q_block(meta, n_q - 1, n_blk) + 1

    def step_pairs(n):
        return [BACK_PAIRS * n + e for e in range(BACK_PAIRS)]

    def parts(n):
        for at in step_pairs(n):
            j, ka = q_list[at], k_slot(meta, jnp.minimum(k_list[at], n_k - 1), n_blk)
            for m, h in enumerate(heads):
                yield at, j, ka, m, h, spots[m]

    def weigh(n):
        slot = lax.rem(n, 2)
        allowed = [seen(meta, k_list[at], q_block(meta, q_list[at], n_blk), rows, n_docs) for at in step_pairs(n)]
        scores = [mul(kn_ref[ka, h], q_ref[j, at]) for _, j, ka, _, h, at in parts(n)]
        grads = [mul(vn_ref[ka, h], do_ref[j, at]) for _, j, ka, _, h, at in parts(n)]
        for c, (_, j, ka, m, h, at) in enumerate(parts(n)):
            p = jnp.where(allowed[c // len(heads)], jnp.exp(scores[c] - lse_ref[j, h : h + 1]), 0.0)
            p_ref[slot, c] = p.astype(BF16)
            ds_ref[slot, c] = (p * (grads[c] - delta_ref[j, h : h + 1])).astype(BF16)

    def gather(n):
        slot = lax.rem(n, 2)
        for c, (_, j, ka, m, h, at) in enumerate(parts(n)):
            dv_ref[ka, m] += mul(do_ref[j, at], p_ref[slot, c], NT)
            dk_ref[ka, m] += mul(q_ref[j, at], ds_ref[slot, c], NT)
            dq_ref[j, m] += mul(k_ref[ka, at], ds_ref[slot, c])

    weigh(0)

    def both(n, _):
        gather(n - 1)
        weigh(n)
        return 0

    steps = (found + BACK_PAIRS - 1) // BACK_PAIRS
    lax.fori_loop(1, steps, both, 0)
    gather(steps - 1)

    def finish_k(i, _):
        cos, sin = angles(meta, k_block(meta, i, n_blk), rows, n_docs)
        for n in range(len(heads)):
            at = slice(n * HEAD, (n + 1) * HEAD)
            jk_ref[i, at] = turned(dk_ref[i, n], cos, -sin).astype(BF16)
            jv_ref[i, at] = dv_ref[i, n].astype(BF16)
        return 0

    def finish_q(j, _):
        cos, sin = angles(meta, q_block(meta, j, n_blk), rows, n_docs)
        for n in range(len(heads)):
            jq_ref[j, n * HEAD : (n + 1) * HEAD] = (turned(dq_ref[j, n], cos, -sin) * HEAD**-0.5).astype(BF16)
        return 0

    lax.fori_loop(0, n_k, finish_k, 0)
    lax.fori_loop(0, n_q, finish_q, 0)
    if joins:
        shard_kernel(meta, jq_ref, jk_ref, jv_ref, *joins)


def shard_kernel(meta, jq_ref, jk_ref, jv_ref, normed_ref, go_ref, *refs):
    outs, all_ref = refs[:4], refs[4]
    wide = go_ref.shape[0]
    for third, ref in enumerate((jq_ref, jk_ref, jv_ref)):
        total = mul(ref[0], normed_ref[0])
        for j in range(1, QUADS):
            total = total + mul(ref[j], normed_ref[j])
        all_ref[third * wide : (third + 1) * wide] = total
    all_ref[3 * wide :] = go_ref[...]
    put_pieces(all_ref, meta, outs, 0)


def shard_parts(normed, grad_out):
    wide, width = grad_out.shape
    return [normed, grad_out], [sds((1, wide, width), BF16)] * 4, [pltpu.VMEM((4 * wide, width), F32)]


def shard(meta, grads, *rest):
    operands, outs, scratch = shard_parts(*rest)
    operands = list(grads) + operands
    return call(
        shard_kernel,
        "shard",
        meta,
        (1,),
        operands,
        [once(a.shape) for a in operands],
        outs,
        [once(o.shape) for o in outs],
        0,
        0,
        scratch=scratch,
    )


def join_kernel(meta, jq_ref, jk_ref, jv_ref, x_ref, ngm_ref, w_ref, ng_ref, sums_ref):
    joined = [jnp.concatenate([jq_ref[b], jk_ref[b], jv_ref[b]], axis=0) for b in range(2)]
    parts = [mul(j, w_ref[...], TN) for j in joined]
    gain = bias = 0.0
    for b in range(2):
        ng = ngm_ref[b].astype(F32) + parts[b]
        ng_ref[b] = ng.astype(BF16)
        x = x_ref[b].astype(F32)
        centred = x - jnp.mean(x, axis=1, keepdims=True)
        xhat = centred * lax.rsqrt(jnp.mean(centred * centred, axis=1, keepdims=True) + norm_eps)
        gain = gain + jnp.sum(ng * xhat, axis=0, keepdims=True)
        bias = bias + jnp.sum(ng, axis=0, keepdims=True)

    @pl.when(pl.program_id(0) == 0)
    def _():
        sums_ref[...] = jnp.zeros_like(sums_ref)

    sums_ref[0:1] += gain
    sums_ref[1:2] += bias


def join(meta, grads, x, ngm, w_cut):
    n, rows, width = x.shape
    tiled = list(grads) + [x, ngm]
    return call(
        join_kernel,
        "join",
        meta,
        (n // 2,),
        tiled + [w_cut],
        [rows_at(a.shape, 0, 2) for a in tiled] + [whole(w_cut.shape)],
        [sds((n, rows, width), BF16), sds((16, width), F32)],
        [rows_at(x.shape, 0, 2), whole((16, width))],
        2 * n * rows * width * w_cut.shape[0],
        10 * n * rows * width,
    )


def attend_back(meta, q, do, lse, delta, kn, vn, k, n_blk, n_docs, rest):
    n_q, wide, rows = q.shape
    n_k = k.shape[0]
    n_heads = wide // HEAD
    pairs = 0.56 * n_q * n_k
    grads = [sds((n_q, wide, rows), BF16), sds((n_k, wide, rows), BF16), sds((n_k, wide, rows), BF16)]
    operands = [q, do, lse, delta, kn, vn, k]
    outs, scratch = grads, []
    if rest:
        more, pieces, scratch = shard_parts(*rest)
        operands += more
        outs = pieces + grads

    def body(meta_ref, *refs):
        ins, refs = refs[: len(operands)], refs[len(operands) :]
        given, held = refs[: len(outs)], refs[len(outs) :]
        joins = ins[7:] + given[:-3] + held[: len(scratch)]
        back_kernel(range(n_heads), n_blk, n_docs, n_q, n_k, meta_ref, *ins[:7], *joins, *given[-3:], *held[len(scratch) :])

    return call(
        body,
        "attend_back",
        meta,
        (1,),
        operands,
        [once(a.shape) for a in operands],
        outs,
        [once(o.shape) for o in outs],
        pairs * n_heads * rows * rows * 256 * 2 * 2.5,
        16 * n_q * rows * wide,
        pairs * n_heads * rows * rows,
        scratch=scratch
        + [
            pltpu.VMEM((n_q, n_heads, HEAD, rows), F32),
            pltpu.VMEM((n_k, n_heads, HEAD, rows), F32),
            pltpu.VMEM((n_k, n_heads, HEAD, rows), F32),
            pltpu.VMEM((2, BACK_PAIRS * n_heads, rows, rows), BF16),
            pltpu.VMEM((2, BACK_PAIRS * n_heads, rows, rows), BF16),
            pltpu.SMEM((n_q * n_k + BACK_PAIRS,), jnp.int32),
            pltpu.SMEM((n_q * n_k + BACK_PAIRS,), jnp.int32),
        ],
    )


def swap(x, axis, size, mask):
    return lax.ppermute(x, axis, [(i, i ^ mask) for i in range(size)])


def add(a, b):
    return a.astype(F32) + b.astype(F32)


class Order:
    def __init__(self, sizes):
        self.sizes = sizes
        self.token = []

    def hold(self, arrays):
        arrays = list(arrays)
        held = lax.optimization_barrier(tuple(arrays) + tuple(self.token))
        return list(held[: len(arrays)])

    def done(self, results):
        self.token = jax.tree.leaves(results)[:1]
        return results

    def send(self, exchanges):
        if not isinstance(exchanges[0], tuple):
            return exchanges
        sent = self.hold([array for array, _, _ in exchanges])
        self.token = sent
        return [swap(a, axis, self.sizes[axis], mask) for a, (_, axis, mask) in zip(sent, exchanges)]

    def start(self, generator):
        return Steps(generator, self)

    def advance(self, *chains):
        for chain in chains:
            chain.advance()


class Steps:
    def __init__(self, generator, order):
        self.generator, self.order = generator, order
        self.held = order.send(next(generator))

    def advance(self):
        self.held = self.order.send(self.generator.send(self.order.hold(self.held)))

    def end(self):
        try:
            while True:
                self.advance()
        except StopIteration:
            return self.held


def reduce_pieces(parts):
    got = yield [(part, "dp", k + 1) for k, part in enumerate(parts[1:])]
    return [(add(parts[0], got[0]) + add(got[1], got[2])).astype(BF16)]


def reduce_halves(parts, n_blk):
    send_a, keep_a, send_b, keep_b = parts
    got_a, got_b = yield [(send_a, "dp", 1), (send_b, "dp", 2)]
    sum_a, sum_b = add(keep_a, got_a).astype(BF16), add(keep_b, got_b).astype(BF16)
    got_a, got_b = yield [(sum_a[1], "dp", 2), (sum_b[1], "dp", 1)]
    own = jnp.stack([add(sum_a[0], got_a), add(sum_b[0], got_b)]).astype(BF16)
    (got,) = yield [(own, "blk", n_blk // 2)]
    yield [add(own, got).astype(BF16)]


def sum_halves(own, sums, n_blk):
    a, b = own.reshape(2, -1, own.shape[1])
    own = jnp.stack([jnp.concatenate([sums, a]), jnp.concatenate([sums, b])])
    (got,) = yield [(own, "blk", n_blk // 2)]
    yield from spread_pieces(add(own, got).astype(BF16))


def spread_pieces(total):
    (near,) = yield [(total, "blk", 2)]
    pair_a, pair_b = jnp.stack([total[0], near[0]]), jnp.stack([total[1], near[1]])
    got_a, got_b = yield [(pair_a, "dp", 1), (pair_b, "dp", 2)]
    two = [jnp.stack([pair_a, got_a]), jnp.stack([pair_b, got_b])]
    *far, twin_a, twin_b = yield [(two[0], "dp", 2), (two[1], "dp", 1)] + [(o, "blk", 1) for o in two]
    far_twins = yield [(o, "blk", 1) for o in far]
    yield two + far + [twin_a, twin_b] + far_twins


def placed(k, outer, meta, rows):
    b, far = k % 2, (k // 2) % 2
    cx = jnp.bitwise_xor(meta[X_POS], far if b else outer)
    cy = jnp.bitwise_xor(meta[Y_POS], outer if b else far)
    return ((cx * 2 + cy) * 2 + b) * rows


def fill_kernel(meta, *refs):
    srcs, (up_ref, down_ref) = refs[:8], refs[8:]
    rows = srcs[0].shape[3]
    for core in range(2):

        @pl.when(pl.program_id(0) // 2 == core)
        def _():
            for k in range(4):
                for outer in range(2):
                    at = pl.ds(pl.multiple_of(placed(k, outer, meta, rows), 16), rows)
                    up_ref[at, :] = srcs[k + 4 * core][outer, 0, 0].astype(F32)
                    down_ref[at, :] = srcs[k + 4 * core][outer, 0, 1].astype(F32)


def fill(meta, arrays, shapes):
    _, _, _, rows, width = arrays[0].shape

    def shard(i, s):
        return jnp.bitwise_xor(s[QUARTER], lax.rem(i, 2) * 2 + i // 2)

    def source(k):
        return pl.BlockSpec((2, 1, 2, rows, width), lambda i, s: (0, jnp.clip(i - 2 * (k // 4), 0, 1), 0, 0, 0))

    block = (8 * rows, width)
    return call(
        fill_kernel,
        "fill",
        meta,
        (TENSOR,),
        list(arrays),
        [source(k) for k in range(8)],
        [sds(shape, F32) for shape in shapes],
        [pl.BlockSpec(block, lambda i, s: (0, shard(i, s))), pl.BlockSpec(block, lambda i, s: (shard(i, s), 0))],
        0,
        12 * 8 * 4 * rows * width,
    )


def tail_kernel(wide, meta, *refs):
    srcs, (gq_ref, go_ref, gain_ref, bias_ref, hold_ref, part_ref) = refs[:8], refs[8:]
    rows = srcs[0].shape[2] - 16
    i = pl.program_id(0)

    @pl.when(i == 0)
    def _():
        for k, src in enumerate(srcs):
            for outer in range(2):
                row = placed(k % 4, outer, meta, rows)
                for rt1 in range(2):
                    shard = jnp.bitwise_xor(meta[QUARTER], rt1 * 2 + k // 4)
                    at = pl.multiple_of(shard * 4 * wide + row, 16)
                    hold_ref[pl.ds(at, rows), :] = src[outer, rt1, 16:].astype(F32)
                    if k % 2 == 0:
                        part_ref[shard * 4 + row // (2 * rows)] = src[outer, rt1, 0:16].astype(F32)
        total = part_ref[0]
        for n in range(1, 4 * TENSOR):
            total = total + part_ref[n]
        gain_ref[...] = total[0]
        bias_ref[...] = total[1]

    def block(part):
        return jnp.concatenate([hold_ref[(4 * s + part) * wide : (4 * s + part + 1) * wide, :] for s in range(TENSOR)], axis=0)

    for third in range(3):

        @pl.when(i == third)
        def _():
            gq_ref[...] = block(third).T

    @pl.when(i == 3)
    def _():
        go_ref[...] = block(3)


def tail(meta, arrays, width, wide):
    outs = [sds((width, 3 * TENSOR * wide), F32), sds((TENSOR * wide, width), F32), sds((width,), F32), sds((width,), F32)]
    return call(
        partial(tail_kernel, wide),
        "tail",
        meta,
        (4,),
        list(arrays),
        [once(a.shape) for a in arrays],
        outs,
        [pl.BlockSpec((width, TENSOR * wide), lambda i, s: (0, jnp.minimum(i, 2)))] + [whole(o.shape) for o in outs[1:]],
        0,
        6 * 4 * width * width,
        scratch=[pltpu.VMEM((TENSOR * 4 * wide, width), F32), pltpu.VMEM((4 * TENSOR, 16, width), F32)],
    )


def natural(parts):
    own, to_x, to_y, across = parts
    return jnp.concatenate([own, to_y, to_x, across], axis=1)


def natural_halves(parts):
    send_a, keep_a, send_b, keep_b = parts
    a = jnp.stack([keep_a, send_a])
    b = jnp.stack([keep_b, send_b], axis=1)
    both = jnp.moveaxis(jnp.stack([a, b], axis=2), 3, 0)
    return both.reshape(both.shape[0], -1, both.shape[-1])


def xor_gather(x, n_blk, masks):
    for mask in reversed(masks):
        x = jnp.concatenate([x, swap(x, "blk", n_blk, mask)])
    return x


def scatter_blocks(blocks, n_blk):
    (got,) = yield [(jnp.concatenate([blocks[6:8], blocks[2:4]]), "blk", 1)]
    far = add(blocks[4:6], got[0:2]).astype(BF16)
    near = add(blocks[0:2], got[2:4]).astype(BF16)
    (far_got,) = yield [(far[1], "blk", 2)]
    far_sum = add(far[0], far_got).astype(BF16)
    other, near_got = yield [(far_sum, "blk", n_blk // 2), (near[1], "blk", 2)]
    yield [add(near[0], near_got).astype(BF16), other]


def local(n_dp, n_blk, tokens, cotangent, lengths, norm_gain, norm_bias, w_qkv, w_out, w_up, w_down):
    micro_count, rows, width = tokens.shape
    n_docs = lengths.shape[2]
    n_heads = width // HEAD // TENSOR
    wide = n_heads * HEAD
    inner = w_up.shape[1] // TENSOR
    splits = n_blk // (2 * TENSOR)
    s_masks = [TENSOR << b for b in reversed(range(splits.bit_length() - 1))]
    fast = n_dp == 4 and splits == 1
    me = lax.axis_index("blk")
    dp = lax.axis_index("dp")
    half = me // (n_blk // 2)
    quarter = lax.rem(me, TENSOR)
    x_pos, y_pos = (lax.rem(dp, 2), dp // 2) if fast else (0 * dp, 0 * dp)
    docs = lax.dynamic_index_in_dim(lengths, half, 0, False)[0]
    firsts = jnp.cumsum(docs, dtype=jnp.int32) - docs
    meta = jnp.concatenate([jnp.stack([quarter, x_pos, y_pos, me, half]).astype(jnp.int32), firsts])

    gain = norm_gain.astype(F32).reshape(1, width)
    bias = norm_bias.astype(F32).reshape(1, width)

    def mine(array):
        return lax.dynamic_index_in_dim(array, half, 0, False), lax.dynamic_index_in_dim(array, 1 - half, 0, False)

    def fourfold(own):
        near, twin = yield [(own, "blk", 2), (own, "blk", 1)]
        (far_twin,) = yield [(near, "blk", 1)]
        yield [own, near, twin, far_twin]

    def cross(array):
        (got,) = yield [(array, "blk", n_blk // 2)]
        yield from fourfold(got)

    order = Order({"dp": n_dp, "blk": n_blk})
    x_mine, x_other = mine(tokens)
    c_mine, c_other = mine(cotangent)
    x_far = order.start(cross(x_other))
    x_near = order.start(fourfold(x_mine))
    w_cut = order.done(cut(meta, w_qkv, wide))
    order.advance(x_near, x_far)
    c_far = order.start(cross(c_other))
    order.advance(x_near)
    stage = order.done(project(meta, order.hold(x_near.held), 0, QUADS, gain, bias, w_cut, n_blk, n_docs, None))
    order.advance(x_far)
    c_near = order.start(fourfold(c_mine))
    order.advance(c_far, x_far)
    stage = order.done(project(meta, order.hold(x_far.held), 4, QUADS, gain, bias, w_cut, n_blk, n_docs, stage))
    x_all, normed, q, k, v, kn, vn = stage
    if splits > 1:
        k, v, kn, vn = (xor_gather(a, n_blk, s_masks) for a in (k, v, kn, vn))
    order.advance(c_near)
    order.advance(c_far, c_near, c_far)
    cot, mo, ngm, *mlp_parts = order.done(feed(meta, normed, order.hold(c_near.held + c_far.held), w_up, w_down))
    if fast:
        mlp = order.start(reduce_halves(mlp_parts, n_blk))
    att, lse = order.done(attend(meta, *order.hold([q]), kn, v, n_blk, n_docs))
    if fast:
        order.advance(mlp)
    out_part, do, delta, grad_out_part = order.done(mix(meta, *order.hold([att, cot, mo]), w_out))
    out_steps = order.start(scatter_blocks(out_part, n_blk))
    if fast:
        order.advance(mlp)
    rest = (normed, grad_out_part)
    q, do = order.hold([q, do])
    back = order.done(attend_back(meta, q, do, lse, delta, kn, vn, k, n_blk, n_docs, rest if splits == 1 else None))
    rest_parts, grads = list(back[:-3]), list(back[-3:])
    if splits > 1:
        for at, mask in [(at, mask) for at in (1, 2) for mask in s_masks]:
            count = grads[at].shape[0] // 2
            grads[at] = add(grads[at][:count], swap(grads[at][count:], "blk", n_blk, mask)).astype(BF16)
        rest_parts = order.done(shard(meta, grads, *rest))
    chains = {"O": out_steps}
    if fast:

        def of_rest():
            (own,) = yield from reduce_pieces(rest_parts)
            yield from sum_halves(own[0], sums.astype(BF16), n_blk)

        order.advance(mlp)
        chains["M"] = order.start(spread_pieces(mlp.held[0]))
        chains["Q"] = order.start(of_rest())
    order.advance(out_steps)
    ng_part, sums = order.done(join(meta, order.hold(grads), x_all, ngm, w_cut))

    def finish():
        def ordered(own, other):
            return jnp.where(half == 0, jnp.stack([own, other]), jnp.stack([other, own])).astype(F32)

        output = (tokens.astype(F32) + ordered(*chains["O"].end())).astype(BF16)
        normed_grad = ordered(*chains["N"].end())
        x_rows = tokens.astype(F32)
        centred = x_rows - jnp.mean(x_rows, axis=2, keepdims=True)
        inverse = lax.rsqrt(jnp.mean(centred * centred, axis=2, keepdims=True) + norm_eps)
        scaled = centred * inverse
        scaled_grad = normed_grad * norm_gain.astype(F32)
        input_grad = cotangent.astype(F32) + inverse * (
            scaled_grad
            - jnp.mean(scaled_grad, axis=2, keepdims=True)
            - scaled * jnp.mean(scaled_grad * scaled, axis=2, keepdims=True)
        )
        return output, input_grad

    if fast:
        for name in TAIL:
            if name == "m":
                grad_up, grad_down = order.done(fill(meta, order.hold(chains["M"].end()), [w_up.shape, w_down.shape]))
            elif name == "n":
                output, input_grad = order.done(finish())
            elif name in chains:
                order.advance(chains[name])
            else:
                chains[name] = order.start(scatter_blocks(ng_part, n_blk))
        grad_qkv, grad_out, *norm_sums = tail(meta, chains["Q"].end(), width, wide)
    else:
        chains["N"] = order.start(scatter_blocks(ng_part, n_blk))
        output, input_grad = finish()
        up, down = natural_halves(mlp_parts)
        (rest,) = natural(rest_parts)
        turn = rest[: 3 * wide].T.reshape(width, 3, wide)
        zeros = partial(jnp.zeros, dtype=BF16)
        up = lax.dynamic_update_slice_in_dim(zeros(w_up.shape), up, quarter * inner, 1)
        down = lax.dynamic_update_slice_in_dim(zeros(w_down.shape), down, quarter * inner, 0)
        turn = lax.dynamic_update_slice_in_dim(zeros((width, 3, TENSOR * wide)), turn, quarter * wide, 2)
        out = lax.dynamic_update_slice_in_dim(zeros(w_out.shape), rest[3 * wide :], quarter * wide, 0)
        summed = lax.psum((up, down, turn, out), ("dp", "blk"))
        grad_up, grad_down, turn, grad_out = (g.astype(F32) for g in summed)
        grad_qkv = turn.reshape(w_qkv.shape)
        norm_sums = lax.psum(sums, ("dp", "blk"))
    return (output, input_grad, norm_sums[0], norm_sums[1], grad_qkv, grad_out, grad_up, grad_down)


def solution(mesh):
    tokens = P(None, ("dp", "blk"), None)
    return jax.shard_map(
        partial(local, mesh.shape["dp"], mesh.shape["blk"]),
        mesh=mesh,
        in_specs=(tokens, tokens, P(None, "dp", None)) + (P(),) * 6,
        out_specs=(tokens, tokens) + (P(),) * 6,
        check_vma=False,
    )
```

```python
from functools import partial

import jax
import jax.numpy as jnp
from jax import lax
from jax.experimental import pallas as pl
from jax.experimental.pallas import tpu as pltpu
from jax.sharding import PartitionSpec as P

HEAD = 64
ROT = 16
TENSOR = 4
QUADS = 8
norm_eps = 1e-05
masked_score = -1e30
F32 = jnp.float32
BF16 = jnp.bfloat16
VMEM_LIMIT = 56 * 1024 * 1024
COST = 0.02
ATTEND_PAIRS = 9
BACK_PAIRS = 3
TAIL = "QMNNMQNQMQMmQnQ"

NN = (((1,), (0,)), ((), ()))
NT = (((1,), (1,)), ((), ()))
TN = (((0,), (0,)), ((), ()))

QUARTER, X_POS, Y_POS, PLACE, HALF, DOCS = range(6)


def mul(a, b, dims=NN):
    return lax.dot_general(a, b, dims, preferred_element_type=F32)


def sds(shape, dtype):
    return jax.ShapeDtypeStruct(tuple(shape), dtype)


def whole(shape):
    return pl.BlockSpec(tuple(shape), lambda *_: (0,) * len(shape))


def once(shape):
    return pl.BlockSpec(tuple(shape), lambda *_: (0,) * len(shape), pipeline_mode=pl.Buffered(1))


def rows_at(shape, base=0, count=1):
    zeros = (0,) * (len(shape) - 1)
    return pl.BlockSpec((count,) + tuple(shape[1:]), lambda i, s: (i + base,) + zeros)


def call(body, name, meta, grid, operands, in_specs, out_shapes, out_specs, flops, moved, special=0, scratch=(), aliases=None, after=()):
    after = list(after)
    n_in = len(operands)

    def kernel(meta_ref, *refs):
        body(meta_ref, *refs[:n_in], *refs[n_in + len(after) :])

    return pl.pallas_call(
        kernel,
        out_shape=out_shapes,
        grid_spec=pltpu.PrefetchScalarGridSpec(
            num_scalar_prefetch=1,
            grid=grid,
            in_specs=list(in_specs) + [pl.BlockSpec(memory_space=pl.ANY)] * len(after),
            out_specs=out_specs,
            scratch_shapes=list(scratch),
        ),
        input_output_aliases=aliases or {},
        compiler_params=pltpu.CompilerParams(
            dimension_semantics=("arbitrary",) * len(grid), vmem_limit_bytes=VMEM_LIMIT
        ),
        cost_estimate=pl.CostEstimate(flops=int(flops * COST), bytes_accessed=int(moved * COST), transcendentals=int(special * COST)),
        name=name,
    )(meta, *operands, *after)


def place_mask(j, n_blk):
    return (j // 4) * (n_blk // 2) + lax.rem(j, 2) * 2 + lax.rem(j // 2, 2)


def q_block(meta, j, n_blk):
    return jnp.bitwise_xor(meta[PLACE], place_mask(j, n_blk))


def k_block(meta, i, n_blk):
    return jnp.bitwise_xor(q_block(meta, lax.rem(i, QUADS), n_blk), (i // QUADS) * TENSOR)


def k_slot(meta, block, n_blk):
    r = jnp.bitwise_xor(meta[PLACE], block)
    low = lax.rem(r, TENSOR)
    split = lax.rem(r, n_blk // 2) // TENSOR
    return split * QUADS + (r // (n_blk // 2)) * 4 + lax.rem(low, 2) * 2 + low // 2


def doc_start(meta, index, n_docs):
    start = jnp.zeros_like(index)
    for d in range(n_docs):
        first = meta[DOCS + d]
        start = jnp.where(index >= first, first, start)
    return start


def token_index(block, rows):
    return block * rows + lax.broadcasted_iota(jnp.int32, (1, rows), 1)


def angles(meta, block, rows, n_docs):
    index = token_index(block, rows)
    position = (index - doc_start(meta, index, n_docs)).astype(F32)
    order = lax.broadcasted_iota(jnp.int32, (ROT // 2, 1), 0)
    frequency = jnp.ones((ROT // 2, 1), F32)
    for i in range(1, ROT // 2):
        frequency = jnp.where(order == i, 10000.0 ** (-2.0 * i / ROT), frequency)
    phases = position * frequency
    return jnp.cos(phases), jnp.sin(phases)


def turned(head, cos, sin):
    a, b = head[: ROT // 2], head[ROT // 2 : ROT]
    return jnp.concatenate([a * cos - b * sin, b * cos + a * sin, head[ROT:]], axis=0)


def cut_kernel(wide, meta, *refs):
    srcs, out_ref, hold_ref = refs[:3], refs[3], refs[4]
    first = pl.multiple_of(lax.rem(meta[QUARTER], 2) * wide, 16)
    for third in range(3):
        hold_ref[...] = srcs[third][...].astype(F32).T
        out_ref[third * wide : (third + 1) * wide, :] = hold_ref[pl.ds(first, wide), :].astype(BF16)


def cut(meta, w_qkv, wide):
    width = w_qkv.shape[0]
    per = w_qkv.shape[1] // 3 // (2 * wide)

    def spec(third):
        return pl.BlockSpec((width, 2 * wide), lambda i, s: (0, third * per + s[QUARTER] // 2))

    return call(
        partial(cut_kernel, wide),
        "cut",
        meta,
        (1,),
        [w_qkv] * 3,
        [spec(third) for third in range(3)],
        sds((3 * wide, width), BF16),
        whole((3 * wide, width)),
        0,
        18 * wide * width,
        scratch=[pltpu.VMEM((2 * wide, width), F32)],
    )


def pick_kernel(meta, src_ref, out_ref):
    out_ref[...] = src_ref[0]


def pick(meta, array, other, after=()):
    _, rows, width = array.shape
    return call(
        pick_kernel,
        "pick",
        meta,
        (1,),
        [array],
        [pl.BlockSpec((1, rows, width), lambda i, s: ((1 - s[HALF]) if other else s[HALF], 0, 0))],
        sds((rows, width), array.dtype),
        whole((rows, width)),
        0,
        4 * rows * width,
        after=after,
    )


def project_kernel(n_heads, n_blk, n_docs, base, meta, *refs):
    pieces, (gain_ref, bias_ref, w_ref) = refs[:4], refs[4:7]
    x_ref, normed_ref, q_ref, k_ref, v_ref, kn_ref, vn_ref = refs[-7:]
    i = pl.program_id(0)
    rows = x_ref.shape[1]
    wide = n_heads * HEAD
    for k in range(4):

        @pl.when(i == k // 2)
        def _():
            x_ref[k % 2] = pieces[k][...]

    for b in range(2):
        x = x_ref[b].astype(F32)
        mean = jnp.mean(x, axis=1, keepdims=True)
        centred = x - mean
        inverse = lax.rsqrt(jnp.mean(centred * centred, axis=1, keepdims=True) + norm_eps)
        normed_ref[b] = (centred * inverse * gain_ref[...] + bias_ref[...]).astype(BF16)
    flats = [mul(w_ref[...], normed_ref[b], NT) for b in range(2)]
    for b in range(2):
        flat = flats[b]
        cos, sin = angles(meta, q_block(meta, 2 * i + b + base, n_blk), rows, n_docs)
        for h in range(n_heads):
            at = slice(h * HEAD, (h + 1) * HEAD)
            q_ref[b, at] = (turned(flat[at], cos, sin) * HEAD**-0.5).astype(BF16)
            key = turned(flat[wide + h * HEAD : wide + (h + 1) * HEAD], cos, sin)
            k_ref[b, at] = key.astype(BF16)
            kn_ref[b, h] = key.T.astype(BF16)
            value = flat[2 * wide + h * HEAD : 2 * wide + (h + 1) * HEAD]
            v_ref[b, at] = value.astype(BF16)
            vn_ref[b, h] = value.T.astype(BF16)


def project(meta, pieces, base, total, gain, bias, w_cut, n_blk, n_docs, earlier, after=()):
    rows, width = pieces[0].shape
    wide = w_cut.shape[0] // 3
    n_heads = wide // HEAD
    outs = [
        sds((total, rows, width), BF16),
        sds((total, rows, width), BF16),
        sds((total, wide, rows), BF16),
        sds((total, wide, rows), BF16),
        sds((total, wide, rows), BF16),
        sds((total, n_heads, rows, HEAD), BF16),
        sds((total, n_heads, rows, HEAD), BF16),
    ]
    operands = list(pieces) + [gain, bias, w_cut]
    specs = [whole(o.shape) for o in operands]
    aliases = {}
    if earlier is not None:
        aliases = {1 + len(operands) + k: k for k in range(len(outs))}
        operands += list(earlier)
        specs += [pl.BlockSpec(memory_space=pl.ANY)] * len(outs)
    return call(
        partial(project_kernel, n_heads, n_blk, n_docs, base),
        "project",
        meta,
        (2,),
        operands,
        specs,
        outs,
        [rows_at(o.shape, base // 2, 2) for o in outs],
        8 * rows * width * 3 * wide,
        4 * rows * width * 10,
        aliases=aliases,
        after=after,
    )


def list_pairs(meta, base, count, rows, n_blk, n_docs, q_list, k_list):
    def of_block(j, found):
        block = q_block(meta, base + j, n_blk)
        first = doc_start(meta, block * rows, n_docs) // rows

        def put(kb, at):
            q_list[at] = j
            k_list[at] = kb
            return at + 1

        return lax.fori_loop(first, block + 1, put, found)

    return lax.fori_loop(0, count, of_block, jnp.int32(0))


def seen(meta, kb, block, rows, n_docs):
    index = token_index(block, rows)
    k_index = kb * rows + lax.broadcasted_iota(jnp.int32, (rows, rows), 0)
    return (k_index >= doc_start(meta, index, n_docs)) & (k_index <= index)


def attend_kernel(n_heads, n_blk, n_docs, meta, q_ref, kn_ref, v_ref, att_ref, lse_ref, s_ref, acc_ref, top_ref, sum_ref, q_list, k_list):
    count, _, rows = q_ref.shape
    heads = range(n_heads)
    base = pl.program_id(0) * count
    found = list_pairs(meta, base, count, rows, n_blk, n_docs, q_list, k_list)
    for extra in range(ATTEND_PAIRS - 1):
        q_list[found + extra] = count
        k_list[found + extra] = 0
    steps = (found + ATTEND_PAIRS - 1) // ATTEND_PAIRS
    top_ref[...] = jnp.full_like(top_ref, masked_score)
    sum_ref[...] = jnp.zeros_like(sum_ref)
    acc_ref[...] = jnp.zeros_like(acc_ref)

    def fold(tile, how):
        return how(tile.reshape(rows // 8, 8, rows), axis=0)

    def score(n, _):
        for at in [ATTEND_PAIRS * n + e for e in range(ATTEND_PAIRS)]:
            j, kb = q_list[at], k_list[at]
            jq = jnp.minimum(j, count - 1)
            ka = k_slot(meta, kb, n_blk)
            allowed = seen(meta, kb, q_block(meta, base + jq, n_blk), rows, n_docs)
            scores = [mul(kn_ref[ka, h], q_ref[jq, h * HEAD : (h + 1) * HEAD]) for h in heads]
            for h in heads:
                s = jnp.where(allowed, scores[h], masked_score)
                s_ref[at, h] = s
                top_ref[j, h] = jnp.maximum(top_ref[j, h], fold(s, jnp.max))
        return 0

    lax.fori_loop(0, steps, score, 0)

    def settle(j, _):
        for h in heads:
            top_ref[j, h, 0:1] = jnp.max(top_ref[j, h], axis=0, keepdims=True)
        return 0

    lax.fori_loop(0, count + 1, settle, 0)

    def weigh(n, _):
        many = [ATTEND_PAIRS * n + e for e in range(ATTEND_PAIRS)]
        weights = []
        for at in many:
            j = q_list[at]
            for h in heads:
                p = jnp.exp(s_ref[at, h] - top_ref[j, h, 0:1])
                sum_ref[j, h] += fold(p, jnp.sum)
                weights.append(p.astype(BF16))
        for m, at in enumerate(many):
            j, ka = q_list[at], k_slot(meta, k_list[at], n_blk)
            for h in heads:
                acc_ref[j, h] += mul(v_ref[ka, h * HEAD : (h + 1) * HEAD], weights[m * n_heads + h])
        return 0

    lax.fori_loop(0, steps, weigh, 0)
    lse_ref[...] = jnp.zeros_like(lse_ref)

    def finish(j, _):
        for h in heads:
            at = slice(h * HEAD, (h + 1) * HEAD)
            total = jnp.sum(sum_ref[j, h], axis=0, keepdims=True)
            att_ref[j, at] = (acc_ref[j, h] / total).astype(BF16)
            lse_ref[j, h : h + 1] = top_ref[j, h, 0:1] + jnp.log(total)
        return 0

    lax.fori_loop(0, count, finish, 0)


def attend(meta, q, kn, v, n_blk, n_docs, after=()):
    n, wide, rows = q.shape
    n_k, n_heads = kn.shape[:2]
    pairs = 0.56 * n * n_k
    count = n if n_k == n else 1
    most = (n * (n + 1) // 2 if n_k == n else n_k) + ATTEND_PAIRS
    outs = [sds((n, wide, rows), BF16), sds((n, 8, rows), F32)]

    def some(shape):
        zeros = (0,) * (len(shape) - 1)
        return pl.BlockSpec((count,) + tuple(shape[1:]), lambda i, s: (i,) + zeros)

    return call(
        partial(attend_kernel, n_heads, n_blk, n_docs),
        "attend",
        meta,
        (n // count,),
        [q, kn, v],
        [some(q.shape), once(kn.shape), once(v.shape)],
        outs,
        [some(o.shape) for o in outs],
        pairs * n_heads * rows * rows * 256 * 2,
        16 * n * rows * wide,
        pairs * n_heads * rows * rows,
        scratch=[
            pltpu.VMEM((most, n_heads, rows, rows), F32),
            pltpu.VMEM((count + 1, n_heads, HEAD, rows), F32),
            pltpu.VMEM((count + 1, n_heads, 8, rows), F32),
            pltpu.VMEM((count + 1, n_heads, 8, rows), F32),
            pltpu.SMEM((most,), jnp.int32),
            pltpu.SMEM((most,), jnp.int32),
        ],
        after=after,
    )


def gelu_pair(hidden):
    bell = jnp.exp(hidden * hidden * -0.5)
    t = 1.0 / (1.0 + (0.3275911 * 0.5**0.5) * jnp.abs(hidden))
    tail = ((((0.5 * 1.061405429 * t - 0.5 * 1.453152027) * t + 0.5 * 1.421413741) * t - 0.5 * 0.284496736) * t + 0.5 * 0.254829592) * t * bell
    cdf = jnp.where(hidden >= 0, 1.0 - tail, tail)
    return hidden * cdf, cdf + hidden * bell * 0.3989422804014327


def put_pieces(scratch, meta, outs, slot):
    rows = scratch.shape[0] // 4
    for k, out in enumerate(outs):
        cx, cy = jnp.bitwise_xor(meta[X_POS], k % 2), jnp.bitwise_xor(meta[Y_POS], k // 2)
        out[slot] = scratch[pl.ds(pl.multiple_of((cx * 2 + cy) * rows, 16), rows), :].astype(BF16)


def put_halves(scratch, meta, outs, slot):
    x, y = meta[X_POS], meta[Y_POS]
    rows = scratch.shape[0] // 8

    def part(cx, cy, b):
        return scratch[pl.ds(pl.multiple_of(((cx * 2 + cy) * 2 + b) * rows, 16), rows), :].astype(BF16)

    for other in range(2):
        cx, cy = jnp.bitwise_xor(x, other), jnp.bitwise_xor(y, other)
        outs[0][other, slot] = part(1 - x, cy, 0)
        outs[1][other, slot] = part(x, cy, 0)
        outs[2][other, slot] = part(cx, 1 - y, 1)
        outs[3][other, slot] = part(cx, y, 1)


def feed_kernel(meta, *refs):
    pieces, (normed_ref, up_ref, down_ref), (cot_ref, mo_ref, ng_ref), outs, (gup_ref, gdn_ref) = (
        refs[:QUADS],
        refs[QUADS : QUADS + 3],
        refs[QUADS + 3 : QUADS + 6],
        refs[QUADS + 6 : -2],
        refs[-2:],
    )
    i = pl.program_id(0)
    rows, width = pieces[0].shape
    for k in range(QUADS):

        @pl.when(i == k // 2)
        def _():
            cot_ref[k % 2] = pieces[k][...]

    @pl.when(i == 0)
    def _():
        gup_ref[...] = jnp.zeros_like(gup_ref)
        gdn_ref[...] = jnp.zeros_like(gdn_ref)

    normed = normed_ref[...].reshape(2 * rows, width)
    cot = cot_ref[...].reshape(2 * rows, width)
    inner = up_ref.shape[1]
    chunk = inner // 3 if inner % 768 == 0 else inner
    spans = [slice(c, c + chunk) for c in range(0, inner, chunk)]

    def open_up(at):
        return mul(normed, up_ref[:, at]), mul(cot, down_ref[at, :], NT)

    opened = [open_up(at) for at in spans[:2]]
    mo = ng = None
    for c, at in enumerate(spans):
        hidden, active_grad = opened[c]
        active, slope = gelu_pair(hidden)
        active = active.astype(BF16)
        hidden_grad = (active_grad * slope).astype(BF16)
        if c + 2 < len(spans):
            opened.append(open_up(spans[c + 2]))
        part, back = mul(active, down_ref[at, :]), mul(hidden_grad, up_ref[:, at], NT)
        mo, ng = (part, back) if c == 0 else (mo + part, ng + back)
        gdn_ref[at, :] += mul(active, cot, TN)
        gup_ref[:, at] += mul(normed, hidden_grad, TN)
    mo_ref[...] = mo.astype(BF16).reshape(2, rows, width)
    ng_ref[...] = ng.astype(BF16).reshape(2, rows, width)

    @pl.when(i == QUADS // 2 - 1)
    def _():
        put_halves(gup_ref, meta, outs, 0)
        put_halves(gdn_ref, meta, outs, 1)


def feed(meta, normed, pieces, w_up, w_down, after=()):
    rows, width = pieces[0].shape
    inner = w_up.shape[1] // TENSOR
    two = rows_at(normed.shape, 0, 2)
    piece = sds((2, 2, inner // 8, width), BF16)
    return call(
        feed_kernel,
        "feed",
        meta,
        (QUADS // 2,),
        list(pieces) + [normed, w_up, w_down],
        [whole(p.shape) for p in pieces]
        + [
            two,
            pl.BlockSpec((width, inner), lambda i, s: (0, s[QUARTER])),
            pl.BlockSpec((inner, width), lambda i, s: (s[QUARTER], 0)),
        ],
        [sds(normed.shape, BF16)] * 3 + [piece] * 4,
        [two] * 3 + [whole(piece.shape)] * 4,
        12 * QUADS * rows * width * inner,
        8 * QUADS * rows * width + 8 * width * inner,
        scratch=[pltpu.VMEM((width, inner), F32), pltpu.VMEM((inner, width), F32)],
        after=after,
    )


def mix_kernel(n_heads, meta, att_ref, cot_ref, mo_ref, w_ref, out_ref, do_ref, delta_ref, go_ref):
    i = pl.program_id(0)
    w = w_ref[...]
    both = range(2)
    grads = [mul(w, cot_ref[b], NT).astype(BF16) for b in both]
    outs = [mul(att_ref[b], w, TN) for b in both]
    go = mul(att_ref[0], cot_ref[0]) + mul(att_ref[1], cot_ref[1])
    delta_ref[...] = jnp.zeros_like(delta_ref)
    for b in both:
        out_ref[b] = (mo_ref[b].astype(F32) + outs[b]).astype(BF16)
        do_ref[b] = grads[b]
        product = grads[b].astype(F32) * att_ref[b].astype(F32)
        for h in range(n_heads):
            delta_ref[b, h : h + 1] = jnp.sum(product[h * HEAD : (h + 1) * HEAD], axis=0, keepdims=True)

    @pl.when(i == 0)
    def _():
        go_ref[...] = go

    @pl.when(i > 0)
    def _():
        go_ref[...] += go


def mix(meta, att, cot, mo, w_out, after=()):
    n, rows, width = cot.shape
    wide = att.shape[1]
    outs = [
        sds((n, rows, width), BF16),
        sds((n, wide, rows), BF16),
        sds((n, 8, rows), F32),
        sds((wide, width), F32),
    ]
    return call(
        partial(mix_kernel, wide // HEAD),
        "mix",
        meta,
        (n // 2,),
        [att, cot, mo, w_out],
        [rows_at(a.shape, 0, 2) for a in (att, cot, mo)]
        + [pl.BlockSpec((wide, width), lambda i, s: (s[QUARTER], 0))],
        outs,
        [rows_at(o.shape, 0, 2) for o in outs[:3]] + [whole((wide, width))],
        6 * n * rows * width * wide,
        10 * n * rows * width,
        after=after,
    )


def back_kernel(heads, n_blk, n_docs, n_q, n_k, meta, q_ref, do_ref, lse_ref, delta_ref, kn_ref, vn_ref, k_ref, *refs):
    rest, (dq_ref, dk_ref, dv_ref, p_ref, ds_ref, q_list, k_list) = refs[:-7], refs[-7:]
    if len(rest) > 3:
        joins, (jq_ref, jk_ref, jv_ref) = rest[:-3], rest[-3:]
    else:
        joins, (jq_ref, jk_ref, jv_ref) = (), rest
    rows = k_ref.shape[2]
    spots = [slice(h * HEAD, (h + 1) * HEAD) for h in heads]
    dq_ref[...] = jnp.zeros_like(dq_ref)
    dk_ref[...] = jnp.zeros_like(dk_ref)
    dv_ref[...] = jnp.zeros_like(dv_ref)
    found = list_pairs(meta, 0, n_q, rows, n_blk, n_docs, q_list, k_list)

    for extra in range(BACK_PAIRS - 1):
        q_list[found + extra] = n_q - 1
        k_list[found + extra] = q_block(meta, n_q - 1, n_blk) + 1

    def step_pairs(n):
        return [BACK_PAIRS * n + e for e in range(BACK_PAIRS)]

    def parts(n):
        for at in step_pairs(n):
            j, ka = q_list[at], k_slot(meta, jnp.minimum(k_list[at], n_k - 1), n_blk)
            for m, h in enumerate(heads):
                yield at, j, ka, m, h, spots[m]

    def weigh(n):
        slot = lax.rem(n, 2)
        allowed = [seen(meta, k_list[at], q_block(meta, q_list[at], n_blk), rows, n_docs) for at in step_pairs(n)]
        scores = [mul(kn_ref[ka, h], q_ref[j, at]) for _, j, ka, _, h, at in parts(n)]
        grads = [mul(vn_ref[ka, h], do_ref[j, at]) for _, j, ka, _, h, at in parts(n)]
        for c, (_, j, ka, m, h, at) in enumerate(parts(n)):
            p = jnp.where(allowed[c // len(heads)], jnp.exp(scores[c] - lse_ref[j, h : h + 1]), 0.0)
            p_ref[slot, c] = p.astype(BF16)
            ds_ref[slot, c] = (p * (grads[c] - delta_ref[j, h : h + 1])).astype(BF16)

    def gather(n):
        slot = lax.rem(n, 2)
        for c, (_, j, ka, m, h, at) in enumerate(parts(n)):
            dv_ref[ka, m] += mul(do_ref[j, at], p_ref[slot, c], NT)
            dk_ref[ka, m] += mul(q_ref[j, at], ds_ref[slot, c], NT)
            dq_ref[j, m] += mul(k_ref[ka, at], ds_ref[slot, c])

    weigh(0)

    def both(n, _):
        gather(n - 1)
        weigh(n)
        return 0

    steps = (found + BACK_PAIRS - 1) // BACK_PAIRS
    lax.fori_loop(1, steps, both, 0)
    gather(steps - 1)

    def finish_k(i, _):
        cos, sin = angles(meta, k_block(meta, i, n_blk), rows, n_docs)
        for n in range(len(heads)):
            at = slice(n * HEAD, (n + 1) * HEAD)
            jk_ref[i, at] = turned(dk_ref[i, n], cos, -sin).astype(BF16)
            jv_ref[i, at] = dv_ref[i, n].astype(BF16)
        return 0

    def finish_q(j, _):
        cos, sin = angles(meta, q_block(meta, j, n_blk), rows, n_docs)
        for n in range(len(heads)):
            jq_ref[j, n * HEAD : (n + 1) * HEAD] = (turned(dq_ref[j, n], cos, -sin) * HEAD**-0.5).astype(BF16)
        return 0

    lax.fori_loop(0, n_k, finish_k, 0)
    lax.fori_loop(0, n_q, finish_q, 0)
    if joins:
        shard_kernel(meta, jq_ref, jk_ref, jv_ref, *joins)


def shard_kernel(meta, jq_ref, jk_ref, jv_ref, normed_ref, go_ref, *refs):
    outs, all_ref = refs[:4], refs[4]
    wide = go_ref.shape[0]
    for third, ref in enumerate((jq_ref, jk_ref, jv_ref)):
        total = mul(ref[0], normed_ref[0])
        for j in range(1, QUADS):
            total = total + mul(ref[j], normed_ref[j])
        all_ref[third * wide : (third + 1) * wide] = total
    all_ref[3 * wide :] = go_ref[...]
    put_pieces(all_ref, meta, outs, 0)


def shard_parts(normed, grad_out):
    wide, width = grad_out.shape
    return [normed, grad_out], [sds((1, wide, width), BF16)] * 4, [pltpu.VMEM((4 * wide, width), F32)]


def shard(meta, grads, *rest):
    operands, outs, scratch = shard_parts(*rest)
    operands = list(grads) + operands
    return call(
        shard_kernel,
        "shard",
        meta,
        (1,),
        operands,
        [once(a.shape) for a in operands],
        outs,
        [once(o.shape) for o in outs],
        0,
        0,
        scratch=scratch,
    )


def join_kernel(meta, jq_ref, jk_ref, jv_ref, x_ref, ngm_ref, w_ref, ng_ref, sums_ref):
    joined = [jnp.concatenate([jq_ref[b], jk_ref[b], jv_ref[b]], axis=0) for b in range(2)]
    parts = [mul(j, w_ref[...], TN) for j in joined]
    gain = bias = 0.0
    for b in range(2):
        ng = ngm_ref[b].astype(F32) + parts[b]
        ng_ref[b] = ng.astype(BF16)
        x = x_ref[b].astype(F32)
        centred = x - jnp.mean(x, axis=1, keepdims=True)
        xhat = centred * lax.rsqrt(jnp.mean(centred * centred, axis=1, keepdims=True) + norm_eps)
        gain = gain + jnp.sum(ng * xhat, axis=0, keepdims=True)
        bias = bias + jnp.sum(ng, axis=0, keepdims=True)

    @pl.when(pl.program_id(0) == 0)
    def _():
        sums_ref[...] = jnp.zeros_like(sums_ref)

    sums_ref[0:1] += gain
    sums_ref[1:2] += bias


def join(meta, grads, x, ngm, w_cut):
    n, rows, width = x.shape
    tiled = list(grads) + [x, ngm]
    return call(
        join_kernel,
        "join",
        meta,
        (n // 2,),
        tiled + [w_cut],
        [rows_at(a.shape, 0, 2) for a in tiled] + [whole(w_cut.shape)],
        [sds((n, rows, width), BF16), sds((16, width), F32)],
        [rows_at(x.shape, 0, 2), whole((16, width))],
        2 * n * rows * width * w_cut.shape[0],
        10 * n * rows * width,
    )


def attend_back(meta, q, do, lse, delta, kn, vn, k, n_blk, n_docs, rest):
    n_q, wide, rows = q.shape
    n_k = k.shape[0]
    n_heads = wide // HEAD
    pairs = 0.56 * n_q * n_k
    grads = [sds((n_q, wide, rows), BF16), sds((n_k, wide, rows), BF16), sds((n_k, wide, rows), BF16)]
    operands = [q, do, lse, delta, kn, vn, k]
    outs, scratch = grads, []
    if rest:
        more, pieces, scratch = shard_parts(*rest)
        operands += more
        outs = pieces + grads

    def body(meta_ref, *refs):
        ins, refs = refs[: len(operands)], refs[len(operands) :]
        given, held = refs[: len(outs)], refs[len(outs) :]
        joins = ins[7:] + given[:-3] + held[: len(scratch)]
        back_kernel(range(n_heads), n_blk, n_docs, n_q, n_k, meta_ref, *ins[:7], *joins, *given[-3:], *held[len(scratch) :])

    return call(
        body,
        "attend_back",
        meta,
        (1,),
        operands,
        [once(a.shape) for a in operands],
        outs,
        [once(o.shape) for o in outs],
        pairs * n_heads * rows * rows * 256 * 2 * 2.5,
        16 * n_q * rows * wide,
        pairs * n_heads * rows * rows,
        scratch=scratch
        + [
            pltpu.VMEM((n_q, n_heads, HEAD, rows), F32),
            pltpu.VMEM((n_k, n_heads, HEAD, rows), F32),
            pltpu.VMEM((n_k, n_heads, HEAD, rows), F32),
            pltpu.VMEM((2, BACK_PAIRS * n_heads, rows, rows), BF16),
            pltpu.VMEM((2, BACK_PAIRS * n_heads, rows, rows), BF16),
            pltpu.SMEM((n_q * n_k + BACK_PAIRS,), jnp.int32),
            pltpu.SMEM((n_q * n_k + BACK_PAIRS,), jnp.int32),
        ],
    )


def swap(x, axis, size, mask):
    return lax.ppermute(x, axis, [(i, i ^ mask) for i in range(size)])


def add(a, b):
    return a.astype(F32) + b.astype(F32)


class Order:
    def __init__(self, sizes):
        self.sizes = sizes
        self.token = []

    def hold(self, arrays):
        arrays = list(arrays)
        held = lax.optimization_barrier(tuple(arrays) + tuple(self.token))
        return list(held[: len(arrays)])

    def done(self, results):
        self.token = jax.tree.leaves(results)[:1]
        return results

    def send(self, exchanges):
        if not isinstance(exchanges[0], tuple):
            return exchanges
        sent = self.hold([array for array, _, _ in exchanges])
        self.token = sent
        return [swap(a, axis, self.sizes[axis], mask) for a, (_, axis, mask) in zip(sent, exchanges)]

    def start(self, generator):
        return Steps(generator, self)

    def advance(self, *chains):
        for chain in chains:
            chain.advance()


class Steps:
    def __init__(self, generator, order):
        self.generator, self.order = generator, order
        self.held = order.send(next(generator))

    def advance(self):
        self.held = self.order.send(self.generator.send(self.order.hold(self.held)))

    def end(self):
        try:
            while True:
                self.advance()
        except StopIteration:
            return self.held


def reduce_pieces(parts):
    got = yield [(part, "dp", k + 1) for k, part in enumerate(parts[1:])]
    return [(add(parts[0], got[0]) + add(got[1], got[2])).astype(BF16)]


def reduce_halves(parts, n_blk):
    send_a, keep_a, send_b, keep_b = parts
    got_a, got_b = yield [(send_a, "dp", 1), (send_b, "dp", 2)]
    sum_a, sum_b = add(keep_a, got_a).astype(BF16), add(keep_b, got_b).astype(BF16)
    got_a, got_b = yield [(sum_a[1], "dp", 2), (sum_b[1], "dp", 1)]
    own = jnp.stack([add(sum_a[0], got_a), add(sum_b[0], got_b)]).astype(BF16)
    (got,) = yield [(own, "blk", n_blk // 2)]
    yield [add(own, got).astype(BF16)]


def sum_halves(own, sums, n_blk):
    a, b = own.reshape(2, -1, own.shape[1])
    own = jnp.stack([jnp.concatenate([sums, a]), jnp.concatenate([sums, b])])
    (got,) = yield [(own, "blk", n_blk // 2)]
    yield from spread_pieces(add(own, got).astype(BF16))


def spread_pieces(total):
    (near,) = yield [(total, "blk", 2)]
    pair_a, pair_b = jnp.stack([total[0], near[0]]), jnp.stack([total[1], near[1]])
    got_a, got_b = yield [(pair_a, "dp", 1), (pair_b, "dp", 2)]
    two = [jnp.stack([pair_a, got_a]), jnp.stack([pair_b, got_b])]
    *far, twin_a, twin_b = yield [(two[0], "dp", 2), (two[1], "dp", 1)] + [(o, "blk", 1) for o in two]
    far_twins = yield [(o, "blk", 1) for o in far]
    yield two + far + [twin_a, twin_b] + far_twins


def placed(k, outer, meta, rows):
    b, far = k % 2, (k // 2) % 2
    cx = jnp.bitwise_xor(meta[X_POS], far if b else outer)
    cy = jnp.bitwise_xor(meta[Y_POS], outer if b else far)
    return ((cx * 2 + cy) * 2 + b) * rows


def fill_kernel(meta, *refs):
    srcs, (up_ref, down_ref) = refs[:8], refs[8:]
    rows = srcs[0].shape[3]
    for core in range(2):

        @pl.when(pl.program_id(0) // 2 == core)
        def _():
            for k in range(4):
                for outer in range(2):
                    at = pl.ds(pl.multiple_of(placed(k, outer, meta, rows), 16), rows)
                    up_ref[at, :] = srcs[k + 4 * core][outer, 0, 0].astype(F32)
                    down_ref[at, :] = srcs[k + 4 * core][outer, 0, 1].astype(F32)


def fill(meta, arrays, shapes):
    _, _, _, rows, width = arrays[0].shape

    def shard(i, s):
        return jnp.bitwise_xor(s[QUARTER], lax.rem(i, 2) * 2 + i // 2)

    def source(k):
        return pl.BlockSpec((2, 1, 2, rows, width), lambda i, s: (0, jnp.clip(i - 2 * (k // 4), 0, 1), 0, 0, 0))

    block = (8 * rows, width)
    return call(
        fill_kernel,
        "fill",
        meta,
        (TENSOR,),
        list(arrays),
        [source(k) for k in range(8)],
        [sds(shape, F32) for shape in shapes],
        [pl.BlockSpec(block, lambda i, s: (0, shard(i, s))), pl.BlockSpec(block, lambda i, s: (shard(i, s), 0))],
        0,
        12 * 8 * 4 * rows * width,
    )


def tail_kernel(wide, meta, *refs):
    srcs, (gq_ref, go_ref, gain_ref, bias_ref, hold_ref, part_ref) = refs[:8], refs[8:]
    rows = srcs[0].shape[2] - 16
    i = pl.program_id(0)

    @pl.when(i == 0)
    def _():
        for k, src in enumerate(srcs):
            for outer in range(2):
                row = placed(k % 4, outer, meta, rows)
                for rt1 in range(2):
                    shard = jnp.bitwise_xor(meta[QUARTER], rt1 * 2 + k // 4)
                    at = pl.multiple_of(shard * 4 * wide + row, 16)
                    hold_ref[pl.ds(at, rows), :] = src[outer, rt1, 16:].astype(F32)
                    if k % 2 == 0:
                        part_ref[shard * 4 + row // (2 * rows)] = src[outer, rt1, 0:16].astype(F32)
        total = part_ref[0]
        for n in range(1, 4 * TENSOR):
            total = total + part_ref[n]
        gain_ref[...] = total[0]
        bias_ref[...] = total[1]

    def block(part):
        return jnp.concatenate([hold_ref[(4 * s + part) * wide : (4 * s + part + 1) * wide, :] for s in range(TENSOR)], axis=0)

    for third in range(3):

        @pl.when(i == third)
        def _():
            gq_ref[...] = block(third).T

    @pl.when(i == 3)
    def _():
        go_ref[...] = block(3)


def tail(meta, arrays, width, wide):
    outs = [sds((width, 3 * TENSOR * wide), F32), sds((TENSOR * wide, width), F32), sds((width,), F32), sds((width,), F32)]
    return call(
        partial(tail_kernel, wide),
        "tail",
        meta,
        (4,),
        list(arrays),
        [once(a.shape) for a in arrays],
        outs,
        [pl.BlockSpec((width, TENSOR * wide), lambda i, s: (0, jnp.minimum(i, 2)))] + [whole(o.shape) for o in outs[1:]],
        0,
        6 * 4 * width * width,
        scratch=[pltpu.VMEM((TENSOR * 4 * wide, width), F32), pltpu.VMEM((4 * TENSOR, 16, width), F32)],
    )


def natural(parts):
    own, to_x, to_y, across = parts
    return jnp.concatenate([own, to_y, to_x, across], axis=1)


def natural_halves(parts):
    send_a, keep_a, send_b, keep_b = parts
    a = jnp.stack([keep_a, send_a])
    b = jnp.stack([keep_b, send_b], axis=1)
    both = jnp.moveaxis(jnp.stack([a, b], axis=2), 3, 0)
    return both.reshape(both.shape[0], -1, both.shape[-1])


def xor_gather(x, n_blk, masks):
    for mask in reversed(masks):
        x = jnp.concatenate([x, swap(x, "blk", n_blk, mask)])
    return x


def scatter_blocks(arrays, n_blk):
    n = len(arrays)

    def cut(first):
        return [a[first : first + 2] for a in arrays]

    (got,) = yield [(jnp.concatenate(cut(6) + cut(2)), "blk", 1)]
    far = add(jnp.stack(cut(4)), got[: 2 * n].reshape((n, 2) + got.shape[1:])).astype(BF16)
    near = add(jnp.stack(cut(0)), got[2 * n :].reshape((n, 2) + got.shape[1:])).astype(BF16)
    (far_got,) = yield [(far[:, 1], "blk", 2)]
    far_sum = add(far[:, 0], far_got).astype(BF16)
    other, near_got = yield [(far_sum, "blk", n_blk // 2), (near[:, 1], "blk", 2)]
    yield [add(near[:, 0], near_got).astype(BF16), other]


def local(n_dp, n_blk, tokens, cotangent, lengths, norm_gain, norm_bias, w_qkv, w_out, w_up, w_down):
    micro_count, rows, width = tokens.shape
    n_docs = lengths.shape[2]
    n_heads = width // HEAD // TENSOR
    wide = n_heads * HEAD
    inner = w_up.shape[1] // TENSOR
    splits = n_blk // (2 * TENSOR)
    s_masks = [TENSOR << b for b in reversed(range(splits.bit_length() - 1))]
    fast = n_dp == 4 and splits == 1
    me = lax.axis_index("blk")
    dp = lax.axis_index("dp")
    half = me // (n_blk // 2)
    quarter = lax.rem(me, TENSOR)
    x_pos, y_pos = (lax.rem(dp, 2), dp // 2) if fast else (0 * dp, 0 * dp)
    docs = lax.dynamic_index_in_dim(lengths, half, 0, False)[0]
    firsts = jnp.cumsum(docs, dtype=jnp.int32) - docs
    meta = jnp.concatenate([jnp.stack([quarter, x_pos, y_pos, me, half]).astype(jnp.int32), firsts])

    gain = norm_gain.astype(F32).reshape(1, width)
    bias = norm_bias.astype(F32).reshape(1, width)

    def mine(array):
        return lax.dynamic_index_in_dim(array, half, 0, False), lax.dynamic_index_in_dim(array, 1 - half, 0, False)

    def fourfold(own):
        near, twin = yield [(own, "blk", 2), (own, "blk", 1)]
        (far_twin,) = yield [(near, "blk", 1)]
        yield [own, near, twin, far_twin]

    def cross(array):
        (got,) = yield [(array, "blk", n_blk // 2)]
        yield from fourfold(got)

    order = Order({"dp": n_dp, "blk": n_blk})
    x_mine, x_other = mine(tokens)
    c_mine, c_other = mine(cotangent)
    x_far = order.start(cross(x_other))
    x_near = order.start(fourfold(x_mine))
    w_cut = order.done(cut(meta, w_qkv, wide))
    order.advance(x_near, x_far)
    c_far = order.start(cross(c_other))
    order.advance(x_near)
    stage = order.done(project(meta, order.hold(x_near.held), 0, QUADS, gain, bias, w_cut, n_blk, n_docs, None))
    order.advance(x_far)
    c_near = order.start(fourfold(c_mine))
    order.advance(c_far, x_far)
    stage = order.done(project(meta, order.hold(x_far.held), 4, QUADS, gain, bias, w_cut, n_blk, n_docs, stage))
    x_all, normed, q, k, v, kn, vn = stage
    if splits > 1:
        k, v, kn, vn = (xor_gather(a, n_blk, s_masks) for a in (k, v, kn, vn))
    order.advance(c_near)
    order.advance(c_far, c_near, c_far)
    cot, mo, ngm, *mlp_parts = order.done(feed(meta, normed, order.hold(c_near.held + c_far.held), w_up, w_down))
    if fast:
        mlp = order.start(reduce_halves(mlp_parts, n_blk))
    att, lse = order.done(attend(meta, *order.hold([q]), kn, v, n_blk, n_docs))
    if fast:
        order.advance(mlp)
    out_part, do, delta, grad_out_part = order.done(mix(meta, *order.hold([att, cot, mo]), w_out))
    if fast:
        order.advance(mlp)
    rest = (normed, grad_out_part)
    q, do = order.hold([q, do])
    back = order.done(attend_back(meta, q, do, lse, delta, kn, vn, k, n_blk, n_docs, rest if splits == 1 else None))
    rest_parts, grads = list(back[:-3]), list(back[-3:])
    if splits > 1:
        for at, mask in [(at, mask) for at in (1, 2) for mask in s_masks]:
            count = grads[at].shape[0] // 2
            grads[at] = add(grads[at][:count], swap(grads[at][count:], "blk", n_blk, mask)).astype(BF16)
        rest_parts = order.done(shard(meta, grads, *rest))
    chains = {}
    if fast:

        def of_rest():
            (own,) = yield from reduce_pieces(rest_parts)
            yield from sum_halves(own[0], sums.astype(BF16), n_blk)

        order.advance(mlp)
        chains["M"] = order.start(spread_pieces(mlp.held[0]))
        chains["Q"] = order.start(of_rest())
    ng_part, sums = order.done(join(meta, order.hold(grads), x_all, ngm, w_cut))

    def finish():
        def ordered(own, other):
            return jnp.where(half == 0, jnp.stack([own, other]), jnp.stack([other, own])).astype(F32)

        own, other = chains["N"].end()
        output = (tokens.astype(F32) + ordered(own[0], other[0])).astype(BF16)
        normed_grad = ordered(own[1], other[1])
        x_rows = tokens.astype(F32)
        centred = x_rows - jnp.mean(x_rows, axis=2, keepdims=True)
        inverse = lax.rsqrt(jnp.mean(centred * centred, axis=2, keepdims=True) + norm_eps)
        scaled = centred * inverse
        scaled_grad = normed_grad * norm_gain.astype(F32)
        input_grad = cotangent.astype(F32) + inverse * (
            scaled_grad
            - jnp.mean(scaled_grad, axis=2, keepdims=True)
            - scaled * jnp.mean(scaled_grad * scaled, axis=2, keepdims=True)
        )
        return output, input_grad

    if fast:
        for name in TAIL:
            if name == "m":
                grad_up, grad_down = order.done(fill(meta, order.hold(chains["M"].end()), [w_up.shape, w_down.shape]))
            elif name == "n":
                output, input_grad = order.done(finish())
            elif name in chains:
                order.advance(chains[name])
            else:
                chains[name] = order.start(scatter_blocks([out_part, ng_part], n_blk))
        grad_qkv, grad_out, *norm_sums = tail(meta, chains["Q"].end(), width, wide)
    else:
        chains["N"] = order.start(scatter_blocks([out_part, ng_part], n_blk))
        output, input_grad = finish()
        up, down = natural_halves(mlp_parts)
        (rest,) = natural(rest_parts)
        turn = rest[: 3 * wide].T.reshape(width, 3, wide)
        zeros = partial(jnp.zeros, dtype=BF16)
        up = lax.dynamic_update_slice_in_dim(zeros(w_up.shape), up, quarter * inner, 1)
        down = lax.dynamic_update_slice_in_dim(zeros(w_down.shape), down, quarter * inner, 0)
        turn = lax.dynamic_update_slice_in_dim(zeros((width, 3, TENSOR * wide)), turn, quarter * wide, 2)
        out = lax.dynamic_update_slice_in_dim(zeros(w_out.shape), rest[3 * wide :], quarter * wide, 0)
        summed = lax.psum((up, down, turn, out), ("dp", "blk"))
        grad_up, grad_down, turn, grad_out = (g.astype(F32) for g in summed)
        grad_qkv = turn.reshape(w_qkv.shape)
        norm_sums = lax.psum(sums, ("dp", "blk"))
    return (output, input_grad, norm_sums[0], norm_sums[1], grad_qkv, grad_out, grad_up, grad_down)


def solution(mesh):
    tokens = P(None, ("dp", "blk"), None)
    return jax.shard_map(
        partial(local, mesh.shape["dp"], mesh.shape["blk"]),
        mesh=mesh,
        in_specs=(tokens, tokens, P(None, "dp", None)) + (P(),) * 6,
        out_specs=(tokens, tokens) + (P(),) * 6,
        check_vma=False,
    )
```

```python
from functools import partial

import jax
import jax.numpy as jnp
from jax import lax
from jax.experimental import pallas as pl
from jax.experimental.pallas import tpu as pltpu
from jax.sharding import PartitionSpec as P

HEAD = 64
ROT = 16
TENSOR = 4
QUADS = 8
norm_eps = 1e-05
masked_score = -1e30
F32 = jnp.float32
BF16 = jnp.bfloat16
VMEM_LIMIT = 56 * 1024 * 1024
COST = 0.02
ATTEND_PAIRS = 9
BACK_PAIRS = 3
TAIL = "QMNNMQNQMMmQNQnQ"

NN = (((1,), (0,)), ((), ()))
NT = (((1,), (1,)), ((), ()))
TN = (((0,), (0,)), ((), ()))

QUARTER, X_POS, Y_POS, PLACE, HALF, DOCS = range(6)


def mul(a, b, dims=NN):
    return lax.dot_general(a, b, dims, preferred_element_type=F32)


def sds(shape, dtype):
    return jax.ShapeDtypeStruct(tuple(shape), dtype)


def whole(shape):
    return pl.BlockSpec(tuple(shape), lambda *_: (0,) * len(shape))


def once(shape):
    return pl.BlockSpec(tuple(shape), lambda *_: (0,) * len(shape), pipeline_mode=pl.Buffered(1))


def rows_at(shape, base=0, count=1):
    zeros = (0,) * (len(shape) - 1)
    return pl.BlockSpec((count,) + tuple(shape[1:]), lambda i, s: (i + base,) + zeros)


def call(body, name, meta, grid, operands, in_specs, out_shapes, out_specs, flops, moved, special=0, scratch=(), aliases=None, after=()):
    after = list(after)
    n_in = len(operands)

    def kernel(meta_ref, *refs):
        body(meta_ref, *refs[:n_in], *refs[n_in + len(after) :])

    return pl.pallas_call(
        kernel,
        out_shape=out_shapes,
        grid_spec=pltpu.PrefetchScalarGridSpec(
            num_scalar_prefetch=1,
            grid=grid,
            in_specs=list(in_specs) + [pl.BlockSpec(memory_space=pl.ANY)] * len(after),
            out_specs=out_specs,
            scratch_shapes=list(scratch),
        ),
        input_output_aliases=aliases or {},
        compiler_params=pltpu.CompilerParams(
            dimension_semantics=("arbitrary",) * len(grid), vmem_limit_bytes=VMEM_LIMIT
        ),
        cost_estimate=pl.CostEstimate(flops=int(flops * COST), bytes_accessed=int(moved * COST), transcendentals=int(special * COST)),
        name=name,
    )(meta, *operands, *after)


def place_mask(j, n_blk):
    return (j // 4) * (n_blk // 2) + lax.rem(j, 2) * 2 + lax.rem(j // 2, 2)


def q_block(meta, j, n_blk):
    return jnp.bitwise_xor(meta[PLACE], place_mask(j, n_blk))


def k_block(meta, i, n_blk):
    return jnp.bitwise_xor(q_block(meta, lax.rem(i, QUADS), n_blk), (i // QUADS) * TENSOR)


def k_slot(meta, block, n_blk):
    r = jnp.bitwise_xor(meta[PLACE], block)
    low = lax.rem(r, TENSOR)
    split = lax.rem(r, n_blk // 2) // TENSOR
    return split * QUADS + (r // (n_blk // 2)) * 4 + lax.rem(low, 2) * 2 + low // 2


def doc_start(meta, index, n_docs):
    start = jnp.zeros_like(index)
    for d in range(n_docs):
        first = meta[DOCS + d]
        start = jnp.where(index >= first, first, start)
    return start


def token_index(block, rows):
    return block * rows + lax.broadcasted_iota(jnp.int32, (1, rows), 1)


def angles(meta, block, rows, n_docs):
    index = token_index(block, rows)
    position = (index - doc_start(meta, index, n_docs)).astype(F32)
    order = lax.broadcasted_iota(jnp.int32, (ROT // 2, 1), 0)
    frequency = jnp.ones((ROT // 2, 1), F32)
    for i in range(1, ROT // 2):
        frequency = jnp.where(order == i, 10000.0 ** (-2.0 * i / ROT), frequency)
    phases = position * frequency
    return jnp.cos(phases), jnp.sin(phases)


def turned(head, cos, sin):
    a, b = head[: ROT // 2], head[ROT // 2 : ROT]
    return jnp.concatenate([a * cos - b * sin, b * cos + a * sin, head[ROT:]], axis=0)


def cut_kernel(wide, meta, *refs):
    srcs, out_ref, hold_ref = refs[:3], refs[3], refs[4]
    first = pl.multiple_of(lax.rem(meta[QUARTER], 2) * wide, 16)
    for third in range(3):
        hold_ref[...] = srcs[third][...].astype(F32).T
        out_ref[third * wide : (third + 1) * wide, :] = hold_ref[pl.ds(first, wide), :].astype(BF16)


def cut(meta, w_qkv, wide):
    width = w_qkv.shape[0]
    per = w_qkv.shape[1] // 3 // (2 * wide)

    def spec(third):
        return pl.BlockSpec((width, 2 * wide), lambda i, s: (0, third * per + s[QUARTER] // 2))

    return call(
        partial(cut_kernel, wide),
        "cut",
        meta,
        (1,),
        [w_qkv] * 3,
        [spec(third) for third in range(3)],
        sds((3 * wide, width), BF16),
        whole((3 * wide, width)),
        0,
        18 * wide * width,
        scratch=[pltpu.VMEM((2 * wide, width), F32)],
    )


def pick_kernel(meta, src_ref, out_ref):
    out_ref[...] = src_ref[0]


def pick(meta, array, other, after=()):
    _, rows, width = array.shape
    return call(
        pick_kernel,
        "pick",
        meta,
        (1,),
        [array],
        [pl.BlockSpec((1, rows, width), lambda i, s: ((1 - s[HALF]) if other else s[HALF], 0, 0))],
        sds((rows, width), array.dtype),
        whole((rows, width)),
        0,
        4 * rows * width,
        after=after,
    )


def project_kernel(n_heads, n_blk, n_docs, base, meta, *refs):
    pieces, (gain_ref, bias_ref, w_ref) = refs[:4], refs[4:7]
    x_ref, normed_ref, q_ref, k_ref, v_ref, kn_ref, vn_ref = refs[-7:]
    i = pl.program_id(0)
    rows = x_ref.shape[1]
    wide = n_heads * HEAD
    for k in range(4):

        @pl.when(i == k // 2)
        def _():
            x_ref[k % 2] = pieces[k][...]

    for b in range(2):
        x = x_ref[b].astype(F32)
        mean = jnp.mean(x, axis=1, keepdims=True)
        centred = x - mean
        inverse = lax.rsqrt(jnp.mean(centred * centred, axis=1, keepdims=True) + norm_eps)
        normed_ref[b] = (centred * inverse * gain_ref[...] + bias_ref[...]).astype(BF16)
    flats = [mul(w_ref[...], normed_ref[b], NT) for b in range(2)]
    for b in range(2):
        flat = flats[b]
        cos, sin = angles(meta, q_block(meta, 2 * i + b + base, n_blk), rows, n_docs)
        for h in range(n_heads):
            at = slice(h * HEAD, (h + 1) * HEAD)
            q_ref[b, at] = (turned(flat[at], cos, sin) * HEAD**-0.5).astype(BF16)
            key = turned(flat[wide + h * HEAD : wide + (h + 1) * HEAD], cos, sin)
            k_ref[b, at] = key.astype(BF16)
            kn_ref[b, h] = key.T.astype(BF16)
            value = flat[2 * wide + h * HEAD : 2 * wide + (h + 1) * HEAD]
            v_ref[b, at] = value.astype(BF16)
            vn_ref[b, h] = value.T.astype(BF16)


def project(meta, pieces, base, total, gain, bias, w_cut, n_blk, n_docs, earlier, after=()):
    rows, width = pieces[0].shape
    wide = w_cut.shape[0] // 3
    n_heads = wide // HEAD
    outs = [
        sds((total, rows, width), BF16),
        sds((total, rows, width), BF16),
        sds((total, wide, rows), BF16),
        sds((total, wide, rows), BF16),
        sds((total, wide, rows), BF16),
        sds((total, n_heads, rows, HEAD), BF16),
        sds((total, n_heads, rows, HEAD), BF16),
    ]
    operands = list(pieces) + [gain, bias, w_cut]
    specs = [whole(o.shape) for o in operands]
    aliases = {}
    if earlier is not None:
        aliases = {1 + len(operands) + k: k for k in range(len(outs))}
        operands += list(earlier)
        specs += [pl.BlockSpec(memory_space=pl.ANY)] * len(outs)
    return call(
        partial(project_kernel, n_heads, n_blk, n_docs, base),
        "project",
        meta,
        (2,),
        operands,
        specs,
        outs,
        [rows_at(o.shape, base // 2, 2) for o in outs],
        8 * rows * width * 3 * wide,
        4 * rows * width * 10,
        aliases=aliases,
        after=after,
    )


def list_pairs(meta, base, count, rows, n_blk, n_docs, q_list, k_list):
    def of_block(j, found):
        block = q_block(meta, base + j, n_blk)
        first = doc_start(meta, block * rows, n_docs) // rows

        def put(kb, at):
            q_list[at] = j
            k_list[at] = kb
            return at + 1

        return lax.fori_loop(first, block + 1, put, found)

    return lax.fori_loop(0, count, of_block, jnp.int32(0))


def seen(meta, kb, block, rows, n_docs):
    index = token_index(block, rows)
    k_index = kb * rows + lax.broadcasted_iota(jnp.int32, (rows, rows), 0)
    return (k_index >= doc_start(meta, index, n_docs)) & (k_index <= index)


def attend_kernel(n_heads, n_blk, n_docs, meta, q_ref, kn_ref, v_ref, att_ref, lse_ref, s_ref, acc_ref, top_ref, sum_ref, q_list, k_list):
    count, _, rows = q_ref.shape
    heads = range(n_heads)
    base = pl.program_id(0) * count
    found = list_pairs(meta, base, count, rows, n_blk, n_docs, q_list, k_list)
    for extra in range(ATTEND_PAIRS - 1):
        q_list[found + extra] = count
        k_list[found + extra] = 0
    steps = (found + ATTEND_PAIRS - 1) // ATTEND_PAIRS
    top_ref[...] = jnp.full_like(top_ref, masked_score)
    sum_ref[...] = jnp.zeros_like(sum_ref)
    acc_ref[...] = jnp.zeros_like(acc_ref)

    def fold(tile, how):
        return how(tile.reshape(rows // 8, 8, rows), axis=0)

    def score(n, _):
        for at in [ATTEND_PAIRS * n + e for e in range(ATTEND_PAIRS)]:
            j, kb = q_list[at], k_list[at]
            jq = jnp.minimum(j, count - 1)
            ka = k_slot(meta, kb, n_blk)
            allowed = seen(meta, kb, q_block(meta, base + jq, n_blk), rows, n_docs)
            scores = [mul(kn_ref[ka, h], q_ref[jq, h * HEAD : (h + 1) * HEAD]) for h in heads]
            for h in heads:
                s = jnp.where(allowed, scores[h], masked_score)
                s_ref[at, h] = s
                top_ref[j, h] = jnp.maximum(top_ref[j, h], fold(s, jnp.max))
        return 0

    lax.fori_loop(0, steps, score, 0)

    def settle(j, _):
        for h in heads:
            top_ref[j, h, 0:1] = jnp.max(top_ref[j, h], axis=0, keepdims=True)
        return 0

    lax.fori_loop(0, count + 1, settle, 0)

    def weigh(n, _):
        many = [ATTEND_PAIRS * n + e for e in range(ATTEND_PAIRS)]
        weights = []
        for at in many:
            j = q_list[at]
            for h in heads:
                p = jnp.exp(s_ref[at, h] - top_ref[j, h, 0:1])
                sum_ref[j, h] += fold(p, jnp.sum)
                weights.append(p.astype(BF16))
        for m, at in enumerate(many):
            j, ka = q_list[at], k_slot(meta, k_list[at], n_blk)
            for h in heads:
                acc_ref[j, h] += mul(v_ref[ka, h * HEAD : (h + 1) * HEAD], weights[m * n_heads + h])
        return 0

    lax.fori_loop(0, steps, weigh, 0)
    lse_ref[...] = jnp.zeros_like(lse_ref)

    def finish(j, _):
        for h in heads:
            at = slice(h * HEAD, (h + 1) * HEAD)
            total = jnp.sum(sum_ref[j, h], axis=0, keepdims=True)
            att_ref[j, at] = (acc_ref[j, h] / total).astype(BF16)
            lse_ref[j, h : h + 1] = top_ref[j, h, 0:1] + jnp.log(total)
        return 0

    lax.fori_loop(0, count, finish, 0)


def attend(meta, q, kn, v, n_blk, n_docs, after=()):
    n, wide, rows = q.shape
    n_k, n_heads = kn.shape[:2]
    pairs = 0.56 * n * n_k
    count = n if n_k == n else 1
    most = (n * (n + 1) // 2 if n_k == n else n_k) + ATTEND_PAIRS
    outs = [sds((n, wide, rows), BF16), sds((n, 8, rows), F32)]

    def some(shape):
        zeros = (0,) * (len(shape) - 1)
        return pl.BlockSpec((count,) + tuple(shape[1:]), lambda i, s: (i,) + zeros)

    return call(
        partial(attend_kernel, n_heads, n_blk, n_docs),
        "attend",
        meta,
        (n // count,),
        [q, kn, v],
        [some(q.shape), once(kn.shape), once(v.shape)],
        outs,
        [some(o.shape) for o in outs],
        pairs * n_heads * rows * rows * 256 * 2,
        16 * n * rows * wide,
        pairs * n_heads * rows * rows,
        scratch=[
            pltpu.VMEM((most, n_heads, rows, rows), F32),
            pltpu.VMEM((count + 1, n_heads, HEAD, rows), F32),
            pltpu.VMEM((count + 1, n_heads, 8, rows), F32),
            pltpu.VMEM((count + 1, n_heads, 8, rows), F32),
            pltpu.SMEM((most,), jnp.int32),
            pltpu.SMEM((most,), jnp.int32),
        ],
        after=after,
    )


def gelu_pair(hidden):
    bell = jnp.exp(hidden * hidden * -0.5)
    t = 1.0 / (1.0 + (0.3275911 * 0.5**0.5) * jnp.abs(hidden))
    tail = ((((0.5 * 1.061405429 * t - 0.5 * 1.453152027) * t + 0.5 * 1.421413741) * t - 0.5 * 0.284496736) * t + 0.5 * 0.254829592) * t * bell
    cdf = jnp.where(hidden >= 0, 1.0 - tail, tail)
    return hidden * cdf, cdf + hidden * bell * 0.3989422804014327


def put_pieces(scratch, meta, outs, slot):
    rows = scratch.shape[0] // 4
    for k, out in enumerate(outs):
        cx, cy = jnp.bitwise_xor(meta[X_POS], k % 2), jnp.bitwise_xor(meta[Y_POS], k // 2)
        out[slot] = scratch[pl.ds(pl.multiple_of((cx * 2 + cy) * rows, 16), rows), :].astype(BF16)


def put_halves(scratch, meta, outs, slot):
    x, y = meta[X_POS], meta[Y_POS]
    rows = scratch.shape[0] // 8

    def part(cx, cy, b):
        return scratch[pl.ds(pl.multiple_of(((cx * 2 + cy) * 2 + b) * rows, 16), rows), :].astype(BF16)

    for other in range(2):
        cx, cy = jnp.bitwise_xor(x, other), jnp.bitwise_xor(y, other)
        outs[0][other, slot] = part(1 - x, cy, 0)
        outs[1][other, slot] = part(x, cy, 0)
        outs[2][other, slot] = part(cx, 1 - y, 1)
        outs[3][other, slot] = part(cx, y, 1)


def feed_kernel(meta, *refs):
    pieces, (normed_ref, up_ref, down_ref), (cot_ref, mo_ref, ng_ref), outs, (gup_ref, gdn_ref) = (
        refs[:QUADS],
        refs[QUADS : QUADS + 3],
        refs[QUADS + 3 : QUADS + 6],
        refs[QUADS + 6 : -2],
        refs[-2:],
    )
    i = pl.program_id(0)
    rows, width = pieces[0].shape
    for k in range(QUADS):

        @pl.when(i == k // 2)
        def _():
            cot_ref[k % 2] = pieces[k][...]

    @pl.when(i == 0)
    def _():
        gup_ref[...] = jnp.zeros_like(gup_ref)
        gdn_ref[...] = jnp.zeros_like(gdn_ref)

    normed = normed_ref[...].reshape(2 * rows, width)
    cot = cot_ref[...].reshape(2 * rows, width)
    inner = up_ref.shape[1]
    chunk = inner // 3 if inner % 768 == 0 else inner
    spans = [slice(c, c + chunk) for c in range(0, inner, chunk)]

    def open_up(at):
        return mul(normed, up_ref[:, at]), mul(cot, down_ref[at, :], NT)

    opened = [open_up(at) for at in spans[:2]]
    mo = ng = None
    for c, at in enumerate(spans):
        hidden, active_grad = opened[c]
        active, slope = gelu_pair(hidden)
        active = active.astype(BF16)
        hidden_grad = (active_grad * slope).astype(BF16)
        if c + 2 < len(spans):
            opened.append(open_up(spans[c + 2]))
        part, back = mul(active, down_ref[at, :]), mul(hidden_grad, up_ref[:, at], NT)
        mo, ng = (part, back) if c == 0 else (mo + part, ng + back)
        gdn_ref[at, :] += mul(active, cot, TN)
        gup_ref[:, at] += mul(normed, hidden_grad, TN)
    mo_ref[...] = mo.astype(BF16).reshape(2, rows, width)
    ng_ref[...] = ng.astype(BF16).reshape(2, rows, width)

    @pl.when(i == QUADS // 2 - 1)
    def _():
        put_halves(gup_ref, meta, outs, 0)
        put_halves(gdn_ref, meta, outs, 1)


def feed(meta, normed, pieces, w_up, w_down, after=()):
    rows, width = pieces[0].shape
    inner = w_up.shape[1] // TENSOR
    two = rows_at(normed.shape, 0, 2)
    piece = sds((2, 2, inner // 8, width), BF16)
    return call(
        feed_kernel,
        "feed",
        meta,
        (QUADS // 2,),
        list(pieces) + [normed, w_up, w_down],
        [whole(p.shape) for p in pieces]
        + [
            two,
            pl.BlockSpec((width, inner), lambda i, s: (0, s[QUARTER])),
            pl.BlockSpec((inner, width), lambda i, s: (s[QUARTER], 0)),
        ],
        [sds(normed.shape, BF16)] * 3 + [piece] * 4,
        [two] * 3 + [whole(piece.shape)] * 4,
        12 * QUADS * rows * width * inner,
        8 * QUADS * rows * width + 8 * width * inner,
        scratch=[pltpu.VMEM((width, inner), F32), pltpu.VMEM((inner, width), F32)],
        after=after,
    )


def mix_kernel(n_heads, meta, att_ref, cot_ref, mo_ref, w_ref, out_ref, do_ref, delta_ref, go_ref):
    i = pl.program_id(0)
    w = w_ref[...]
    both = range(2)
    grads = [mul(w, cot_ref[b], NT).astype(BF16) for b in both]
    outs = [mul(att_ref[b], w, TN) for b in both]
    go = mul(att_ref[0], cot_ref[0]) + mul(att_ref[1], cot_ref[1])
    delta_ref[...] = jnp.zeros_like(delta_ref)
    for b in both:
        out_ref[b] = (mo_ref[b].astype(F32) + outs[b]).astype(BF16)
        do_ref[b] = grads[b]
        product = grads[b].astype(F32) * att_ref[b].astype(F32)
        for h in range(n_heads):
            delta_ref[b, h : h + 1] = jnp.sum(product[h * HEAD : (h + 1) * HEAD], axis=0, keepdims=True)

    @pl.when(i == 0)
    def _():
        go_ref[...] = go

    @pl.when(i > 0)
    def _():
        go_ref[...] += go


def mix(meta, att, cot, mo, w_out, after=()):
    n, rows, width = cot.shape
    wide = att.shape[1]
    outs = [
        sds((n, rows, width), BF16),
        sds((n, wide, rows), BF16),
        sds((n, 8, rows), F32),
        sds((wide, width), F32),
    ]
    return call(
        partial(mix_kernel, wide // HEAD),
        "mix",
        meta,
        (n // 2,),
        [att, cot, mo, w_out],
        [rows_at(a.shape, 0, 2) for a in (att, cot, mo)]
        + [pl.BlockSpec((wide, width), lambda i, s: (s[QUARTER], 0))],
        outs,
        [rows_at(o.shape, 0, 2) for o in outs[:3]] + [whole((wide, width))],
        6 * n * rows * width * wide,
        10 * n * rows * width,
        after=after,
    )


def back_kernel(heads, n_blk, n_docs, n_q, n_k, meta, q_ref, do_ref, lse_ref, delta_ref, kn_ref, vn_ref, k_ref, *refs):
    rest, (dq_ref, dk_ref, dv_ref, p_ref, ds_ref, q_list, k_list) = refs[:-7], refs[-7:]
    if len(rest) > 3:
        joins, (jq_ref, jk_ref, jv_ref) = rest[:-3], rest[-3:]
    else:
        joins, (jq_ref, jk_ref, jv_ref) = (), rest
    rows = k_ref.shape[2]
    spots = [slice(h * HEAD, (h + 1) * HEAD) for h in heads]
    dq_ref[...] = jnp.zeros_like(dq_ref)
    dk_ref[...] = jnp.zeros_like(dk_ref)
    dv_ref[...] = jnp.zeros_like(dv_ref)
    found = list_pairs(meta, 0, n_q, rows, n_blk, n_docs, q_list, k_list)

    for extra in range(BACK_PAIRS - 1):
        q_list[found + extra] = n_q - 1
        k_list[found + extra] = q_block(meta, n_q - 1, n_blk) + 1

    def step_pairs(n):
        return [BACK_PAIRS * n + e for e in range(BACK_PAIRS)]

    def parts(n):
        for at in step_pairs(n):
            j, ka = q_list[at], k_slot(meta, jnp.minimum(k_list[at], n_k - 1), n_blk)
            for m, h in enumerate(heads):
                yield at, j, ka, m, h, spots[m]

    def weigh(n):
        slot = lax.rem(n, 2)
        allowed = [seen(meta, k_list[at], q_block(meta, q_list[at], n_blk), rows, n_docs) for at in step_pairs(n)]
        scores = [mul(kn_ref[ka, h], q_ref[j, at]) for _, j, ka, _, h, at in parts(n)]
        grads = [mul(vn_ref[ka, h], do_ref[j, at]) for _, j, ka, _, h, at in parts(n)]
        for c, (_, j, ka, m, h, at) in enumerate(parts(n)):
            p = jnp.where(allowed[c // len(heads)], jnp.exp(scores[c] - lse_ref[j, h : h + 1]), 0.0)
            p_ref[slot, c] = p.astype(BF16)
            ds_ref[slot, c] = (p * (grads[c] - delta_ref[j, h : h + 1])).astype(BF16)

    def gather(n):
        slot = lax.rem(n, 2)
        for c, (_, j, ka, m, h, at) in enumerate(parts(n)):
            dv_ref[ka, m] += mul(do_ref[j, at], p_ref[slot, c], NT)
            dk_ref[ka, m] += mul(q_ref[j, at], ds_ref[slot, c], NT)
            dq_ref[j, m] += mul(k_ref[ka, at], ds_ref[slot, c])

    weigh(0)

    def both(n, _):
        gather(n - 1)
        weigh(n)
        return 0

    steps = (found + BACK_PAIRS - 1) // BACK_PAIRS
    lax.fori_loop(1, steps, both, 0)
    gather(steps - 1)

    def finish_k(i, _):
        cos, sin = angles(meta, k_block(meta, i, n_blk), rows, n_docs)
        for n in range(len(heads)):
            at = slice(n * HEAD, (n + 1) * HEAD)
            jk_ref[i, at] = turned(dk_ref[i, n], cos, -sin).astype(BF16)
            jv_ref[i, at] = dv_ref[i, n].astype(BF16)
        return 0

    def finish_q(j, _):
        cos, sin = angles(meta, q_block(meta, j, n_blk), rows, n_docs)
        for n in range(len(heads)):
            jq_ref[j, n * HEAD : (n + 1) * HEAD] = (turned(dq_ref[j, n], cos, -sin) * HEAD**-0.5).astype(BF16)
        return 0

    lax.fori_loop(0, n_k, finish_k, 0)
    lax.fori_loop(0, n_q, finish_q, 0)
    if joins:
        shard_kernel(meta, jq_ref, jk_ref, jv_ref, *joins)


def shard_kernel(meta, jq_ref, jk_ref, jv_ref, normed_ref, go_ref, *refs):
    outs, all_ref = refs[:4], refs[4]
    wide = go_ref.shape[0]
    for third, ref in enumerate((jq_ref, jk_ref, jv_ref)):
        total = mul(ref[0], normed_ref[0])
        for j in range(1, QUADS):
            total = total + mul(ref[j], normed_ref[j])
        all_ref[third * wide : (third + 1) * wide] = total
    all_ref[3 * wide :] = go_ref[...]
    put_pieces(all_ref, meta, outs, 0)


def shard_parts(normed, grad_out):
    wide, width = grad_out.shape
    return [normed, grad_out], [sds((1, wide, width), BF16)] * 4, [pltpu.VMEM((4 * wide, width), F32)]


def shard(meta, grads, *rest):
    operands, outs, scratch = shard_parts(*rest)
    operands = list(grads) + operands
    return call(
        shard_kernel,
        "shard",
        meta,
        (1,),
        operands,
        [once(a.shape) for a in operands],
        outs,
        [once(o.shape) for o in outs],
        0,
        0,
        scratch=scratch,
    )


def join_kernel(meta, jq_ref, jk_ref, jv_ref, x_ref, ngm_ref, w_ref, ng_ref, sums_ref):
    joined = [jnp.concatenate([jq_ref[b], jk_ref[b], jv_ref[b]], axis=0) for b in range(2)]
    parts = [mul(j, w_ref[...], TN) for j in joined]
    gain = bias = 0.0
    for b in range(2):
        ng = ngm_ref[b].astype(F32) + parts[b]
        ng_ref[b] = ng.astype(BF16)
        x = x_ref[b].astype(F32)
        centred = x - jnp.mean(x, axis=1, keepdims=True)
        xhat = centred * lax.rsqrt(jnp.mean(centred * centred, axis=1, keepdims=True) + norm_eps)
        gain = gain + jnp.sum(ng * xhat, axis=0, keepdims=True)
        bias = bias + jnp.sum(ng, axis=0, keepdims=True)

    @pl.when(pl.program_id(0) == 0)
    def _():
        sums_ref[...] = jnp.zeros_like(sums_ref)

    sums_ref[0:1] += gain
    sums_ref[1:2] += bias


def join(meta, grads, x, ngm, w_cut):
    n, rows, width = x.shape
    tiled = list(grads) + [x, ngm]
    return call(
        join_kernel,
        "join",
        meta,
        (n // 2,),
        tiled + [w_cut],
        [rows_at(a.shape, 0, 2) for a in tiled] + [whole(w_cut.shape)],
        [sds((n, rows, width), BF16), sds((16, width), F32)],
        [rows_at(x.shape, 0, 2), whole((16, width))],
        2 * n * rows * width * w_cut.shape[0],
        10 * n * rows * width,
    )


def attend_back(meta, q, do, lse, delta, kn, vn, k, n_blk, n_docs, rest):
    n_q, wide, rows = q.shape
    n_k = k.shape[0]
    n_heads = wide // HEAD
    pairs = 0.56 * n_q * n_k
    grads = [sds((n_q, wide, rows), BF16), sds((n_k, wide, rows), BF16), sds((n_k, wide, rows), BF16)]
    operands = [q, do, lse, delta, kn, vn, k]
    outs, scratch = grads, []
    if rest:
        more, pieces, scratch = shard_parts(*rest)
        operands += more
        outs = pieces + grads

    def body(meta_ref, *refs):
        ins, refs = refs[: len(operands)], refs[len(operands) :]
        given, held = refs[: len(outs)], refs[len(outs) :]
        joins = ins[7:] + given[:-3] + held[: len(scratch)]
        back_kernel(range(n_heads), n_blk, n_docs, n_q, n_k, meta_ref, *ins[:7], *joins, *given[-3:], *held[len(scratch) :])

    return call(
        body,
        "attend_back",
        meta,
        (1,),
        operands,
        [once(a.shape) for a in operands],
        outs,
        [once(o.shape) for o in outs],
        pairs * n_heads * rows * rows * 256 * 2 * 2.5,
        16 * n_q * rows * wide,
        pairs * n_heads * rows * rows,
        scratch=scratch
        + [
            pltpu.VMEM((n_q, n_heads, HEAD, rows), F32),
            pltpu.VMEM((n_k, n_heads, HEAD, rows), F32),
            pltpu.VMEM((n_k, n_heads, HEAD, rows), F32),
            pltpu.VMEM((2, BACK_PAIRS * n_heads, rows, rows), BF16),
            pltpu.VMEM((2, BACK_PAIRS * n_heads, rows, rows), BF16),
            pltpu.SMEM((n_q * n_k + BACK_PAIRS,), jnp.int32),
            pltpu.SMEM((n_q * n_k + BACK_PAIRS,), jnp.int32),
        ],
    )


def swap(x, axis, size, mask):
    return lax.ppermute(x, axis, [(i, i ^ mask) for i in range(size)])


def add(a, b):
    return a.astype(F32) + b.astype(F32)


class Order:
    def __init__(self, sizes):
        self.sizes = sizes
        self.token = []

    def hold(self, arrays):
        arrays = list(arrays)
        held = lax.optimization_barrier(tuple(arrays) + tuple(self.token))
        return list(held[: len(arrays)])

    def done(self, results):
        self.token = jax.tree.leaves(results)[:1]
        return results

    def send(self, exchanges):
        if not isinstance(exchanges[0], tuple):
            self.token = exchanges[-1:]
            return exchanges
        sent = self.hold([array for array, _, _ in exchanges])
        self.token = sent
        return [swap(a, axis, self.sizes[axis], mask) for a, (_, axis, mask) in zip(sent, exchanges)]

    def start(self, generator):
        return Steps(generator, self)

    def advance(self, *chains):
        for chain in chains:
            chain.advance()


class Steps:
    def __init__(self, generator, order):
        self.generator, self.order = generator, order
        self.held = order.send(next(generator))

    def advance(self):
        self.held = self.order.send(self.generator.send(self.order.hold(self.held)))

    def end(self):
        try:
            while True:
                self.advance()
        except StopIteration:
            return self.held


def reduce_pieces(parts):
    got = yield [(part, "dp", k + 1) for k, part in enumerate(parts[1:])]
    return [(add(parts[0], got[0]) + add(got[1], got[2])).astype(BF16)]


def reduce_halves(parts, n_blk):
    send_a, keep_a, send_b, keep_b = parts
    got_a, got_b = yield [(send_a, "dp", 1), (send_b, "dp", 2)]
    sum_a, sum_b = add(keep_a, got_a).astype(BF16), add(keep_b, got_b).astype(BF16)
    got_a, got_b = yield [(sum_a[1], "dp", 2), (sum_b[1], "dp", 1)]
    own = jnp.stack([add(sum_a[0], got_a), add(sum_b[0], got_b)]).astype(BF16)
    (got,) = yield [(own, "blk", n_blk // 2)]
    yield [add(own, got).astype(BF16)]


def sum_halves(own, sums, n_blk):
    a, b = own.reshape(2, -1, own.shape[1])
    own = jnp.stack([jnp.concatenate([sums, a]), jnp.concatenate([sums, b])])
    (got,) = yield [(own, "blk", n_blk // 2)]
    yield from spread_pieces(add(own, got).astype(BF16))


def spread_pieces(total, twins_last=False):
    (near,) = yield [(total, "blk", 2)]
    pair_a, pair_b = jnp.stack([total[0], near[0]]), jnp.stack([total[1], near[1]])
    got_a, got_b = yield [(pair_a, "dp", 1), (pair_b, "dp", 2)]
    two = [jnp.stack([pair_a, got_a]), jnp.stack([pair_b, got_b])]
    far = yield [(two[0], "dp", 2), (two[1], "dp", 1)] + [(o, "blk", 1) for o in two if not twins_last]
    if twins_last:
        twins = yield [(o, "blk", 1) for o in two + far]
        yield two + far + twins
    else:
        far_twins = yield [(o, "blk", 1) for o in far[:2]]
        yield two + far + far_twins


def placed(k, outer, meta, rows):
    b, far = k % 2, (k // 2) % 2
    cx = jnp.bitwise_xor(meta[X_POS], far if b else outer)
    cy = jnp.bitwise_xor(meta[Y_POS], outer if b else far)
    return ((cx * 2 + cy) * 2 + b) * rows


def fill_kernel(meta, *refs):
    srcs, (up_ref, down_ref) = refs[:8], refs[8:]
    rows = srcs[0].shape[3]
    for core in range(2):

        @pl.when(pl.program_id(0) // 2 == core)
        def _():
            for k in range(4):
                for outer in range(2):
                    at = pl.ds(pl.multiple_of(placed(k, outer, meta, rows), 16), rows)
                    up_ref[at, :] = srcs[k + 4 * core][outer, 0, 0].astype(F32)
                    down_ref[at, :] = srcs[k + 4 * core][outer, 0, 1].astype(F32)


def fill(meta, arrays, shapes):
    _, _, _, rows, width = arrays[0].shape

    def shard(i, s):
        return jnp.bitwise_xor(s[QUARTER], lax.rem(i, 2) * 2 + i // 2)

    def source(k):
        return pl.BlockSpec((2, 1, 2, rows, width), lambda i, s: (0, jnp.clip(i - 2 * (k // 4), 0, 1), 0, 0, 0))

    block = (8 * rows, width)
    return call(
        fill_kernel,
        "fill",
        meta,
        (TENSOR,),
        list(arrays),
        [source(k) for k in range(8)],
        [sds(shape, F32) for shape in shapes],
        [pl.BlockSpec(block, lambda i, s: (0, shard(i, s))), pl.BlockSpec(block, lambda i, s: (shard(i, s), 0))],
        0,
        12 * 8 * 4 * rows * width,
    )


def tail_kernel(wide, meta, *refs):
    srcs, (gq_ref, go_ref, gain_ref, bias_ref, hold_ref, part_ref) = refs[:8], refs[8:]
    rows = srcs[0].shape[2] - 16
    i = pl.program_id(0)

    @pl.when(i == 0)
    def _():
        for k, src in enumerate(srcs):
            for outer in range(2):
                row = placed(k % 4, outer, meta, rows)
                for rt1 in range(2):
                    shard = jnp.bitwise_xor(meta[QUARTER], rt1 * 2 + k // 4)
                    at = pl.multiple_of(shard * 4 * wide + row, 16)
                    hold_ref[pl.ds(at, rows), :] = src[outer, rt1, 16:].astype(F32)
                    if k % 2 == 0:
                        part_ref[shard * 4 + row // (2 * rows)] = src[outer, rt1, 0:16].astype(F32)
        total = part_ref[0]
        for n in range(1, 4 * TENSOR):
            total = total + part_ref[n]
        gain_ref[...] = total[0]
        bias_ref[...] = total[1]

    def block(part):
        return jnp.concatenate([hold_ref[(4 * s + part) * wide : (4 * s + part + 1) * wide, :] for s in range(TENSOR)], axis=0)

    for third in range(3):

        @pl.when(i == third)
        def _():
            gq_ref[...] = block(third).T

    @pl.when(i == 3)
    def _():
        go_ref[...] = block(3)


def tail(meta, arrays, width, wide):
    outs = [sds((width, 3 * TENSOR * wide), F32), sds((TENSOR * wide, width), F32), sds((width,), F32), sds((width,), F32)]
    return call(
        partial(tail_kernel, wide),
        "tail",
        meta,
        (4,),
        list(arrays),
        [once(a.shape) for a in arrays],
        outs,
        [pl.BlockSpec((width, TENSOR * wide), lambda i, s: (0, jnp.minimum(i, 2)))] + [whole(o.shape) for o in outs[1:]],
        0,
        6 * 4 * width * width,
        scratch=[pltpu.VMEM((TENSOR * 4 * wide, width), F32), pltpu.VMEM((4 * TENSOR, 16, width), F32)],
    )


def natural(parts):
    own, to_x, to_y, across = parts
    return jnp.concatenate([own, to_y, to_x, across], axis=1)


def natural_halves(parts):
    send_a, keep_a, send_b, keep_b = parts
    a = jnp.stack([keep_a, send_a])
    b = jnp.stack([keep_b, send_b], axis=1)
    both = jnp.moveaxis(jnp.stack([a, b], axis=2), 3, 0)
    return both.reshape(both.shape[0], -1, both.shape[-1])


def xor_gather(x, n_blk, masks):
    for mask in reversed(masks):
        x = jnp.concatenate([x, swap(x, "blk", n_blk, mask)])
    return x


def scatter_blocks(arrays, n_blk):
    n = len(arrays)

    def cut(first):
        return [a[first : first + 2] for a in arrays]

    (got,) = yield [(jnp.concatenate(cut(6) + cut(2)), "blk", 1)]
    far = add(jnp.stack(cut(4)), got[: 2 * n].reshape((n, 2) + got.shape[1:])).astype(BF16)
    near = add(jnp.stack(cut(0)), got[2 * n :].reshape((n, 2) + got.shape[1:])).astype(BF16)
    (far_got,) = yield [(far[:, 1], "blk", 2)]
    far_sum = add(far[:, 0], far_got).astype(BF16)
    other, near_got = yield [(far_sum, "blk", n_blk // 2), (near[:, 1], "blk", 2)]
    yield [add(near[:, 0], near_got).astype(BF16), other]


def local(n_dp, n_blk, tokens, cotangent, lengths, norm_gain, norm_bias, w_qkv, w_out, w_up, w_down):
    micro_count, rows, width = tokens.shape
    n_docs = lengths.shape[2]
    n_heads = width // HEAD // TENSOR
    wide = n_heads * HEAD
    inner = w_up.shape[1] // TENSOR
    splits = n_blk // (2 * TENSOR)
    s_masks = [TENSOR << b for b in reversed(range(splits.bit_length() - 1))]
    fast = n_dp == 4 and splits == 1
    me = lax.axis_index("blk")
    dp = lax.axis_index("dp")
    half = me // (n_blk // 2)
    quarter = lax.rem(me, TENSOR)
    x_pos, y_pos = (lax.rem(dp, 2), dp // 2) if fast else (0 * dp, 0 * dp)
    docs = lax.dynamic_index_in_dim(lengths, half, 0, False)[0]
    firsts = jnp.cumsum(docs, dtype=jnp.int32) - docs
    meta = jnp.concatenate([jnp.stack([quarter, x_pos, y_pos, me, half]).astype(jnp.int32), firsts])

    gain = norm_gain.astype(F32).reshape(1, width)
    bias = norm_bias.astype(F32).reshape(1, width)

    def mine(array):
        return lax.dynamic_index_in_dim(array, half, 0, False), lax.dynamic_index_in_dim(array, 1 - half, 0, False)

    def fourfold(own):
        near, twin = yield [(own, "blk", 2), (own, "blk", 1)]
        (far_twin,) = yield [(near, "blk", 1)]
        yield [own, near, twin, far_twin]

    def cross(array):
        (got,) = yield [(array, "blk", n_blk // 2)]
        yield from fourfold(got)

    order = Order({"dp": n_dp, "blk": n_blk})
    x_mine, x_other = mine(tokens)
    c_mine, c_other = mine(cotangent)
    x_far = order.start(cross(x_other))
    x_near = order.start(fourfold(x_mine))
    w_cut = order.done(cut(meta, w_qkv, wide))
    order.advance(x_near, x_far)
    c_far = order.start(cross(c_other))
    order.advance(x_near)
    stage = order.done(project(meta, order.hold(x_near.held), 0, QUADS, gain, bias, w_cut, n_blk, n_docs, None))
    order.advance(x_far)
    c_near = order.start(fourfold(c_mine))
    order.advance(c_far, x_far)
    stage = order.done(project(meta, order.hold(x_far.held), 4, QUADS, gain, bias, w_cut, n_blk, n_docs, stage))
    x_all, normed, q, k, v, kn, vn = stage
    if splits > 1:
        k, v, kn, vn = (xor_gather(a, n_blk, s_masks) for a in (k, v, kn, vn))
    order.advance(c_near)
    order.advance(c_far, c_near, c_far)
    cot, mo, ngm, *mlp_parts = order.done(feed(meta, normed, order.hold(c_near.held + c_far.held), w_up, w_down))
    if fast:
        mlp = order.start(reduce_halves(mlp_parts, n_blk))
    att, lse = order.done(attend(meta, *order.hold([q]), kn, v, n_blk, n_docs))
    if fast:
        order.advance(mlp)
    out_part, do, delta, grad_out_part = order.done(mix(meta, *order.hold([att, cot, mo]), w_out))
    if fast:
        order.advance(mlp)
    rest = (normed, grad_out_part)
    q, do = order.hold([q, do])
    back = order.done(attend_back(meta, q, do, lse, delta, kn, vn, k, n_blk, n_docs, rest if splits == 1 else None))
    rest_parts, grads = list(back[:-3]), list(back[-3:])
    if splits > 1:
        for at, mask in [(at, mask) for at in (1, 2) for mask in s_masks]:
            count = grads[at].shape[0] // 2
            grads[at] = add(grads[at][:count], swap(grads[at][count:], "blk", n_blk, mask)).astype(BF16)
        rest_parts = order.done(shard(meta, grads, *rest))
    chains = {}
    if fast:

        def of_rest():
            (own,) = yield from reduce_pieces(rest_parts)
            yield from sum_halves(own[0], sums.astype(BF16), n_blk)

        order.advance(mlp)
        chains["M"] = order.start(spread_pieces(mlp.held[0], True))
        chains["Q"] = order.start(of_rest())
    ng_part, sums = order.done(join(meta, order.hold(grads), x_all, ngm, w_cut))

    def finish():
        def ordered(own, other):
            return jnp.where(half == 0, jnp.stack([own, other]), jnp.stack([other, own])).astype(F32)

        own, other = chains["N"].end()
        output = (tokens.astype(F32) + ordered(own[0], other[0])).astype(BF16)
        normed_grad = ordered(own[1], other[1])
        x_rows = tokens.astype(F32)
        centred = x_rows - jnp.mean(x_rows, axis=2, keepdims=True)
        inverse = lax.rsqrt(jnp.mean(centred * centred, axis=2, keepdims=True) + norm_eps)
        scaled = centred * inverse
        scaled_grad = normed_grad * norm_gain.astype(F32)
        input_grad = cotangent.astype(F32) + inverse * (
            scaled_grad
            - jnp.mean(scaled_grad, axis=2, keepdims=True)
            - scaled * jnp.mean(scaled_grad * scaled, axis=2, keepdims=True)
        )
        return output, input_grad

    if fast:
        for name in TAIL:
            if name == "m":
                grad_up, grad_down = order.done(fill(meta, order.hold(chains["M"].end()), [w_up.shape, w_down.shape]))
            elif name == "n":
                output, input_grad = order.done(finish())
            elif name in chains:
                order.advance(chains[name])
            else:
                chains[name] = order.start(scatter_blocks([out_part, ng_part], n_blk))
        grad_qkv, grad_out, *norm_sums = tail(meta, chains["Q"].end(), width, wide)
    else:
        chains["N"] = order.start(scatter_blocks([out_part, ng_part], n_blk))
        output, input_grad = finish()
        up, down = natural_halves(mlp_parts)
        (rest,) = natural(rest_parts)
        turn = rest[: 3 * wide].T.reshape(width, 3, wide)
        zeros = partial(jnp.zeros, dtype=BF16)
        up = lax.dynamic_update_slice_in_dim(zeros(w_up.shape), up, quarter * inner, 1)
        down = lax.dynamic_update_slice_in_dim(zeros(w_down.shape), down, quarter * inner, 0)
        turn = lax.dynamic_update_slice_in_dim(zeros((width, 3, TENSOR * wide)), turn, quarter * wide, 2)
        out = lax.dynamic_update_slice_in_dim(zeros(w_out.shape), rest[3 * wide :], quarter * wide, 0)
        summed = lax.psum((up, down, turn, out), ("dp", "blk"))
        grad_up, grad_down, turn, grad_out = (g.astype(F32) for g in summed)
        grad_qkv = turn.reshape(w_qkv.shape)
        norm_sums = lax.psum(sums, ("dp", "blk"))
    return (output, input_grad, norm_sums[0], norm_sums[1], grad_qkv, grad_out, grad_up, grad_down)


def solution(mesh):
    tokens = P(None, ("dp", "blk"), None)
    return jax.shard_map(
        partial(local, mesh.shape["dp"], mesh.shape["blk"]),
        mesh=mesh,
        in_specs=(tokens, tokens, P(None, "dp", None)) + (P(),) * 6,
        out_specs=(tokens, tokens) + (P(),) * 6,
        check_vma=False,
    )
```

```python
from functools import partial

import jax
import jax.numpy as jnp
from jax import lax
from jax.experimental import pallas as pl
from jax.experimental.pallas import tpu as pltpu
from jax.sharding import PartitionSpec as P

HEAD = 64
ROT = 16
TENSOR = 4
QUADS = 8
norm_eps = 1e-05
masked_score = -1e30
F32 = jnp.float32
BF16 = jnp.bfloat16
VMEM_LIMIT = 56 * 1024 * 1024
COST = 0.02
ATTEND_PAIRS = 9
BACK_PAIRS = 3
TAIL = "QMNNMQNQMMmQNQnQ"

NN = (((1,), (0,)), ((), ()))
NT = (((1,), (1,)), ((), ()))
TN = (((0,), (0,)), ((), ()))

QUARTER, X_POS, Y_POS, PLACE, HALF, DOCS = range(6)


def mul(a, b, dims=NN):
    return lax.dot_general(a, b, dims, preferred_element_type=F32)


def sds(shape, dtype):
    return jax.ShapeDtypeStruct(tuple(shape), dtype)


def whole(shape):
    return pl.BlockSpec(tuple(shape), lambda *_: (0,) * len(shape))


def once(shape):
    return pl.BlockSpec(tuple(shape), lambda *_: (0,) * len(shape), pipeline_mode=pl.Buffered(1))


def rows_at(shape, base=0, count=1):
    zeros = (0,) * (len(shape) - 1)
    return pl.BlockSpec((count,) + tuple(shape[1:]), lambda i, s: (i + base,) + zeros)


def call(body, name, meta, grid, operands, in_specs, out_shapes, out_specs, flops, moved, special=0, scratch=(), aliases=None, after=()):
    after = list(after)
    n_in = len(operands)

    def kernel(meta_ref, *refs):
        body(meta_ref, *refs[:n_in], *refs[n_in + len(after) :])

    return pl.pallas_call(
        kernel,
        out_shape=out_shapes,
        grid_spec=pltpu.PrefetchScalarGridSpec(
            num_scalar_prefetch=1,
            grid=grid,
            in_specs=list(in_specs) + [pl.BlockSpec(memory_space=pl.ANY)] * len(after),
            out_specs=out_specs,
            scratch_shapes=list(scratch),
        ),
        input_output_aliases=aliases or {},
        compiler_params=pltpu.CompilerParams(
            dimension_semantics=("arbitrary",) * len(grid), vmem_limit_bytes=VMEM_LIMIT
        ),
        cost_estimate=pl.CostEstimate(flops=int(flops * COST), bytes_accessed=int(moved * COST), transcendentals=int(special * COST)),
        name=name,
    )(meta, *operands, *after)


def place_mask(j, n_blk):
    return (j // 4) * (n_blk // 2) + lax.rem(j, 2) * 2 + lax.rem(j // 2, 2)


def q_block(meta, j, n_blk):
    return jnp.bitwise_xor(meta[PLACE], place_mask(j, n_blk))


def k_block(meta, i, n_blk):
    return jnp.bitwise_xor(q_block(meta, lax.rem(i, QUADS), n_blk), (i // QUADS) * TENSOR)


def k_slot(meta, block, n_blk):
    r = jnp.bitwise_xor(meta[PLACE], block)
    low = lax.rem(r, TENSOR)
    split = lax.rem(r, n_blk // 2) // TENSOR
    return split * QUADS + (r // (n_blk // 2)) * 4 + lax.rem(low, 2) * 2 + low // 2


def doc_start(meta, index, n_docs):
    start = jnp.zeros_like(index)
    for d in range(n_docs):
        first = meta[DOCS + d]
        start = jnp.where(index >= first, first, start)
    return start


def token_index(block, rows):
    return block * rows + lax.broadcasted_iota(jnp.int32, (1, rows), 1)


def angles(meta, block, rows, n_docs):
    index = token_index(block, rows)
    position = (index - doc_start(meta, index, n_docs)).astype(F32)
    order = lax.broadcasted_iota(jnp.int32, (ROT // 2, 1), 0)
    frequency = jnp.ones((ROT // 2, 1), F32)
    for i in range(1, ROT // 2):
        frequency = jnp.where(order == i, 10000.0 ** (-2.0 * i / ROT), frequency)
    phases = position * frequency
    return jnp.cos(phases), jnp.sin(phases)


def turned(head, cos, sin):
    a, b = head[: ROT // 2], head[ROT // 2 : ROT]
    return jnp.concatenate([a * cos - b * sin, b * cos + a * sin, head[ROT:]], axis=0)


def cut_kernel(wide, meta, *refs):
    srcs, out_ref, hold_ref = refs[:3], refs[3], refs[4]
    first = pl.multiple_of(lax.rem(meta[QUARTER], 2) * wide, 16)
    for third in range(3):
        hold_ref[...] = srcs[third][...].astype(F32).T
        out_ref[third * wide : (third + 1) * wide, :] = hold_ref[pl.ds(first, wide), :].astype(BF16)


def cut(meta, w_qkv, wide):
    width = w_qkv.shape[0]
    per = w_qkv.shape[1] // 3 // (2 * wide)

    def spec(third):
        return pl.BlockSpec((width, 2 * wide), lambda i, s: (0, third * per + s[QUARTER] // 2))

    return call(
        partial(cut_kernel, wide),
        "cut",
        meta,
        (1,),
        [w_qkv] * 3,
        [spec(third) for third in range(3)],
        sds((3 * wide, width), BF16),
        whole((3 * wide, width)),
        0,
        18 * wide * width,
        scratch=[pltpu.VMEM((2 * wide, width), F32)],
    )


def pick_kernel(meta, src_ref, out_ref):
    out_ref[...] = src_ref[0]


def pick(meta, array, other, after=()):
    _, rows, width = array.shape
    return call(
        pick_kernel,
        "pick",
        meta,
        (1,),
        [array],
        [pl.BlockSpec((1, rows, width), lambda i, s: ((1 - s[HALF]) if other else s[HALF], 0, 0))],
        sds((rows, width), array.dtype),
        whole((rows, width)),
        0,
        4 * rows * width,
        after=after,
    )


def project_kernel(n_heads, n_blk, n_docs, base, meta, *refs):
    pieces, (gain_ref, bias_ref, w_ref) = refs[:4], refs[4:7]
    x_ref, normed_ref, q_ref, k_ref, v_ref, kn_ref, vn_ref = refs[-7:]
    i = pl.program_id(0)
    rows = x_ref.shape[1]
    wide = n_heads * HEAD
    for k in range(4):

        @pl.when(i == k // 2)
        def _():
            x_ref[k % 2] = pieces[k][...]

    for b in range(2):
        x = x_ref[b].astype(F32)
        mean = jnp.mean(x, axis=1, keepdims=True)
        centred = x - mean
        inverse = lax.rsqrt(jnp.mean(centred * centred, axis=1, keepdims=True) + norm_eps)
        normed_ref[b] = (centred * inverse * gain_ref[...] + bias_ref[...]).astype(BF16)
    flats = [mul(w_ref[...], normed_ref[b], NT) for b in range(2)]
    for b in range(2):
        flat = flats[b]
        cos, sin = angles(meta, q_block(meta, 2 * i + b + base, n_blk), rows, n_docs)
        for h in range(n_heads):
            at = slice(h * HEAD, (h + 1) * HEAD)
            q_ref[b, at] = (turned(flat[at], cos, sin) * HEAD**-0.5).astype(BF16)
            key = turned(flat[wide + h * HEAD : wide + (h + 1) * HEAD], cos, sin)
            k_ref[b, at] = key.astype(BF16)
            kn_ref[b, h] = key.T.astype(BF16)
            value = flat[2 * wide + h * HEAD : 2 * wide + (h + 1) * HEAD]
            v_ref[b, at] = value.astype(BF16)
            vn_ref[b, h] = value.T.astype(BF16)


def project(meta, pieces, base, total, gain, bias, w_cut, n_blk, n_docs, earlier, after=()):
    rows, width = pieces[0].shape
    wide = w_cut.shape[0] // 3
    n_heads = wide // HEAD
    outs = [
        sds((total, rows, width), BF16),
        sds((total, rows, width), BF16),
        sds((total, wide, rows), BF16),
        sds((total, wide, rows), BF16),
        sds((total, wide, rows), BF16),
        sds((total, n_heads, rows, HEAD), BF16),
        sds((total, n_heads, rows, HEAD), BF16),
    ]
    operands = list(pieces) + [gain, bias, w_cut]
    specs = [whole(o.shape) for o in operands]
    aliases = {}
    if earlier is not None:
        aliases = {1 + len(operands) + k: k for k in range(len(outs))}
        operands += list(earlier)
        specs += [pl.BlockSpec(memory_space=pl.ANY)] * len(outs)
    return call(
        partial(project_kernel, n_heads, n_blk, n_docs, base),
        "project",
        meta,
        (2,),
        operands,
        specs,
        outs,
        [rows_at(o.shape, base // 2, 2) for o in outs],
        8 * rows * width * 3 * wide,
        4 * rows * width * 10,
        aliases=aliases,
        after=after,
    )


def list_pairs(meta, base, count, rows, n_blk, n_docs, q_list, k_list):
    def of_block(j, found):
        block = q_block(meta, base + j, n_blk)
        first = doc_start(meta, block * rows, n_docs) // rows

        def put(kb, at):
            q_list[at] = j
            k_list[at] = kb
            return at + 1

        return lax.fori_loop(first, block + 1, put, found)

    return lax.fori_loop(0, count, of_block, jnp.int32(0))


def seen(meta, kb, block, rows, n_docs):
    index = token_index(block, rows)
    k_index = kb * rows + lax.broadcasted_iota(jnp.int32, (rows, rows), 0)
    return (k_index >= doc_start(meta, index, n_docs)) & (k_index <= index)


def attend_kernel(n_heads, n_blk, n_docs, meta, q_ref, kn_ref, v_ref, att_ref, lse_ref, s_ref, acc_ref, top_ref, sum_ref, q_list, k_list):
    count, _, rows = q_ref.shape
    heads = range(n_heads)
    base = pl.program_id(0) * count
    found = list_pairs(meta, base, count, rows, n_blk, n_docs, q_list, k_list)
    for extra in range(ATTEND_PAIRS - 1):
        q_list[found + extra] = count
        k_list[found + extra] = 0
    steps = (found + ATTEND_PAIRS - 1) // ATTEND_PAIRS
    top_ref[...] = jnp.full_like(top_ref, masked_score)
    sum_ref[...] = jnp.zeros_like(sum_ref)
    acc_ref[...] = jnp.zeros_like(acc_ref)

    def fold(tile, how):
        return how(tile.reshape(rows // 8, 8, rows), axis=0)

    def score(n, _):
        for at in [ATTEND_PAIRS * n + e for e in range(ATTEND_PAIRS)]:
            j, kb = q_list[at], k_list[at]
            jq = jnp.minimum(j, count - 1)
            ka = k_slot(meta, kb, n_blk)
            allowed = seen(meta, kb, q_block(meta, base + jq, n_blk), rows, n_docs)
            scores = [mul(kn_ref[ka, h], q_ref[jq, h * HEAD : (h + 1) * HEAD]) for h in heads]
            for h in heads:
                s = jnp.where(allowed, scores[h], masked_score)
                s_ref[at, h] = s
                top_ref[j, h] = jnp.maximum(top_ref[j, h], fold(s, jnp.max))
        return 0

    lax.fori_loop(0, steps, score, 0)

    def settle(j, _):
        for h in heads:
            top_ref[j, h, 0:1] = jnp.max(top_ref[j, h], axis=0, keepdims=True)
        return 0

    lax.fori_loop(0, count + 1, settle, 0)

    def weigh(n, _):
        many = [ATTEND_PAIRS * n + e for e in range(ATTEND_PAIRS)]
        weights = []
        for at in many:
            j = q_list[at]
            for h in heads:
                p = jnp.exp(s_ref[at, h] - top_ref[j, h, 0:1])
                sum_ref[j, h] += fold(p, jnp.sum)
                weights.append(p.astype(BF16))
        for m, at in enumerate(many):
            j, ka = q_list[at], k_slot(meta, k_list[at], n_blk)
            for h in heads:
                acc_ref[j, h] += mul(v_ref[ka, h * HEAD : (h + 1) * HEAD], weights[m * n_heads + h])
        return 0

    lax.fori_loop(0, steps, weigh, 0)
    lse_ref[...] = jnp.zeros_like(lse_ref)

    def finish(j, _):
        for h in heads:
            at = slice(h * HEAD, (h + 1) * HEAD)
            total = jnp.sum(sum_ref[j, h], axis=0, keepdims=True)
            att_ref[j, at] = (acc_ref[j, h] / total).astype(BF16)
            lse_ref[j, h : h + 1] = top_ref[j, h, 0:1] + jnp.log(total)
        return 0

    lax.fori_loop(0, count, finish, 0)


def attend(meta, q, kn, v, n_blk, n_docs, after=()):
    n, wide, rows = q.shape
    n_k, n_heads = kn.shape[:2]
    pairs = 0.56 * n * n_k
    count = n if n_k == n else 1
    most = (n * (n + 1) // 2 if n_k == n else n_k) + ATTEND_PAIRS
    outs = [sds((n, wide, rows), BF16), sds((n, 8, rows), F32)]

    def some(shape):
        zeros = (0,) * (len(shape) - 1)
        return pl.BlockSpec((count,) + tuple(shape[1:]), lambda i, s: (i,) + zeros)

    return call(
        partial(attend_kernel, n_heads, n_blk, n_docs),
        "attend",
        meta,
        (n // count,),
        [q, kn, v],
        [some(q.shape), once(kn.shape), once(v.shape)],
        outs,
        [some(o.shape) for o in outs],
        pairs * n_heads * rows * rows * 256 * 2,
        16 * n * rows * wide,
        pairs * n_heads * rows * rows,
        scratch=[
            pltpu.VMEM((most, n_heads, rows, rows), F32),
            pltpu.VMEM((count + 1, n_heads, HEAD, rows), F32),
            pltpu.VMEM((count + 1, n_heads, 8, rows), F32),
            pltpu.VMEM((count + 1, n_heads, 8, rows), F32),
            pltpu.SMEM((most,), jnp.int32),
            pltpu.SMEM((most,), jnp.int32),
        ],
        after=after,
    )


def gelu_pair(hidden):
    bell = jnp.exp(hidden * hidden * -0.5)
    t = 1.0 / (1.0 + (0.3275911 * 0.5**0.5) * jnp.abs(hidden))
    tail = ((((0.5 * 1.061405429 * t - 0.5 * 1.453152027) * t + 0.5 * 1.421413741) * t - 0.5 * 0.284496736) * t + 0.5 * 0.254829592) * t * bell
    cdf = jnp.where(hidden >= 0, 1.0 - tail, tail)
    return hidden * cdf, cdf + hidden * bell * 0.3989422804014327


def put_pieces(scratch, meta, outs, slot):
    rows = scratch.shape[0] // 4
    for k, out in enumerate(outs):
        cx, cy = jnp.bitwise_xor(meta[X_POS], k % 2), jnp.bitwise_xor(meta[Y_POS], k // 2)
        out[slot] = scratch[pl.ds(pl.multiple_of((cx * 2 + cy) * rows, 16), rows), :].astype(BF16)


def put_halves(scratch, meta, outs, slot):
    x, y = meta[X_POS], meta[Y_POS]
    rows = scratch.shape[0] // 8

    def part(cx, cy, b):
        return scratch[pl.ds(pl.multiple_of(((cx * 2 + cy) * 2 + b) * rows, 16), rows), :].astype(BF16)

    for other in range(2):
        cx, cy = jnp.bitwise_xor(x, other), jnp.bitwise_xor(y, other)
        outs[0][other, slot] = part(1 - x, cy, 0)
        outs[1][other, slot] = part(x, cy, 0)
        outs[2][other, slot] = part(cx, 1 - y, 1)
        outs[3][other, slot] = part(cx, y, 1)


def feed_kernel(meta, *refs):
    pieces, (normed_ref, up_ref, down_ref), (cot_ref, mo_ref, ng_ref), outs, (gup_ref, gdn_ref) = (
        refs[:QUADS],
        refs[QUADS : QUADS + 3],
        refs[QUADS + 3 : QUADS + 6],
        refs[QUADS + 6 : -2],
        refs[-2:],
    )
    i = pl.program_id(0)
    rows, width = pieces[0].shape
    for k in range(QUADS):

        @pl.when(i == k // 2)
        def _():
            cot_ref[k % 2] = pieces[k][...]

    @pl.when(i == 0)
    def _():
        gup_ref[...] = jnp.zeros_like(gup_ref)
        gdn_ref[...] = jnp.zeros_like(gdn_ref)

    normed = normed_ref[...].reshape(2 * rows, width)
    cot = cot_ref[...].reshape(2 * rows, width)
    inner = up_ref.shape[1]
    chunk = inner // 3 if inner % 768 == 0 else inner
    spans = [slice(c, c + chunk) for c in range(0, inner, chunk)]

    def open_up(at):
        return mul(normed, up_ref[:, at]), mul(cot, down_ref[at, :], NT)

    opened = [open_up(at) for at in spans[:2]]
    mo = ng = None
    for c, at in enumerate(spans):
        hidden, active_grad = opened[c]
        active, slope = gelu_pair(hidden)
        active = active.astype(BF16)
        hidden_grad = (active_grad * slope).astype(BF16)
        if c + 2 < len(spans):
            opened.append(open_up(spans[c + 2]))
        part, back = mul(active, down_ref[at, :]), mul(hidden_grad, up_ref[:, at], NT)
        mo, ng = (part, back) if c == 0 else (mo + part, ng + back)
        gdn_ref[at, :] += mul(active, cot, TN)
        gup_ref[:, at] += mul(normed, hidden_grad, TN)
    mo_ref[...] = mo.astype(BF16).reshape(2, rows, width)
    ng_ref[...] = ng.astype(BF16).reshape(2, rows, width)

    @pl.when(i == QUADS // 2 - 1)
    def _():
        put_halves(gup_ref, meta, outs, 0)
        put_halves(gdn_ref, meta, outs, 1)


def feed(meta, normed, pieces, w_up, w_down, after=()):
    rows, width = pieces[0].shape
    inner = w_up.shape[1] // TENSOR
    two = rows_at(normed.shape, 0, 2)
    piece = sds((2, 2, inner // 8, width), BF16)
    return call(
        feed_kernel,
        "feed",
        meta,
        (QUADS // 2,),
        list(pieces) + [normed, w_up, w_down],
        [whole(p.shape) for p in pieces]
        + [
            two,
            pl.BlockSpec((width, inner), lambda i, s: (0, s[QUARTER])),
            pl.BlockSpec((inner, width), lambda i, s: (s[QUARTER], 0)),
        ],
        [sds(normed.shape, BF16)] * 3 + [piece] * 4,
        [two] * 3 + [whole(piece.shape)] * 4,
        12 * QUADS * rows * width * inner,
        8 * QUADS * rows * width + 8 * width * inner,
        scratch=[pltpu.VMEM((width, inner), F32), pltpu.VMEM((inner, width), F32)],
        after=after,
    )


def mix_kernel(n_heads, meta, att_ref, cot_ref, mo_ref, w_ref, out_ref, do_ref, delta_ref, go_ref):
    i = pl.program_id(0)
    w = w_ref[...]
    both = range(2)
    grads = [mul(w, cot_ref[b], NT).astype(BF16) for b in both]
    outs = [mul(att_ref[b], w, TN) for b in both]
    go = mul(att_ref[0], cot_ref[0]) + mul(att_ref[1], cot_ref[1])
    delta_ref[...] = jnp.zeros_like(delta_ref)
    for b in both:
        out_ref[b] = (mo_ref[b].astype(F32) + outs[b]).astype(BF16)
        do_ref[b] = grads[b]
        product = grads[b].astype(F32) * att_ref[b].astype(F32)
        for h in range(n_heads):
            delta_ref[b, h : h + 1] = jnp.sum(product[h * HEAD : (h + 1) * HEAD], axis=0, keepdims=True)

    @pl.when(i == 0)
    def _():
        go_ref[...] = go

    @pl.when(i > 0)
    def _():
        go_ref[...] += go


def mix(meta, att, cot, mo, w_out, after=()):
    n, rows, width = cot.shape
    wide = att.shape[1]
    outs = [
        sds((n, rows, width), BF16),
        sds((n, wide, rows), BF16),
        sds((n, 8, rows), F32),
        sds((wide, width), F32),
    ]
    return call(
        partial(mix_kernel, wide // HEAD),
        "mix",
        meta,
        (n // 2,),
        [att, cot, mo, w_out],
        [rows_at(a.shape, 0, 2) for a in (att, cot, mo)]
        + [pl.BlockSpec((wide, width), lambda i, s: (s[QUARTER], 0))],
        outs,
        [rows_at(o.shape, 0, 2) for o in outs[:3]] + [whole((wide, width))],
        6 * n * rows * width * wide,
        10 * n * rows * width,
        after=after,
    )


def back_kernel(heads, n_blk, n_docs, n_q, n_k, meta, q_ref, do_ref, lse_ref, delta_ref, kn_ref, vn_ref, k_ref, *refs):
    rest, (dq_ref, dk_ref, dv_ref, p_ref, ds_ref, q_list, k_list) = refs[:-7], refs[-7:]
    if len(rest) > 3:
        joins, (jq_ref, jk_ref, jv_ref) = rest[:-3], rest[-3:]
    else:
        joins, (jq_ref, jk_ref, jv_ref) = (), rest
    rows = k_ref.shape[2]
    spots = [slice(h * HEAD, (h + 1) * HEAD) for h in heads]
    dq_ref[...] = jnp.zeros_like(dq_ref)
    dk_ref[...] = jnp.zeros_like(dk_ref)
    dv_ref[...] = jnp.zeros_like(dv_ref)
    found = list_pairs(meta, 0, n_q, rows, n_blk, n_docs, q_list, k_list)

    for extra in range(BACK_PAIRS - 1):
        q_list[found + extra] = n_q - 1
        k_list[found + extra] = q_block(meta, n_q - 1, n_blk) + 1

    def step_pairs(n):
        return [BACK_PAIRS * n + e for e in range(BACK_PAIRS)]

    def parts(n):
        for at in step_pairs(n):
            j, ka = q_list[at], k_slot(meta, jnp.minimum(k_list[at], n_k - 1), n_blk)
            for m, h in enumerate(heads):
                yield at, j, ka, m, h, spots[m]

    def weigh(n):
        slot = lax.rem(n, 2)
        allowed = [seen(meta, k_list[at], q_block(meta, q_list[at], n_blk), rows, n_docs) for at in step_pairs(n)]
        scores = [mul(kn_ref[ka, h], q_ref[j, at]) for _, j, ka, _, h, at in parts(n)]
        grads = [mul(vn_ref[ka, h], do_ref[j, at]) for _, j, ka, _, h, at in parts(n)]
        for c, (_, j, ka, m, h, at) in enumerate(parts(n)):
            p = jnp.where(allowed[c // len(heads)], jnp.exp(scores[c] - lse_ref[j, h : h + 1]), 0.0)
            p_ref[slot, c] = p.astype(BF16)
            ds_ref[slot, c] = (p * (grads[c] - delta_ref[j, h : h + 1])).astype(BF16)

    def gather(n):
        slot = lax.rem(n, 2)
        for c, (_, j, ka, m, h, at) in enumerate(parts(n)):
            dv_ref[ka, m] += mul(do_ref[j, at], p_ref[slot, c], NT)
            dk_ref[ka, m] += mul(q_ref[j, at], ds_ref[slot, c], NT)
            dq_ref[j, m] += mul(k_ref[ka, at], ds_ref[slot, c])

    weigh(0)

    def both(n, _):
        gather(n - 1)
        weigh(n)
        return 0

    steps = (found + BACK_PAIRS - 1) // BACK_PAIRS
    lax.fori_loop(1, steps, both, 0)
    gather(steps - 1)

    def finish_k(i, _):
        cos, sin = angles(meta, k_block(meta, i, n_blk), rows, n_docs)
        for n in range(len(heads)):
            at = slice(n * HEAD, (n + 1) * HEAD)
            jk_ref[i, at] = turned(dk_ref[i, n], cos, -sin).astype(BF16)
            jv_ref[i, at] = dv_ref[i, n].astype(BF16)
        return 0

    def finish_q(j, _):
        cos, sin = angles(meta, q_block(meta, j, n_blk), rows, n_docs)
        for n in range(len(heads)):
            jq_ref[j, n * HEAD : (n + 1) * HEAD] = (turned(dq_ref[j, n], cos, -sin) * HEAD**-0.5).astype(BF16)
        return 0

    lax.fori_loop(0, n_k, finish_k, 0)
    lax.fori_loop(0, n_q, finish_q, 0)
    if joins:
        shard_kernel(meta, jq_ref, jk_ref, jv_ref, *joins)


def shard_kernel(meta, jq_ref, jk_ref, jv_ref, normed_ref, go_ref, *refs):
    outs, all_ref = refs[:4], refs[4]
    wide = go_ref.shape[0]
    for third, ref in enumerate((jq_ref, jk_ref, jv_ref)):
        total = mul(ref[0], normed_ref[0])
        for j in range(1, QUADS):
            total = total + mul(ref[j], normed_ref[j])
        all_ref[third * wide : (third + 1) * wide] = total
    all_ref[3 * wide :] = go_ref[...]
    put_pieces(all_ref, meta, outs, 0)


def shard_parts(normed, grad_out):
    wide, width = grad_out.shape
    return [normed, grad_out], [sds((1, wide, width), BF16)] * 4, [pltpu.VMEM((4 * wide, width), F32)]


def shard(meta, grads, *rest):
    operands, outs, scratch = shard_parts(*rest)
    operands = list(grads) + operands
    return call(
        shard_kernel,
        "shard",
        meta,
        (1,),
        operands,
        [once(a.shape) for a in operands],
        outs,
        [once(o.shape) for o in outs],
        0,
        0,
        scratch=scratch,
    )


def join_kernel(meta, jq_ref, jk_ref, jv_ref, x_ref, ngm_ref, w_ref, ng_ref, sums_ref):
    joined = [jnp.concatenate([jq_ref[b], jk_ref[b], jv_ref[b]], axis=0) for b in range(2)]
    parts = [mul(j, w_ref[...], TN) for j in joined]
    gain = bias = 0.0
    for b in range(2):
        ng = ngm_ref[b].astype(F32) + parts[b]
        ng_ref[b] = ng.astype(BF16)
        x = x_ref[b].astype(F32)
        centred = x - jnp.mean(x, axis=1, keepdims=True)
        xhat = centred * lax.rsqrt(jnp.mean(centred * centred, axis=1, keepdims=True) + norm_eps)
        gain = gain + jnp.sum(ng * xhat, axis=0, keepdims=True)
        bias = bias + jnp.sum(ng, axis=0, keepdims=True)

    @pl.when(pl.program_id(0) == 0)
    def _():
        sums_ref[...] = jnp.zeros_like(sums_ref)

    sums_ref[0:1] += gain
    sums_ref[1:2] += bias


def join(meta, grads, x, ngm, w_cut):
    n, rows, width = x.shape
    tiled = list(grads) + [x, ngm]
    return call(
        join_kernel,
        "join",
        meta,
        (n // 2,),
        tiled + [w_cut],
        [rows_at(a.shape, 0, 2) for a in tiled] + [whole(w_cut.shape)],
        [sds((n, rows, width), BF16), sds((16, width), F32)],
        [rows_at(x.shape, 0, 2), whole((16, width))],
        2 * n * rows * width * w_cut.shape[0],
        10 * n * rows * width,
    )


def attend_back(meta, q, do, lse, delta, kn, vn, k, n_blk, n_docs, rest):
    n_q, wide, rows = q.shape
    n_k = k.shape[0]
    n_heads = wide // HEAD
    pairs = 0.56 * n_q * n_k
    grads = [sds((n_q, wide, rows), BF16), sds((n_k, wide, rows), BF16), sds((n_k, wide, rows), BF16)]
    operands = [q, do, lse, delta, kn, vn, k]
    outs, scratch = grads, []
    if rest:
        more, pieces, scratch = shard_parts(*rest)
        operands += more
        outs = pieces + grads

    def body(meta_ref, *refs):
        ins, refs = refs[: len(operands)], refs[len(operands) :]
        given, held = refs[: len(outs)], refs[len(outs) :]
        joins = ins[7:] + given[:-3] + held[: len(scratch)]
        back_kernel(range(n_heads), n_blk, n_docs, n_q, n_k, meta_ref, *ins[:7], *joins, *given[-3:], *held[len(scratch) :])

    return call(
        body,
        "attend_back",
        meta,
        (1,),
        operands,
        [once(a.shape) for a in operands],
        outs,
        [once(o.shape) for o in outs],
        pairs * n_heads * rows * rows * 256 * 2 * 2.5,
        16 * n_q * rows * wide,
        pairs * n_heads * rows * rows,
        scratch=scratch
        + [
            pltpu.VMEM((n_q, n_heads, HEAD, rows), F32),
            pltpu.VMEM((n_k, n_heads, HEAD, rows), F32),
            pltpu.VMEM((n_k, n_heads, HEAD, rows), F32),
            pltpu.VMEM((2, BACK_PAIRS * n_heads, rows, rows), BF16),
            pltpu.VMEM((2, BACK_PAIRS * n_heads, rows, rows), BF16),
            pltpu.SMEM((n_q * n_k + BACK_PAIRS,), jnp.int32),
            pltpu.SMEM((n_q * n_k + BACK_PAIRS,), jnp.int32),
        ],
    )


def swap(x, axis, size, mask):
    return lax.ppermute(x, axis, [(i, i ^ mask) for i in range(size)])


def add(a, b):
    return a.astype(F32) + b.astype(F32)


class Order:
    def __init__(self, sizes):
        self.sizes = sizes
        self.token = []

    def hold(self, arrays):
        arrays = list(arrays)
        held = lax.optimization_barrier(tuple(arrays) + tuple(self.token))
        return list(held[: len(arrays)])

    def done(self, results):
        self.token = jax.tree.leaves(results)[:1]
        return results

    def send(self, exchanges):
        if not isinstance(exchanges[0], tuple):
            self.token = exchanges[-1:]
            return exchanges
        sent = self.hold([array for array, _, _ in exchanges])
        self.token = sent
        return [swap(a, axis, self.sizes[axis], mask) for a, (_, axis, mask) in zip(sent, exchanges)]

    def start(self, generator):
        return Steps(generator, self)

    def advance(self, *chains):
        for chain in chains:
            chain.advance()


class Steps:
    def __init__(self, generator, order):
        self.generator, self.order = generator, order
        self.held = order.send(next(generator))

    def advance(self):
        self.held = self.order.send(self.generator.send(self.order.hold(self.held)))

    def end(self):
        try:
            while True:
                self.advance()
        except StopIteration:
            return self.held


def reduce_pieces(parts):
    got = yield [(part, "dp", k + 1) for k, part in enumerate(parts[1:])]
    return [(add(parts[0], got[0]) + add(got[1], got[2])).astype(BF16)]


def reduce_halves(parts, n_blk):
    send_a, keep_a, send_b, keep_b = parts
    got_a, got_b = yield [(send_a, "dp", 1), (send_b, "dp", 2)]
    sum_a, sum_b = add(keep_a, got_a).astype(BF16), add(keep_b, got_b).astype(BF16)
    got_a, got_b = yield [(sum_a[1], "dp", 2), (sum_b[1], "dp", 1)]
    own = jnp.stack([add(sum_a[0], got_a), add(sum_b[0], got_b)]).astype(BF16)
    (got,) = yield [(own, "blk", n_blk // 2)]
    yield [add(own, got).astype(BF16)]


def sum_halves(own, sums, n_blk):
    a, b = own.reshape(2, -1, own.shape[1])
    own = jnp.stack([jnp.concatenate([sums, a]), jnp.concatenate([sums, b])])
    (got,) = yield [(own, "blk", n_blk // 2)]
    yield from spread_pieces(add(own, got).astype(BF16))


def spread_pieces(total, twins_last=False):
    (near,) = yield [(total, "blk", 2)]
    pair_a, pair_b = jnp.stack([total[0], near[0]]), jnp.stack([total[1], near[1]])
    got_a, got_b = yield [(pair_a, "dp", 1), (pair_b, "dp", 2)]
    two = [jnp.stack([pair_a, got_a]), jnp.stack([pair_b, got_b])]
    far = yield [(two[0], "dp", 2), (two[1], "dp", 1)] + [(o, "blk", 1) for o in two if not twins_last]
    if twins_last:
        twins = yield [(o, "blk", 1) for o in two + far]
        yield two + far + twins
    else:
        far_twins = yield [(o, "blk", 1) for o in far[:2]]
        yield two + far + far_twins


def placed(k, outer, meta, rows):
    b, far = k % 2, (k // 2) % 2
    cx = jnp.bitwise_xor(meta[X_POS], far if b else outer)
    cy = jnp.bitwise_xor(meta[Y_POS], outer if b else far)
    return ((cx * 2 + cy) * 2 + b) * rows


def fill_kernel(meta, *refs):
    srcs, (up_ref, down_ref) = refs[:8], refs[8:]
    rows = srcs[0].shape[3]
    for core in range(2):

        @pl.when(pl.program_id(0) // 2 == core)
        def _():
            for k in range(4):
                for outer in range(2):
                    at = pl.ds(pl.multiple_of(placed(k, outer, meta, rows), 16), rows)
                    up_ref[at, :] = srcs[k + 4 * core][outer, 0, 0].astype(F32)
                    down_ref[at, :] = srcs[k + 4 * core][outer, 0, 1].astype(F32)


def fill(meta, arrays, shapes):
    _, _, _, rows, width = arrays[0].shape

    def shard(i, s):
        return jnp.bitwise_xor(s[QUARTER], lax.rem(i, 2) * 2 + i // 2)

    def source(k):
        return pl.BlockSpec((2, 1, 2, rows, width), lambda i, s: (0, jnp.clip(i - 2 * (k // 4), 0, 1), 0, 0, 0))

    block = (8 * rows, width)
    return call(
        fill_kernel,
        "fill",
        meta,
        (TENSOR,),
        list(arrays),
        [source(k) for k in range(8)],
        [sds(shape, F32) for shape in shapes],
        [pl.BlockSpec(block, lambda i, s: (0, shard(i, s))), pl.BlockSpec(block, lambda i, s: (shard(i, s), 0))],
        0,
        12 * 8 * 4 * rows * width,
    )


def tail_kernel(wide, meta, *refs):
    srcs, (gq_ref, go_ref, gain_ref, bias_ref, hold_ref, part_ref) = refs[:8], refs[8:]
    rows = srcs[0].shape[2] - 16
    i = pl.program_id(0)
    apart = (jnp.bitwise_xor(meta[Y_POS], lax.rem(i, 2)), jnp.bitwise_xor(meta[X_POS], i // 2))
    for k, src in enumerate(srcs):
        b, far, core = k % 2, (k // 2) % 2, k // 4

        @pl.when(apart[b] == far)
        def _():
            for rt1 in range(2):
                shard = jnp.bitwise_xor(meta[QUARTER], rt1 * 2 + core)
                at = pl.multiple_of(shard * wide + b * rows, 16)
                hold_ref[pl.ds(at, rows), :] = src[0, rt1, 16:].astype(F32)
                if b == 0:
                    part_ref[shard * 4 + i] = src[0, rt1, 0:16].astype(F32)

    @pl.when(i < 3)
    def _():
        gq_ref[...] = hold_ref[...].T

    @pl.when(i == 3)
    def _():
        go_ref[...] = hold_ref[...]
        total = part_ref[0]
        for n in range(1, 4 * TENSOR):
            total = total + part_ref[n]
        gain_ref[...] = total[0]
        bias_ref[...] = total[1]


def tail(meta, arrays, width, wide):
    outs = [sds((width, 3 * TENSOR * wide), F32), sds((TENSOR * wide, width), F32), sds((width,), F32), sds((width,), F32)]
    def source(k):
        def at(i, s):
            outer = jnp.bitwise_xor(s[Y_POS], lax.rem(i, 2)) if k % 2 else jnp.bitwise_xor(s[X_POS], i // 2)
            return outer, 0, 0, 0

        return pl.BlockSpec((1,) + arrays[k].shape[1:], at)

    return call(
        partial(tail_kernel, wide),
        "tail",
        meta,
        (4,),
        list(arrays),
        [source(k) for k in range(8)],
        outs,
        [pl.BlockSpec((width, TENSOR * wide), lambda i, s: (0, jnp.minimum(i, 2)))] + [whole(o.shape) for o in outs[1:]],
        0,
        6 * 4 * width * width,
        scratch=[pltpu.VMEM((TENSOR * wide, width), F32), pltpu.VMEM((4 * TENSOR, 16, width), F32)],
    )


def natural(parts):
    own, to_x, to_y, across = parts
    return jnp.concatenate([own, to_y, to_x, across], axis=1)


def natural_halves(parts):
    send_a, keep_a, send_b, keep_b = parts
    a = jnp.stack([keep_a, send_a])
    b = jnp.stack([keep_b, send_b], axis=1)
    both = jnp.moveaxis(jnp.stack([a, b], axis=2), 3, 0)
    return both.reshape(both.shape[0], -1, both.shape[-1])


def xor_gather(x, n_blk, masks):
    for mask in reversed(masks):
        x = jnp.concatenate([x, swap(x, "blk", n_blk, mask)])
    return x


def scatter_blocks(arrays, n_blk):
    n = len(arrays)

    def cut(first):
        return [a[first : first + 2] for a in arrays]

    (got,) = yield [(jnp.concatenate(cut(6) + cut(2)), "blk", 1)]
    far = add(jnp.stack(cut(4)), got[: 2 * n].reshape((n, 2) + got.shape[1:])).astype(BF16)
    near = add(jnp.stack(cut(0)), got[2 * n :].reshape((n, 2) + got.shape[1:])).astype(BF16)
    (far_got,) = yield [(far[:, 1], "blk", 2)]
    far_sum = add(far[:, 0], far_got).astype(BF16)
    other, near_got = yield [(far_sum, "blk", n_blk // 2), (near[:, 1], "blk", 2)]
    yield [add(near[:, 0], near_got).astype(BF16), other]


def local(n_dp, n_blk, tokens, cotangent, lengths, norm_gain, norm_bias, w_qkv, w_out, w_up, w_down):
    micro_count, rows, width = tokens.shape
    n_docs = lengths.shape[2]
    n_heads = width // HEAD // TENSOR
    wide = n_heads * HEAD
    inner = w_up.shape[1] // TENSOR
    splits = n_blk // (2 * TENSOR)
    s_masks = [TENSOR << b for b in reversed(range(splits.bit_length() - 1))]
    fast = n_dp == 4 and splits == 1
    me = lax.axis_index("blk")
    dp = lax.axis_index("dp")
    half = me // (n_blk // 2)
    quarter = lax.rem(me, TENSOR)
    x_pos, y_pos = (lax.rem(dp, 2), dp // 2) if fast else (0 * dp, 0 * dp)
    docs = lax.dynamic_index_in_dim(lengths, half, 0, False)[0]
    firsts = jnp.cumsum(docs, dtype=jnp.int32) - docs
    meta = jnp.concatenate([jnp.stack([quarter, x_pos, y_pos, me, half]).astype(jnp.int32), firsts])

    gain = norm_gain.astype(F32).reshape(1, width)
    bias = norm_bias.astype(F32).reshape(1, width)

    def mine(array):
        return lax.dynamic_index_in_dim(array, half, 0, False), lax.dynamic_index_in_dim(array, 1 - half, 0, False)

    def fourfold(own):
        near, twin = yield [(own, "blk", 2), (own, "blk", 1)]
        (far_twin,) = yield [(near, "blk", 1)]
        yield [own, near, twin, far_twin]

    def cross(array):
        (got,) = yield [(array, "blk", n_blk // 2)]
        yield from fourfold(got)

    order = Order({"dp": n_dp, "blk": n_blk})
    x_mine, x_other = mine(tokens)
    c_mine, c_other = mine(cotangent)
    x_far = order.start(cross(x_other))
    x_near = order.start(fourfold(x_mine))
    w_cut = order.done(cut(meta, w_qkv, wide))
    order.advance(x_near, x_far)
    c_far = order.start(cross(c_other))
    order.advance(x_near)
    stage = order.done(project(meta, order.hold(x_near.held), 0, QUADS, gain, bias, w_cut, n_blk, n_docs, None))
    order.advance(x_far)
    c_near = order.start(fourfold(c_mine))
    order.advance(c_far, x_far)
    stage = order.done(project(meta, order.hold(x_far.held), 4, QUADS, gain, bias, w_cut, n_blk, n_docs, stage))
    x_all, normed, q, k, v, kn, vn = stage
    if splits > 1:
        k, v, kn, vn = (xor_gather(a, n_blk, s_masks) for a in (k, v, kn, vn))
    order.advance(c_near)
    order.advance(c_far, c_near, c_far)
    cot, mo, ngm, *mlp_parts = order.done(feed(meta, normed, order.hold(c_near.held + c_far.held), w_up, w_down))
    if fast:
        mlp = order.start(reduce_halves(mlp_parts, n_blk))
    att, lse = order.done(attend(meta, *order.hold([q]), kn, v, n_blk, n_docs))
    if fast:
        order.advance(mlp)
    out_part, do, delta, grad_out_part = order.done(mix(meta, *order.hold([att, cot, mo]), w_out))
    if fast:
        order.advance(mlp)
    rest = (normed, grad_out_part)
    q, do = order.hold([q, do])
    back = order.done(attend_back(meta, q, do, lse, delta, kn, vn, k, n_blk, n_docs, rest if splits == 1 else None))
    rest_parts, grads = list(back[:-3]), list(back[-3:])
    if splits > 1:
        for at, mask in [(at, mask) for at in (1, 2) for mask in s_masks]:
            count = grads[at].shape[0] // 2
            grads[at] = add(grads[at][:count], swap(grads[at][count:], "blk", n_blk, mask)).astype(BF16)
        rest_parts = order.done(shard(meta, grads, *rest))
    chains = {}
    if fast:

        def of_rest():
            (own,) = yield from reduce_pieces(rest_parts)
            yield from sum_halves(own[0], sums.astype(BF16), n_blk)

        order.advance(mlp)
        chains["M"] = order.start(spread_pieces(mlp.held[0], True))
        chains["Q"] = order.start(of_rest())
    ng_part, sums = order.done(join(meta, order.hold(grads), x_all, ngm, w_cut))

    def finish():
        def ordered(own, other):
            return jnp.where(half == 0, jnp.stack([own, other]), jnp.stack([other, own])).astype(F32)

        own, other = chains["N"].end()
        output = (tokens.astype(F32) + ordered(own[0], other[0])).astype(BF16)
        normed_grad = ordered(own[1], other[1])
        x_rows = tokens.astype(F32)
        centred = x_rows - jnp.mean(x_rows, axis=2, keepdims=True)
        inverse = lax.rsqrt(jnp.mean(centred * centred, axis=2, keepdims=True) + norm_eps)
        scaled = centred * inverse
        scaled_grad = normed_grad * norm_gain.astype(F32)
        input_grad = cotangent.astype(F32) + inverse * (
            scaled_grad
            - jnp.mean(scaled_grad, axis=2, keepdims=True)
            - scaled * jnp.mean(scaled_grad * scaled, axis=2, keepdims=True)
        )
        return output, input_grad

    if fast:
        for name in TAIL:
            if name == "m":
                grad_up, grad_down = order.done(fill(meta, order.hold(chains["M"].end()), [w_up.shape, w_down.shape]))
            elif name == "n":
                output, input_grad = order.done(finish())
            elif name in chains:
                order.advance(chains[name])
            else:
                chains[name] = order.start(scatter_blocks([out_part, ng_part], n_blk))
        grad_qkv, grad_out, *norm_sums = tail(meta, chains["Q"].end(), width, wide)
    else:
        chains["N"] = order.start(scatter_blocks([out_part, ng_part], n_blk))
        output, input_grad = finish()
        up, down = natural_halves(mlp_parts)
        (rest,) = natural(rest_parts)
        turn = rest[: 3 * wide].T.reshape(width, 3, wide)
        zeros = partial(jnp.zeros, dtype=BF16)
        up = lax.dynamic_update_slice_in_dim(zeros(w_up.shape), up, quarter * inner, 1)
        down = lax.dynamic_update_slice_in_dim(zeros(w_down.shape), down, quarter * inner, 0)
        turn = lax.dynamic_update_slice_in_dim(zeros((width, 3, TENSOR * wide)), turn, quarter * wide, 2)
        out = lax.dynamic_update_slice_in_dim(zeros(w_out.shape), rest[3 * wide :], quarter * wide, 0)
        summed = lax.psum((up, down, turn, out), ("dp", "blk"))
        grad_up, grad_down, turn, grad_out = (g.astype(F32) for g in summed)
        grad_qkv = turn.reshape(w_qkv.shape)
        norm_sums = lax.psum(sums, ("dp", "blk"))
    return (output, input_grad, norm_sums[0], norm_sums[1], grad_qkv, grad_out, grad_up, grad_down)


def solution(mesh):
    tokens = P(None, ("dp", "blk"), None)
    return jax.shard_map(
        partial(local, mesh.shape["dp"], mesh.shape["blk"]),
        mesh=mesh,
        in_specs=(tokens, tokens, P(None, "dp", None)) + (P(),) * 6,
        out_specs=(tokens, tokens) + (P(),) * 6,
        check_vma=False,
    )
```
